32 devices in a mesh: dp: 2 (over y), context: 2 (over x), expert: 8 (over z, core).
Axes of the slice: x: 2, y: 2, z: 4, core: 2. Of those that a mesh axis runs over, the one named last changes fastest.
Arguments:
- tokens: bfloat16 [16, 256, 2048], P(('dp', 'expert'), 'context'), may hold values from -6 to 6
- cotangent: bfloat16 [16, 256, 2048], P(('dp', 'expert'), 'context'), may hold values from -6 to 6
- deal_order: int32 [16, 256], P(('dp', 'expert')), may hold values from 0 to 255, each once within a row
- seq_lengths: int32 [16, 2], P(('dp', 'expert')), may hold values from 1 to 192, 256 in all within a row
- expert_ids: int32 [16, 256, 4], P(('dp', 'expert'), 'context'), may hold values from 0 to 7, all different within a row
- w_query: bfloat16 [2048, 2048], P(('dp', 'context', 'expert')), may hold values from -0.125 to 0.125
- w_key: bfloat16 [2048, 2048], P(('dp', 'context', 'expert')), may hold values from -0.125 to 0.125
- w_value: bfloat16 [2048, 2048], P(('dp', 'context', 'expert')), may hold values from -0.125 to 0.125
- w_out: bfloat16 [2048, 2048], P(('dp', 'context', 'expert')), may hold values from -1 to 1
- bias_query: bfloat16 [2048], P(('dp', 'context', 'expert')), may hold values from -3 to 3
- bias_key: bfloat16 [2048], P(('dp', 'context', 'expert')), may hold values from -3 to 3
- bias_value: bfloat16 [2048], P(('dp', 'context', 'expert')), may hold values from -3 to 3
- norm_attn: bfloat16 [2048], P(('dp', 'context', 'expert')), may hold values from 0.099609375 to 1.8984375
- norm_ffn: bfloat16 [2048], P(('dp', 'context', 'expert')), may hold values from 0.099609375 to 1.8984375
- w_router: bfloat16 [2048, 8], P(('dp', 'context', 'expert')), may hold values from -0.06591797 to 0.06591797
- shared_gate: bfloat16 [2048, 5632], P(('dp', 'context'), 'expert'), may hold values from -0.125 to 0.125
- shared_up: bfloat16 [2048, 5632], P(('dp', 'context'), 'expert'), may hold values from -0.125 to 0.125
- shared_down: bfloat16 [5632, 2048], P('expert', ('dp', 'context')), may hold values from -0.21875 to 0.21875
- shared_switch: bfloat16 [2048], P(('dp', 'context', 'expert')), may hold values from -0.125 to 0.125
- expert_gate: bfloat16 [8, 2048, 1408], P('expert', ('dp', 'context')), may hold values from -0.125 to 0.125
- expert_up: bfloat16 [8, 2048, 1408], P('expert', ('dp', 'context')), may hold values from -0.125 to 0.125
- expert_down: bfloat16 [8, 1408, 2048], P('expert', None, ('dp', 'context')), may hold values from -1.25 to 1.25
Outputs:
- out_tokens: bfloat16 [16, 256, 2048], P(('dp', 'expert'), 'context')
- grad_tokens: bfloat16 [16, 256, 2048], P(('dp', 'expert'), 'context')
- grad_w_query: float32 [2048, 2048], P(('dp', 'context', 'expert'))
- grad_w_key: float32 [2048, 2048], P(('dp', 'context', 'expert'))
- grad_w_value: float32 [2048, 2048], P(('dp', 'context', 'expert'))
- grad_w_out: float32 [2048, 2048], P(('dp', 'context', 'expert'))
- grad_bias_query: float32 [2048], P(('dp', 'context', 'expert'))
- grad_bias_key: float32 [2048], P(('dp', 'context', 'expert'))
- grad_bias_value: float32 [2048], P(('dp', 'context', 'expert'))
- grad_norm_attn: float32 [2048], P(('dp', 'context', 'expert'))
- grad_norm_ffn: float32 [2048], P(('dp', 'context', 'expert'))
- grad_router: float32 [2048, 8], P(('dp', 'context', 'expert'))
- grad_shared_gate: float32 [2048, 5632], P(('dp', 'context'), 'expert')
- grad_shared_up: float32 [2048, 5632], P(('dp', 'context'), 'expert')
- grad_shared_down: float32 [5632, 2048], P('expert', ('dp', 'context'))
- grad_shared_switch: float32 [2048], P(('dp', 'context', 'expert'))
- grad_expert_gate: float32 [8, 2048, 1408], P('expert', ('dp', 'context'))
- grad_expert_up: float32 [8, 2048, 1408], P('expert', ('dp', 'context'))
- grad_expert_down: float32 [8, 1408, 2048], P('expert', None, ('dp', 'context'))
The draws below stay inside these ranges and needn't reach their ends.
Inputs may be any that keep to these rules, and one draw needn't show every extreme that they name: `deal_order`: each row is a permutation of the 256 places of a group. `seq_lengths`: the 2 lengths of a group sum to 256; the longest is at most 192. `expert_ids`: the 4 experts of a token differ.
All inputs are finite; a program needn't handle non-finite values.
Results may differ from the reference program's by a relative error of at most 0.022.
Values may be sent and summed in bfloat16 or wider, within the bound.
No kernel may reach another device: no remote copies, remote signals or barrier semaphores. Data moves between devices by JAX's collectives and lax.ppermute only.
A program may use at most 448 MiB of HBM per device.

```python
import math
import jax
import jax.numpy as jnp
import numpy as np
from jax import lax

D = 2048
HEADS = 16
HD = 128
FE = 1408
FS = 5632
TOP = 4
SEQS = 2
TOK_DEV = 128
EXPERTS = 8
GROUP_TOK = 256
GROUPS = 16
CAP = 80
N_CONTEXT = 2


def levels(rng, extent, cuts, least, top_value):
    def one(dim, blocks):
        heights = jax.random.uniform(jax.random.fold_in(jax.random.fold_in(rng, 6), dim), (blocks,), jnp.float32, least / len(cuts), top_value / len(cuts))
        return jnp.repeat(jnp.exp(heights), extent[dim] // blocks).reshape((-1,) + (1,) * (len(extent) - dim - 1))

    gain = one(*cuts[0])
    for cut in cuts[1:]:
        gain = gain * one(*cut)
    return gain


def picks_of(stream_key, rows, count, top, lift):
    ranking = jax.random.permutation(jax.random.fold_in(stream_key, 1), count)
    favour = ranking
    for power in range(3):
        favour = favour * favour // count
    favour = favour * lift // count
    chance = jax.random.randint(jax.random.fold_in(stream_key, 2), (rows, count), 0, 4096) + favour
    fixed_rows = jax.random.permutation(jax.random.fold_in(stream_key, 3), rows)[jnp.arange(count) % rows]
    chance = jnp.where(jnp.arange(rows)[:, None] == fixed_rows[None, :], 1 << 14, chance)
    merit = chance * count + jnp.arange(count)
    return lax.top_k(merit.astype(jnp.int32), top)[1].astype(jnp.int32)


def profile(number_of, total, limit, slope):
    portions = [(1 << 20) // math.isqrt(rank ** slope) + 1 for rank in range(2, number_of + 1)]
    surplus, given = total - limit - (number_of - 1), [1] * (number_of - 1)
    while surplus > 0:
        free = [i for i in range(number_of - 1) if given[i] < limit]
        whole, remaining = sum([portions[i] for i in free]), surplus
        for i in free:
            addition = min(limit - given[i], max(1, remaining * portions[i] // whole), surplus)
            given[i] = given[i] + addition
            surplus = surplus - addition
    return np.array([limit] + given)


def ragged(stream_key, amount, total, limit, slope):
    if amount == 2:
        one = jax.random.randint(stream_key, (), max(1, total - limit), min(limit, total - 1) + 1)
        return jnp.stack([one, total - one])
    sizes = jnp.asarray(profile(amount, total, limit, slope), jnp.int32)
    couples = (amount - 1) // 2
    source_of, receiver = sizes[1:1 + 2 * couples:2], sizes[2:2 + 2 * couples:2]
    margin = jnp.minimum(source_of - 1, limit - receiver)
    moved = jax.random.randint(jax.random.fold_in(stream_key, 1), (couples,), 0, 1 << 20) % (margin + 1)
    sizes = sizes.at[1:1 + 2 * couples:2].set(source_of - moved).at[2:2 + 2 * couples:2].set(receiver + moved)
    return sizes[jax.random.permutation(jax.random.fold_in(stream_key, 2), amount)]


def normal_values(rng, extent, width, reach, split=(), kind=jnp.bfloat16):
    drawn = width * jax.random.normal(rng, extent, jnp.float32)
    if split:
        drawn = drawn * levels(rng, extent, split, -0.22, 0.18)
    return jnp.clip(drawn, -reach, reach).astype(kind)


def setup_inputs(seed: int = 0) -> dict:
    keys = jax.random.split(jax.random.key(seed), 23)
    tokens = normal_values(keys[0], (GROUPS, GROUP_TOK, D), 1.0, 6.0, ((0, 16), (1, 2)))
    cotangent = normal_values(keys[1], (GROUPS, GROUP_TOK, D), 1.0, 6.0, ((0, 16), (1, 2)))
    deal_order = jax.vmap(lambda own: jax.random.permutation(own, GROUP_TOK))(jax.random.split(keys[2], GROUPS)).reshape((GROUPS, GROUP_TOK)).astype(jnp.int32)
    seq_lengths = jax.vmap(lambda own: ragged(own, SEQS, GROUP_TOK, GROUP_TOK * 3 // 4, 2))(jax.random.split(keys[3], GROUPS)).reshape((GROUPS, SEQS)).astype(jnp.int32)
    expert_ids = picks_of(keys[4], GROUPS * GROUP_TOK, EXPERTS, TOP, 4096).reshape((GROUPS, GROUP_TOK, TOP))
    w_query = normal_values(keys[5], (D, D), D ** -0.5, 0.125, ((0, 32),))
    w_key = normal_values(keys[6], (D, D), D ** -0.5, 0.125, ((0, 32),))
    w_value = normal_values(keys[7], (D, D), D ** -0.5, 0.125, ((0, 32),))
    w_out = normal_values(keys[8], (D, D), (D // 64) ** -0.5, 1.0, ((0, 32),))
    bias_query = normal_values(keys[9], (D,), 0.5, 3.0, ((0, 32),))
    bias_key = normal_values(keys[10], (D,), 0.5, 3.0, ((0, 32),))
    bias_value = normal_values(keys[11], (D,), 0.5, 3.0, ((0, 32),))
    norm_attn = jnp.clip(1.0 + 0.18 * jax.random.normal(keys[12], (D,), jnp.float32), 0.099609375, 1.8984375).astype(jnp.bfloat16)
    norm_ffn = jnp.clip(1.0 + 0.18 * jax.random.normal(keys[13], (D,), jnp.float32), 0.099609375, 1.8984375).astype(jnp.bfloat16)
    w_router = normal_values(keys[14], (D, EXPERTS), 0.011, 0.06591797, ((0, 32),))
    shared_gate = normal_values(keys[15], (D, FS), D ** -0.5, 0.125, ((0, 4), (1, 8)))
    shared_up = normal_values(keys[16], (D, FS), D ** -0.5, 0.125, ((0, 4), (1, 8)))
    shared_down = normal_values(keys[17], (FS, D), (FS // 8) ** -0.5, 0.21875, ((0, 8), (1, 4)))
    shared_switch = normal_values(keys[18], (D,), D ** -0.5, 0.125, ((0, 32),))
    expert_gate = normal_values(keys[19], (EXPERTS, D, FE), D ** -0.5, 0.125, ((0, 8), (1, 4)))
    expert_up = normal_values(keys[20], (EXPERTS, D, FE), D ** -0.5, 0.125, ((0, 8), (1, 4)))
    expert_down = normal_values(keys[21], (EXPERTS, FE, D), (max(1, FE * TOP // (4 * EXPERTS * EXPERTS))) ** -0.5, 1.25, ((0, 8), (2, 4)))
    return dict(tokens=tokens, cotangent=cotangent, deal_order=deal_order, seq_lengths=seq_lengths, expert_ids=expert_ids, w_query=w_query, w_key=w_key, w_value=w_value, w_out=w_out, bias_query=bias_query, bias_key=bias_key, bias_value=bias_value, norm_attn=norm_attn, norm_ffn=norm_ffn, w_router=w_router, shared_gate=shared_gate, shared_up=shared_up, shared_down=shared_down, shared_switch=shared_switch, expert_gate=expert_gate, expert_up=expert_up, expert_down=expert_down)


EPSILON = 1e-06
ROPE_BASE = 1000000.0
NEGATIVE = -1e+30
HIGHEST = lax.Precision.HIGHEST

@jax.custom_vjp
def low(v):
    return lax.optimization_barrier(v.astype(jnp.bfloat16)).astype(jnp.float32)

@jax.custom_vjp
def low_back(v):
    return v

def low_keep(v):
    return (low(v), None)

def low_pass(kept, grad):
    return (grad,)

def back_keep(v):
    return (v, None)

def back_low(kept, grad):
    return (low(grad),)
low.defvjp(low_keep, low_pass)
low_back.defvjp(back_keep, back_low)

def matmul(left_mat, right_mat):
    return jnp.dot(left_mat, right_mat, precision=HIGHEST)

def rotary(positions):
    halfway = HD // 2
    frequency = ROPE_BASE ** (-2.0 * jnp.arange(halfway, dtype=jnp.float32) / HD)
    angles = positions.astype(jnp.float32)[..., None] * frequency
    cosine = jnp.concatenate([jnp.cos(angles), jnp.cos(angles)], -1)
    sine_table = jnp.concatenate([jnp.sin(angles), jnp.sin(angles)], -1)
    return (cosine, sine_table)

def rotate(head_vals, cosine, sine_table):
    halfway = HD // 2
    turned = jnp.concatenate([-head_vals[..., halfway:], head_vals[..., :halfway]], -1)
    return head_vals * cosine[..., None, :] + turned * sine_table[..., None, :]

def attend(pieces):
    queries, keyed, valued, segment_row, position_row = pieces
    scores = jnp.einsum('qhd,khd->hqk', queries, keyed, precision=HIGHEST) * HD ** (-0.5)
    scores = low_back(scores)
    allowed = (segment_row[:, None] == segment_row[None, :]) & (position_row[None, :] <= position_row[:, None])
    scores = jnp.where(allowed[None], scores, NEGATIVE)
    row_max = lax.optimization_barrier(jnp.max(scores, -1, keepdims=True))
    expo = jnp.exp(scores - row_max)
    attn_prob = low(expo / lax.optimization_barrier(jnp.sum(expo, -1, keepdims=True)))
    return jnp.einsum('hqk,khd->qhd', attn_prob, valued, precision=HIGHEST)

def reference(tokens, cotangent, deal_order, seq_lengths, expert_ids, w_query, w_key, w_value, w_out, bias_query, bias_key, bias_value, norm_attn, norm_ffn, w_router, shared_gate, shared_up, shared_down, shared_switch, expert_gate, expert_up, expert_down):
    groups = tokens.shape[0]
    group_tok = tokens.shape[1]
    pick_index = deal_order[:, :, None]
    dealt_rows = jnp.take_along_axis(tokens.astype(jnp.float32), pick_index, 1)
    dealt_grad = jnp.take_along_axis(cotangent.astype(jnp.float32), pick_index, 1)
    seq_ends = jnp.cumsum(seq_lengths, axis=1).astype(jnp.int32)
    segment = lax.optimization_barrier(jnp.sum((deal_order[:, :, None] >= seq_ends[:, None, :]).astype(jnp.int32), 2)).astype(jnp.int32)
    seq_starts = seq_ends - seq_lengths
    position = deal_order - jnp.take_along_axis(seq_starts, segment, 1)
    cosine, sine_table = rotary(position)
    one_hot = (expert_ids[..., None] == jnp.arange(EXPERTS, dtype=jnp.int32)).astype(jnp.int32)
    per_source = one_hot.reshape(groups * N_CONTEXT, TOK_DEV * TOP, EXPERTS)
    earlier = jnp.cumsum(per_source, 1).astype(jnp.int32) - per_source
    slot_pos = lax.optimization_barrier(jnp.sum(earlier * per_source, 2)).reshape(groups, group_tok, TOP)
    kept_slot = slot_pos < CAP
    shape_four = (groups, group_tok, HEADS, HD)

    def forward(dealt_in, w_query, w_key, w_value, w_out, bias_query, bias_key, bias_value, norm_attn, norm_ffn, w_router, shared_gate, shared_up, shared_down, shared_switch, expert_gate, expert_up, expert_down):
        scale_one = lax.rsqrt(lax.optimization_barrier(jnp.mean(dealt_in * dealt_in, -1, keepdims=True)) + EPSILON)
        normed = low(dealt_in * scale_one * norm_attn)
        queries = low(rotate(low_back(matmul(normed, w_query) + bias_query).reshape(shape_four), cosine, sine_table))
        keyed = low(rotate(low_back(matmul(normed, w_key) + bias_key).reshape(shape_four), cosine, sine_table))
        valued = low(low_back(matmul(normed, w_value) + bias_value)).reshape(shape_four)
        mixed_rows = lax.map(jax.checkpoint(attend), (queries, keyed, valued, segment, position))
        mixed_rows = low(low_back(mixed_rows)).reshape(groups, group_tok, D)
        residual = dealt_in + low_back(matmul(mixed_rows, w_out))
        scale_two = lax.rsqrt(lax.optimization_barrier(jnp.mean(residual * residual, -1, keepdims=True)) + EPSILON)
        normed_two = low(residual * scale_two * norm_ffn)
        logits = low_back(matmul(normed_two, w_router))
        router_prob = jax.nn.softmax(logits, -1)
        gate_share = jnp.where(kept_slot, jnp.take_along_axis(router_prob, expert_ids, -1), 0.0)
        gate_pre = low_back(matmul(normed_two, shared_gate))
        up_pre = low_back(matmul(normed_two, shared_up))
        hidden = low(jax.nn.silu(gate_pre) * up_pre)
        shared_out = low_back(matmul(hidden, shared_down))
        switch = jax.nn.sigmoid(low_back(matmul(normed_two, shared_switch)))
        flat_rows = normed_two.reshape(-1, D)
        share_of = lax.optimization_barrier(jnp.sum(one_hot * gate_share[..., None], 2)).reshape(-1, EXPERTS)

        def expert_step(running, pieces):
            gate_mat, up_mat, down_mat, column = pieces
            entry_rows = low_back(flat_rows)
            gate_e = low_back(matmul(entry_rows, gate_mat))
            up_e = low_back(matmul(entry_rows, up_mat))
            hidden_e = low(jax.nn.silu(gate_e) * up_e)
            out_e = low(low_back(matmul(hidden_e, down_mat)))
            return (running + column[:, None] * out_e, None)
        routed, unused = lax.scan(jax.checkpoint(expert_step), jnp.zeros_like(flat_rows), (expert_gate, expert_up, expert_down, share_of.T))
        return residual + switch[..., None] * shared_out + routed.reshape(groups, group_tok, D)
    weights = [weight_arg.astype(jnp.float32) for weight_arg in (w_query, w_key, w_value, w_out, bias_query, bias_key, bias_value, norm_attn, norm_ffn, w_router, shared_gate, shared_up, shared_down, shared_switch, expert_gate, expert_up, expert_down)]
    output, pullback = jax.vjp(forward, dealt_rows, *weights)
    gradients = pullback(dealt_grad)
    inverse = jnp.zeros_like(deal_order).at[jnp.arange(groups, dtype=jnp.int32)[:, None], deal_order].set(jnp.broadcast_to(jnp.arange(group_tok, dtype=jnp.int32)[None, :], deal_order.shape))
    back_index = inverse[:, :, None]
    out_tokens = jnp.take_along_axis(output, back_index, 1).astype(jnp.bfloat16)
    grad_tokens = jnp.take_along_axis(gradients[0], back_index, 1).astype(jnp.bfloat16)
    return (out_tokens, grad_tokens, gradients[1], gradients[2], gradients[3], gradients[4], gradients[5], gradients[6], gradients[7], gradients[8], gradients[9], gradients[10], gradients[11], gradients[12], gradients[13], gradients[14], gradients[15], gradients[16], gradients[17])
```

```python
import jax
import jax.numpy as jnp
from jax import lax
from jax.sharding import PartitionSpec as P

HD = 128

EPSILON = 1e-06
ROPE_BASE = 1000000.0
NEGATIVE = -1e30
F32 = jnp.float32
BF16 = jnp.bfloat16


def mat_dot(left_mat, right_mat):
    return jnp.dot(left_mat, right_mat, preferred_element_type=F32)


def left_dot(left_mat, right_mat):
    return lax.dot_general(
        left_mat, right_mat, (((0,), (0,)), ((), ())), preferred_element_type=F32
    )


def right_dot(left_mat, right_mat):
    return lax.dot_general(
        left_mat, right_mat, (((1,), (1,)), ((), ())), preferred_element_type=F32
    )


def shift(x, axis, step):
    n = lax.axis_size(axis)
    return lax.ppermute(x, axis, [(i, (i + step) % n) for i in range(n)])


def plane_blocks():
    return (
        lax.axis_size("dp"),
        lax.axis_size("context"),
        lax.axis_index("dp"),
        lax.axis_index("context"),
    )


def plane_gather(x, axis):
    ndp, nc, dp, ctx = plane_blocks()
    half = x.shape[0] // 2
    size = x.shape[axis]
    shape = list(x.shape)
    shape[axis] = size * ndp * nc
    full = jnp.zeros(shape, x.dtype)

    def place(full, piece, d, s, offset):
        block = lax.rem(dp - d + ndp, ndp) * nc + lax.rem(ctx - s + nc, nc)
        start = [0] * x.ndim
        start[0] = offset
        start[axis] = start[axis] + block * size
        return lax.dynamic_update_slice(full, piece, start)

    across = {s: shift(x, "context", s) for s in range(1, nc)}
    along = {d: shift(x, "dp", d) for d in range(1, ndp)}
    full = place(full, x, 0, 0, 0)
    for s in across:
        full = place(full, across[s], 0, s, 0)
    for d in along:
        full = place(full, along[d], d, 0, 0)
    for s in across:
        for d in along:
            full = place(full, shift(across[s][:half], "dp", d), d, s, 0)
            full = place(full, shift(along[d][half:], "context", s), d, s, half)
    return full


def plane_scatter(block_of, half):
    ndp, nc, dp, ctx = plane_blocks()

    def term(d, s):
        return block_of(lax.rem(dp + d, ndp) * nc + lax.rem(ctx + s, nc))

    first, second = {}, {}
    for d in range(1, ndp):
        for s in range(1, nc):
            far = term(d, s).astype(BF16)
            got = shift(far[:half], "context", s).astype(F32)
            first[d] = got if d not in first else first[d] + got
            got = shift(far[half:], "dp", d).astype(F32)
            second[s] = got if s not in second else second[s] + got
    upper, lower = [], []
    for d in range(1, ndp):
        near = term(d, 0)
        lower.append(shift(near[half:].astype(BF16), "dp", d))
        upper.append(shift((near[:half] + first[d]).astype(BF16), "dp", d))
    for s in range(1, nc):
        near = term(0, s)
        upper.append(shift(near[:half].astype(BF16), "context", s))
        lower.append(shift((near[half:] + second[s]).astype(BF16), "context", s))
    own = term(0, 0)
    top, bottom = own[:half], own[half:]
    for piece in upper:
        top = top + piece.astype(F32)
    for piece in lower:
        bottom = bottom + piece.astype(F32)
    return jnp.concatenate([top, bottom], 0)


def doubling_steps(axis):
    n = lax.axis_size(axis)
    step = 1
    while step < n:
        yield step, [(i, i ^ step) for i in range(n)]
        step *= 2


def small_gather(x):
    for axis in ("expert", "context", "dp"):
        place = lax.axis_index(axis)
        for step, pairs in doubling_steps(axis):
            other = lax.ppermute(x, axis, pairs)
            high = (place & step) != 0
            x = jnp.concatenate([jnp.where(high, other, x), jnp.where(high, x, other)], 0)
    return x


def small_scatter(x):
    for axis in ("dp", "context", "expert"):
        place = lax.axis_index(axis)
        for step, pairs in reversed(list(doubling_steps(axis))):
            half = x.shape[0] // 2
            high = (place & step) != 0
            low_part, high_part = x[:half], x[half:]
            other = lax.ppermute(jnp.where(high, low_part, high_part), axis, pairs)
            x = jnp.where(high, high_part, low_part) + other
    return x[0]


def core_exchange(x, group):
    count = lax.axis_size("expert")
    place = lax.rem(lax.axis_index("expert"), group)
    out = x
    for s in range(1, group):
        piece = lax.dynamic_slice_in_dim(x, lax.rem(place + s, group), 1)
        pairs = [(i, i // group * group + (i % group + s) % group) for i in range(count)]
        got = lax.ppermute(piece, "expert", pairs)
        out = lax.dynamic_update_slice_in_dim(out, got, lax.rem(place - s + group, group), 0)
    return out


def rotate(vals, cosine, sine_table):
    halfway = HD // 2
    turned = jnp.concatenate([-vals[..., halfway:], vals[..., :halfway]], -1)
    return vals * cosine[:, None, :] + turned * sine_table[:, None, :]


def rotate_back(grads, cosine, sine_table):
    halfway = HD // 2
    scaled = grads * sine_table[:, None, :]
    turned = jnp.concatenate([scaled[..., halfway:], -scaled[..., :halfway]], -1)
    return grads * cosine[:, None, :] + turned


def rms_unit(values):
    scaling = lax.rsqrt(jnp.mean(values * values, -1, keepdims=True) + EPSILON)
    return values * scaling, scaling


def body(
    tokens,
    cotangent,
    deal_order,
    seq_lengths,
    expert_ids,
    w_query,
    w_key,
    w_value,
    w_out,
    bias_query,
    bias_key,
    bias_value,
    norm_attn,
    norm_ffn,
    w_router,
    shared_gate,
    shared_up,
    shared_down,
    shared_switch,
    expert_gate,
    expert_up,
    expert_down,
):
    ndp, nc, dp, ctx = plane_blocks()
    planes = ndp * nc
    count = lax.axis_size("expert")
    here = lax.axis_index("expert")
    tok_count, width = tokens.shape[1], tokens.shape[2]
    group_tok = deal_order.shape[1]
    seqs = seq_lengths.shape[1]
    top = expert_ids.shape[2]
    rows_flat = w_query.shape[0]
    part = HD // rows_flat
    heads = planes // part
    runs = count // part
    run, member = here // part, lax.rem(here, part)
    fe_width = expert_gate.shape[2]
    fs_width = shared_gate.shape[1]
    hidden_width = fe_width + fs_width
    capacity = min(tok_count, 5 * tok_count * top // (4 * count))
    wide = heads * HD
    all_rows = count * tok_count

    token_rows = tokens[0]
    all_tokens = lax.all_gather(token_rows, "expert", axis=0, tiled=True)

    def by_head(w):
        w = w.reshape(rows_flat, part, heads, runs, HD).transpose(3, 1, 0, 2, 4)
        return w.reshape(count, rows_flat, wide)

    qkv_out = jnp.concatenate([by_head(w) for w in (w_query, w_key, w_value)], -1)
    qkv_rows = lax.all_to_all(qkv_out, "expert", split_axis=0, concat_axis=0, tiled=True)
    w_qkv = plane_gather(qkv_rows.reshape(count * rows_flat, 3 * wide), 0)
    wo_planes = plane_gather(w_out[None].reshape(rows_flat, width), 0)
    wo_mine = core_exchange(wo_planes.reshape(part, heads, rows_flat, width), part)
    w_o = wo_mine.transpose(1, 0, 2, 3).reshape(wide, width)

    small = jnp.concatenate(
        [
            v.astype(F32).reshape(-1)
            for v in (
                bias_query,
                bias_key,
                bias_value,
                norm_attn,
                norm_ffn,
                shared_switch,
                w_router,
                deal_order,
                seq_lengths,
                expert_ids,
            )
        ]
    )
    small_all = small_gather(small[None])
    columns = {}
    place = 0
    for name in ("bq", "bk", "bv", "na", "nf", "sw"):
        columns[name] = small_all[:, place : place + rows_flat].reshape(-1)
        place += rows_flat
    router = small_all[:, place : place + rows_flat * count].reshape(-1, count).astype(BF16)
    place += rows_flat * count
    plane_small = lax.dynamic_index_in_dim(
        small_all.reshape(ndp, nc, count, -1), dp, 0, keepdims=False
    )
    order = plane_small[0, :, place : place + group_tok].astype(jnp.int32)
    place += group_tok
    lengths = plane_small[0, :, place : place + seqs].astype(jnp.int32)
    place += seqs
    ids = plane_small[..., place:].reshape(nc, count, tok_count, top).astype(jnp.int32)
    gain_attn, gain_ffn = columns["na"], columns["nf"]
    router_switch = jnp.concatenate([router, columns["sw"].astype(BF16)[:, None]], 1)

    all_grads = lax.all_gather(cotangent[0], "expert", axis=0, tiled=True)

    gate_own = jnp.concatenate([expert_gate[0], shared_gate], 1)
    up_own = jnp.concatenate([expert_up[0], shared_up], 1)
    down_own = jnp.concatenate([expert_down[0], shared_down], 0)
    w_down = plane_gather(down_own, 1)
    w_gate = plane_gather(gate_own, 0)
    w_up = plane_gather(up_own, 0)

    hit = jnp.any(ids == here, -1)
    below = jnp.arange(tok_count)[:, None] < jnp.arange(tok_count)[None, :]
    slot = mat_dot(hit.reshape(nc * count, tok_count).astype(BF16), below.astype(BF16))
    kept = (hit & (slot.reshape(nc, count, tok_count) < capacity)).astype(F32)
    kept = kept.transpose(1, 0, 2).reshape(count, group_tok)
    local_index = ctx * tok_count + jnp.arange(tok_count, dtype=jnp.int32)
    kept_rows = jnp.sum(
        jnp.where(order[:, None, :] == local_index[None, :, None], kept[:, None, :], 0.0), -1
    ).reshape(all_rows)

    ends = jnp.cumsum(lengths, 1)
    starts = ends - lengths

    def segments(index):
        segment = jnp.sum((index[None, :, None] >= ends[:, None, :]).astype(jnp.int32), -1)
        hot = segment[..., None] == jnp.arange(seqs, dtype=jnp.int32)
        return segment, index[None, :] - jnp.sum(jnp.where(hot, starts[:, None, :], 0), -1)

    query_segment, position = segments(local_index)
    allowed = []
    for s in range(nc):
        key_index = local_index - s * tok_count
        key_segment, _ = segments(key_index)
        allowed.append(
            (query_segment[:, :, None] == key_segment[:, None, :])
            & (key_index[None, None, :] <= local_index[None, :, None])
            & (key_index >= 0)[None, None, :]
        )
    allowed = jnp.concatenate(allowed, -1)[:, None]
    frequency = ROPE_BASE ** (-2.0 * jnp.arange(HD // 2, dtype=F32) / HD)
    angles = position.reshape(-1).astype(F32)[:, None] * frequency[None, :]
    cosine = jnp.concatenate([jnp.cos(angles)] * 2, -1)
    sine_table = jnp.concatenate([jnp.sin(angles)] * 2, -1)

    unit_all, _ = rms_unit(all_tokens.astype(F32))
    normed = (unit_all * gain_attn).astype(BF16)

    def own_heads(row):
        row = row.reshape(part, heads, runs, HD)
        row = lax.dynamic_index_in_dim(row, member, 0, keepdims=False)
        return lax.dynamic_index_in_dim(row, run, 1, keepdims=False).reshape(-1)

    bias = jnp.concatenate([own_heads(columns[k]) for k in ("bq", "bk", "bv")])
    qkv = mat_dot(normed, w_qkv) + bias
    query_heads = rotate(qkv[:, :wide].reshape(all_rows, heads, HD), cosine, sine_table)
    key_heads = rotate(qkv[:, wide : 2 * wide].reshape(all_rows, heads, HD), cosine, sine_table)
    key_value = jnp.concatenate(
        [key_heads.reshape(all_rows, wide), qkv[:, 2 * wide :]], -1
    ).astype(BF16)
    earlier = [key_value] + [
        lax.ppermute(key_value, "context", [(i, i + s) for i in range(nc - s)])
        for s in range(1, nc)
    ]
    keyed = jnp.concatenate([kv.reshape(count, tok_count, 2 * wide) for kv in earlier], 1)
    keys = keyed[..., :wide].reshape(count, nc * tok_count, heads, HD)
    values = keyed[..., wide:].reshape(count, nc * tok_count, heads, HD)
    queries = query_heads.astype(BF16).reshape(count, tok_count, heads, HD)
    scores = jnp.einsum("gqhd,gkhd->ghqk", queries, keys, preferred_element_type=F32)
    scores = jnp.where(allowed, scores * HD ** (-0.5), NEGATIVE)
    expo = jnp.exp(scores - jnp.max(scores, -1, keepdims=True))
    prob = expo / jnp.sum(expo, -1, keepdims=True)
    prob_low = prob.astype(BF16)
    mixed = jnp.einsum("ghqk,gkhd->gqhd", prob_low, values, preferred_element_type=F32)
    mixed = mixed.astype(BF16).reshape(all_rows, wide)
    attn_out = lax.psum_scatter(
        mat_dot(mixed, w_o).astype(BF16), "expert", scatter_dimension=0, tiled=True
    )
    residual = token_rows.astype(F32) + attn_out.astype(F32)
    unit_two, scale_two = rms_unit(residual)
    rows = lax.all_gather(
        (unit_two * gain_ffn).astype(BF16), "expert", axis=0, tiled=True
    )

    grad_hidden = right_dot(all_grads, w_down)
    logits = mat_dot(rows, router_switch)
    prob_router = jax.nn.softmax(logits[:, :count], -1)
    switch = jax.nn.sigmoid(logits[:, count])
    own_hot = (jnp.arange(count) == here).astype(F32)[None, :]
    prob_own = jnp.sum(prob_router * own_hot, 1)
    share = prob_own * kept_rows
    is_expert = (jnp.arange(hidden_width) < fe_width)[None, :]
    scale = jnp.where(is_expert, share[:, None], switch[:, None])
    gate_x = mat_dot(rows, w_gate)
    up_x = mat_dot(rows, w_up)
    sig = jax.nn.sigmoid(gate_x)
    hidden = gate_x * sig * up_x
    product = grad_hidden * hidden
    grad_share = jnp.sum(product[:, :fe_width], 1)
    grad_switch = jnp.sum(product[:, fe_width:], 1)
    scaled = (scale * hidden).astype(BF16)
    grad_scaled = scale * grad_hidden
    grad_gate = (grad_scaled * up_x * sig * (1.0 + gate_x * (1.0 - sig))).astype(BF16)
    grad_up = (grad_scaled * gate_x * sig).astype(BF16)
    grad_small = jnp.concatenate(
        [
            (grad_share * share)[:, None] * (own_hot - prob_router),
            (grad_switch * switch * (1.0 - switch))[:, None],
        ],
        1,
    ).astype(BF16)
    grad_rows = (
        right_dot(grad_gate, w_gate) + right_dot(grad_up, w_up) + right_dot(grad_small, router_switch)
    )
    grad_normed_two = lax.psum_scatter(
        grad_rows.astype(BF16), "expert", scatter_dimension=0, tiled=True
    ).astype(F32)
    grad_router_switch = left_dot(rows, grad_small)

    block = width // planes

    def row_blocks(acts, grads):
        def block_of(r):
            return left_dot(lax.dynamic_slice_in_dim(acts, r * block, block, 1), grads)

        return block_of

    def down_blocks(r):
        return left_dot(scaled, lax.dynamic_slice_in_dim(all_grads, r * block, block, 1))

    grad_down_w = plane_scatter(down_blocks, hidden_width // 2)
    grad_gate_w = plane_scatter(row_blocks(rows, grad_gate), block // 2)
    grad_up_w = plane_scatter(row_blocks(rows, grad_up), block // 2)
    output = lax.psum_scatter(
        mat_dot(scaled, w_down).astype(BF16), "expert", scatter_dimension=0, tiled=True
    )
    out_tokens = (residual + output.astype(F32)).astype(BF16)

    grad_unit = grad_normed_two * gain_ffn
    grad_residual = cotangent[0].astype(F32) + scale_two * (
        grad_unit - unit_two * jnp.mean(grad_unit * unit_two, -1, keepdims=True)
    )
    grad_gain_ffn = jnp.sum(grad_normed_two * unit_two, 0)
    grad_attn = lax.all_gather(grad_residual.astype(BF16), "expert", axis=0, tiled=True)
    grad_mixed = (
        right_dot(grad_attn, w_o).astype(BF16).reshape(count, tok_count, heads, HD)
    )
    grad_value = jnp.einsum("ghqk,gqhd->gkhd", prob_low, grad_mixed, preferred_element_type=F32)
    grad_probs = jnp.einsum("gqhd,gkhd->ghqk", grad_mixed, values, preferred_element_type=F32)
    inner = jnp.sum(grad_probs * prob, -1, keepdims=True)
    grad_scores = (prob * (grad_probs - inner)).astype(BF16)
    grad_query = HD ** (-0.5) * jnp.einsum(
        "ghqk,gkhd->gqhd", grad_scores, keys, preferred_element_type=F32
    )
    grad_key = HD ** (-0.5) * jnp.einsum(
        "ghqk,gqhd->gkhd", grad_scores, queries, preferred_element_type=F32
    )
    grad_kv = jnp.concatenate([grad_key, grad_value], 2)
    kv_sum = grad_kv[:, :tok_count].reshape(all_rows, 2 * wide)
    for s in range(1, nc):
        piece = grad_kv[:, s * tok_count : (s + 1) * tok_count].reshape(all_rows, 2 * wide)
        kv_sum = kv_sum + lax.ppermute(
            piece.astype(BF16), "context", [(i + s, i) for i in range(nc - s)]
        ).astype(F32)
    grad_query = rotate_back(grad_query.reshape(all_rows, heads, HD), cosine, sine_table)
    grad_key = rotate_back(kv_sum[:, :wide].reshape(all_rows, heads, HD), cosine, sine_table)
    grad_qkv = jnp.concatenate(
        [grad_query.reshape(all_rows, wide), grad_key.reshape(all_rows, wide), kv_sum[:, wide:]],
        -1,
    ).astype(BF16)
    grad_normed = right_dot(grad_qkv, w_qkv)
    grad_normed_own = lax.psum_scatter(
        grad_normed.astype(BF16), "expert", scatter_dimension=0, tiled=True
    ).astype(F32)

    qkv_grad_rows = plane_scatter(row_blocks(normed, grad_qkv), block // 2)
    qkv_back = lax.all_to_all(
        qkv_grad_rows.astype(BF16).reshape(count, rows_flat, 3 * wide),
        "expert",
        split_axis=0,
        concat_axis=0,
        tiled=True,
    )

    def from_heads(i):
        w = qkv_back[..., i * wide : (i + 1) * wide].astype(F32)
        w = w.reshape(runs, part, rows_flat, heads, HD).transpose(2, 1, 3, 0, 4)
        return w.reshape(rows_flat, width)

    grad_wo = left_dot(mixed, grad_attn).astype(BF16).reshape(heads, part, rows_flat, width)
    wo_back = core_exchange(grad_wo.transpose(1, 0, 2, 3), part)
    wo_back = wo_back.reshape(planes, rows_flat, width)
    grad_w_out = plane_scatter(
        lambda r: lax.dynamic_index_in_dim(wo_back, r, 0, keepdims=False).astype(F32),
        rows_flat // 2,
    )

    def to_heads(row):
        full = jnp.zeros((part, heads, runs, HD), F32)
        full = lax.dynamic_update_slice(
            full, row.reshape(1, heads, 1, HD), (member, 0, run, 0)
        )
        return full.reshape(planes * count, rows_flat)

    bias_sums = jnp.sum(grad_qkv.astype(F32), 0)
    grad_gain_attn = jnp.sum(grad_normed * unit_all, 0)
    small_grads = jnp.concatenate(
        [to_heads(bias_sums[i * wide : (i + 1) * wide]) for i in range(3)]
        + [
            grad_gain_attn.reshape(-1, rows_flat),
            grad_gain_ffn.reshape(-1, rows_flat),
            grad_router_switch[:, count].reshape(-1, rows_flat),
            grad_router_switch[:, :count].reshape(planes * count, rows_flat * count),
        ],
        1,
    )
    small_sum = small_scatter(small_grads)
    pieces = [small_sum[i * rows_flat : (i + 1) * rows_flat] for i in range(6)]
    grad_router = small_sum[6 * rows_flat :].reshape(rows_flat, count)

    unit_one, scale_one = rms_unit(token_rows.astype(F32))
    grad_unit = grad_normed_own * gain_attn
    grad_tokens = grad_residual + scale_one * (
        grad_unit - unit_one * jnp.mean(grad_unit * unit_one, -1, keepdims=True)
    )
    return (
        out_tokens[None],
        grad_tokens.astype(BF16)[None],
        from_heads(0),
        from_heads(1),
        from_heads(2),
        grad_w_out,
        pieces[0],
        pieces[1],
        pieces[2],
        pieces[3],
        pieces[4],
        grad_router,
        grad_gate_w[:, fe_width:],
        grad_up_w[:, fe_width:],
        grad_down_w[fe_width:],
        pieces[5],
        grad_gate_w[None, :, :fe_width],
        grad_up_w[None, :, :fe_width],
        grad_down_w[None, :fe_width],
    )


def solution(mesh):
    every = ("dp", "context", "expert")
    plane = ("dp", "context")
    rows = P(("dp", "expert"), "context", None)
    groups = P(("dp", "expert"), None)
    return jax.shard_map(
        body,
        mesh=mesh,
        in_specs=(
            rows,
            rows,
            groups,
            groups,
            rows,
            *[P(every, None)] * 4,
            *[P(every)] * 5,
            P(every, None),
            P(plane, "expert"),
            P(plane, "expert"),
            P("expert", plane),
            P(every),
            P("expert", plane, None),
            P("expert", plane, None),
            P("expert", None, plane),
        ),
        out_specs=(
            rows,
            rows,
            *[P(every, None)] * 4,
            *[P(every)] * 5,
            P(every, None),
            P(plane, "expert"),
            P(plane, "expert"),
            P("expert", plane),
            P(every),
            P("expert", plane, None),
            P("expert", plane, None),
            P("expert", None, plane),
        ),
        check_vma=False,
    )
```

```python
import functools

import jax
import jax.numpy as jnp
from jax import lax
from jax.experimental import pallas as pl
from jax.experimental.pallas import tpu as pltpu
from jax.sharding import PartitionSpec as P

HD = 128

EPSILON = 1e-06
ROPE_BASE = 1000000.0
NEGATIVE = -1e30
F32 = jnp.float32
BF16 = jnp.bfloat16


def mat_dot(left_mat, right_mat):
    return jnp.dot(left_mat, right_mat, preferred_element_type=F32)


def left_dot(left_mat, right_mat):
    return lax.dot_general(
        left_mat, right_mat, (((0,), (0,)), ((), ())), preferred_element_type=F32
    )


def right_dot(left_mat, right_mat):
    return lax.dot_general(
        left_mat, right_mat, (((1,), (1,)), ((), ())), preferred_element_type=F32
    )


def shift(x, axis, step):
    n = lax.axis_size(axis)
    return lax.ppermute(x, axis, [(i, (i + step) % n) for i in range(n)])


def tie(value, others):
    return lax.optimization_barrier((value, others))


def plane_blocks():
    return (
        lax.axis_size("dp"),
        lax.axis_size("context"),
        lax.axis_index("dp"),
        lax.axis_index("context"),
    )


class Gather:
    def __init__(self, *own):
        self.own = list(own)
        self.half = own[0].shape[0] * len(own) // 2
        self.across, self.along = [{} for _ in own], [{} for _ in own]

    def send_across(self, h):
        nc = lax.axis_size("context")
        self.across[h] = {s: shift(self.own[h], "context", s) for s in range(1, nc)}

    def send_along(self, h):
        ndp = lax.axis_size("dp")
        self.along[h] = {d: shift(self.own[h], "dp", d) for d in range(1, ndp)}

    def send_far_along(self):
        ndp = lax.axis_size("dp")
        self.far_top = {
            (d, s): shift(x[: self.half], "dp", d)
            for s, x in self.across[0].items()
            for d in range(1, ndp)
        }

    def send_far_across(self):
        nc = lax.axis_size("context")
        self.far_bottom = {
            (d, s): shift(x[-self.half :], "context", s)
            for d, x in self.along[-1].items()
            for s in range(1, nc)
        }

    def direct(self):
        for h in range(len(self.own)):
            self.send_across(h)
            self.send_along(h)

    def far(self):
        self.send_far_along()
        self.send_far_across()


class Pieces:
    def __init__(self, gather):
        ndp, nc, dp, ctx = plane_blocks()
        found = []
        for h in range(len(gather.own)):
            found.append((0, 0, h, gather.own[h]))
            found += [(0, s, h, x) for s, x in gather.across[h].items()]
            found += [(d, 0, h, x) for d, x in gather.along[h].items()]
        found += [(*k, 0, x) for k, x in gather.far_top.items()]
        found += [(*k, 1, x) for k, x in gather.far_bottom.items()]
        self.half, self.columns = gather.half, gather.own[0].shape[1]
        self.arrays, self.counts, self.keys, self.found, places = [], [], [], {}, []
        for d, s, h, x in found:
            plane = lax.rem(dp - d + ndp, ndp) * nc + lax.rem(ctx - s + nc, nc)
            n = x.shape[0] // self.half
            self.arrays.append(x)
            self.counts.append(n)
            for i in range(n):
                self.keys.append((d, s, h + i))
                self.found[d, s, h + i] = (len(self.arrays) - 1, i * self.half)
                places.append(2 * plane + h + i)
        self.places = jnp.stack(places).astype(jnp.int32)


class Scatter:
    def __init__(self, halves_of):
        self.halves_of = halves_of

    def terms(self, keys, dtype):
        ndp, nc, dp, ctx = plane_blocks()
        numbers = [
            2 * (lax.rem(dp + d, ndp) * nc + lax.rem(ctx + s, nc)) + h for d, s, h in keys
        ]
        return dict(zip(keys, self.halves_of(numbers, dtype)))

    def far(self):
        ndp, nc, _, _ = plane_blocks()
        pairs = [(d, s) for d in range(1, ndp) for s in range(1, nc)]
        terms = self.terms([(*k, h) for k in pairs for h in range(2)], BF16)
        return (
            {k: shift(terms[*k, 0], "context", k[1]) for k in pairs},
            {k: shift(terms[*k, 1], "dp", k[0]) for k in pairs},
        )

    def free(self):
        ndp, nc, _, _ = plane_blocks()
        keys = [(0, s, 0) for s in range(1, nc)] + [(d, 0, 1) for d in range(1, ndp)]
        terms = self.terms(keys, BF16)
        return (
            [shift(terms[0, s, 0], "context", s) for s in range(1, nc)],
            [shift(terms[d, 0, 1], "dp", d) for d in range(1, ndp)],
        )

    def last(self, far):
        ndp, nc, _, _ = plane_blocks()
        keys = [(d, 0, 0) for d in range(1, ndp)] + [(0, s, 1) for s in range(1, nc)]
        terms = self.terms(keys + [(0, 0, 0), (0, 0, 1)], F32)
        self.own = [terms[0, 0, h] for h in range(2)]
        along, across = [], []
        for d in range(1, ndp):
            total = terms[d, 0, 0]
            for s in range(1, nc):
                total = total + far[0][d, s].astype(F32)
            along.append(shift(total.astype(BF16), "dp", d))
        for s in range(1, nc):
            total = terms[0, s, 1]
            for d in range(1, ndp):
                total = total + far[1][d, s].astype(F32)
            across.append(shift(total.astype(BF16), "context", s))
        return along, across

    def finish(self, free, last):
        out = []
        for h, pieces in enumerate((free[0] + last[0], free[1] + last[1])):
            total = self.own[h]
            for piece in pieces:
                total = total + piece.astype(F32)
            out.append(total)
        return jnp.concatenate(out, 0)


def doubling_steps(axis):
    n = lax.axis_size(axis)
    step = 1
    while step < n:
        yield step, [(i, i ^ step) for i in range(n)]
        step *= 2


def small_gather(x, axes):
    for axis in axes:
        place = lax.axis_index(axis)
        for step, pairs in doubling_steps(axis):
            other = lax.ppermute(x, axis, pairs)
            high = (place & step) != 0
            x = jnp.concatenate([jnp.where(high, other, x), jnp.where(high, x, other)], 0)
    return x


def small_scatter(x):
    for axis in ("dp", "context", "expert"):
        place = lax.axis_index(axis)
        for step, pairs in reversed(list(doubling_steps(axis))):
            half = x.shape[0] // 2
            high = (place & step) != 0
            low_part, high_part = x[:half], x[half:]
            other = lax.ppermute(jnp.where(high, low_part, high_part), axis, pairs)
            x = jnp.where(high, high_part, low_part) + other
    return x[0]


def core_exchange(x, group):
    count = lax.axis_size("expert")
    place = lax.rem(lax.axis_index("expert"), group)
    out = x
    for s in range(1, group):
        piece = lax.dynamic_slice_in_dim(x, lax.rem(place + s, group), 1)
        pairs = [(i, i // group * group + (i % group + s) % group) for i in range(count)]
        got = lax.ppermute(piece, "expert", pairs)
        out = lax.dynamic_update_slice_in_dim(out, got, lax.rem(place - s + group, group), 0)
    return out


LANES = 128
MIB = 1 << 20


def params(mib):
    return pltpu.CompilerParams(
        dimension_semantics=("arbitrary",), vmem_limit_bytes=mib * MIB
    )


def cost(flops, nbytes):
    return pl.CostEstimate(flops=flops, bytes_accessed=nbytes, transcendentals=0)


def assemble(places, full, refs, counts, half):
    i = 0
    for ref, n in zip(refs, counts):
        for k in range(n):
            start = pl.multiple_of(places[i] * half, half)
            full[pl.ds(start, half), :] = ref[k * half : (k + 1) * half, :]
            i += 1


def weight_grad_kernel(n, half, numbers, *refs):
    acts, grads, outs, turned = refs[:n], refs[n], refs[n + 1 : -1], refs[-1]

    @pl.when(pl.program_id(0) == 0)
    def _():
        for k in range(n):
            turned[k * half : (k + 1) * half, :] = acts[k][...].T

    total = mat_dot(turned[...], grads[...])
    for k in range(n):
        outs[k][...] = total[k * half : (k + 1) * half].astype(outs[k].dtype)


def weight_grad(acts, grads, numbers, half, dtype):
    m, columns = grads.shape
    n = len(numbers)
    tile = tile_of(m)

    def block(k):
        return pl.BlockSpec((m, half), lambda j, p: (0, p[k]))

    return pl.pallas_call(
        functools.partial(weight_grad_kernel, n, half),
        out_shape=[jax.ShapeDtypeStruct((half, columns), dtype)] * n,
        grid_spec=pltpu.PrefetchScalarGridSpec(
            num_scalar_prefetch=1,
            grid=(pl.cdiv(columns, tile),),
            in_specs=[block(k) for k in range(n)]
            + [pl.BlockSpec((m, tile), lambda j, p: (0, j))],
            out_specs=[pl.BlockSpec((half, tile), lambda j, p: (0, j))] * n,
            scratch_shapes=[pltpu.VMEM((n * half, m), BF16)],
        ),
        compiler_params=params(48),
        cost_estimate=cost(2 * m * n * half * columns, 12 * MIB),
        name="weight_grad",
    )(jnp.stack(numbers).astype(jnp.int32), *[acts] * n, grads)


def chunk(m):
    return min(m, 512)


def tile_of(m):
    return 768 if m <= 1024 else 256


def hidden_grad_kernel(counts, half, places, acts, *refs):
    out, full = refs[-2], refs[-1]
    assemble(places, full, refs[:-2], counts, half)
    step = chunk(acts.shape[0])

    @pl.loop(0, acts.shape[0] // step)
    def _(c):
        rows = pl.ds(pl.multiple_of(c * step, step), step)
        out[rows, :] = mat_dot(acts[rows, :], full[...])


def hidden_grad(acts, pieces):
    m, width = acts.shape
    tile_size = tile_of(m)
    tiles = pl.cdiv(pieces.columns, tile_size)
    return pl.pallas_call(
        functools.partial(hidden_grad_kernel, pieces.counts, pieces.half),
        out_shape=jax.ShapeDtypeStruct((m, pieces.columns), F32),
        grid_spec=pltpu.PrefetchScalarGridSpec(
            num_scalar_prefetch=1,
            grid=(tiles,),
            in_specs=[pl.BlockSpec((m, width), lambda j, p: (0, 0))]
            + [pl.BlockSpec((a.shape[0], tile_size), lambda j, p: (0, j)) for a in pieces.arrays],
            out_specs=pl.BlockSpec((m, tile_size), lambda j, p: (0, j)),
            scratch_shapes=[pltpu.VMEM((width, tile_size), BF16)],
        ),
        compiler_params=params(44),
        cost_estimate=cost(2 * m * width * pieces.columns, 20 * MIB),
        name="hidden_grad",
    )(pieces.places, acts, *pieces.arrays)


def fold(x):
    total = x[:, :LANES]
    for i in range(1, x.shape[1] // LANES):
        total = total + x[:, i * LANES : (i + 1) * LANES]
    return total


def ffn_kernel(g_counts, u_counts, half, tile, fe, count, columns, *refs):
    g_places, u_places, here, acts, router, kept, gh = refs[:7]
    refs, n = refs[7:], len(g_counts)
    gates, refs = refs[:n], refs[n:]
    ups, refs = refs[: len(u_counts)], refs[len(u_counts) :]
    scaled, gate_out, up_out, small = refs[:4]
    prob, share, switch, sum_e, sum_s, gate_full, up_full = refs[4:]
    step = chunk(acts.shape[0])
    j = pl.program_id(0)
    chunks = acts.shape[0] // step
    lane = lax.broadcasted_iota(jnp.int32, (1, LANES), 1)

    def rows_of(c):
        return pl.ds(pl.multiple_of(c * step, step), step)

    @pl.when(j == 0)
    def _():
        @pl.loop(0, chunks)
        def _(c):
            rows = rows_of(c)
            logits = mat_dot(acts[rows, :], router[...])
            sig = jax.nn.sigmoid(logits)
            masked = jnp.where(lane < count, logits, NEGATIVE)
            expo = jnp.exp(masked - jnp.max(masked, -1, keepdims=True))
            expo = jnp.where(lane < count, expo, 0.0)
            probs = expo / jnp.sum(expo, -1, keepdims=True)
            prob[rows, :] = probs
            own = jnp.sum(jnp.where(lane == here[0], probs, 0.0), -1, keepdims=True)
            share[rows, :] = own * kept[rows, :]
            switch[rows, :] = jnp.sum(jnp.where(lane == count, sig, 0.0), -1, keepdims=True)
            sum_e[rows, :] = jnp.zeros((step, LANES), F32)
            sum_s[rows, :] = jnp.zeros((step, LANES), F32)

    column = j * tile + lax.broadcasted_iota(jnp.int32, (1, tile), 1)
    routed = column < fe
    shared = (column >= fe) & (column < columns)
    assemble(g_places, gate_full, gates, g_counts, half)
    assemble(u_places, up_full, ups, u_counts, half)

    @pl.loop(0, chunks)
    def _(c):
        rows = rows_of(c)
        gate = mat_dot(acts[rows, :], gate_full[...])
        up = mat_dot(acts[rows, :], up_full[...])
        scale = jnp.where(routed, share[rows, :], switch[rows, :])
        sig = jax.nn.sigmoid(gate)
        silu = gate * sig
        hidden = silu * up
        grad = gh[rows, :]
        product = grad * hidden
        sum_e[rows, :] += fold(jnp.where(routed, product, 0.0))
        sum_s[rows, :] += fold(jnp.where(shared, product, 0.0))
        grad = grad * scale
        scaled[rows, :] = (scale * hidden).astype(BF16)
        gate_out[rows, :] = (grad * up * (sig + silu * (1.0 - sig))).astype(BF16)
        up_out[rows, :] = (grad * silu).astype(BF16)

    @pl.when(j == pl.num_programs(0) - 1)
    def _():
        @pl.loop(0, chunks)
        def _(c):
            rows = rows_of(c)
            grad_share = jnp.sum(sum_e[rows, :], -1, keepdims=True)
            grad_switch = jnp.sum(sum_s[rows, :], -1, keepdims=True)
            hot = (lane == here[0]).astype(F32)
            logit = grad_share * share[rows, :] * (hot - prob[rows, :])
            sw = switch[rows, :]
            pre = grad_switch * sw * (1.0 - sw)
            value = jnp.where(lane < count, logit, jnp.where(lane == count, pre, 0.0))
            small[rows, :] = value.astype(BF16)


def ffn(acts, router, kept, gh, here, gates, ups, fe, count):
    m, width = acts.shape
    columns = gates.columns
    tile_size = tile_of(m)
    tiles = pl.cdiv(columns, tile_size)
    whole = lambda j, g, u, h: (0, 0)
    tile = pl.BlockSpec((m, tile_size), lambda j, g, u, h: (0, j))
    weights = [
        pl.BlockSpec((a.shape[0], tile_size), lambda j, g, u, h: (0, j))
        for a in gates.arrays + ups.arrays
    ]
    hid = jax.ShapeDtypeStruct((m, columns), BF16)
    return pl.pallas_call(
        functools.partial(
            ffn_kernel, gates.counts, ups.counts, gates.half, tile_size, fe, count, columns
        ),
        out_shape=(hid, hid, hid, jax.ShapeDtypeStruct((m, LANES), BF16)),
        grid_spec=pltpu.PrefetchScalarGridSpec(
            num_scalar_prefetch=3,
            grid=(tiles,),
            in_specs=[
                pl.BlockSpec((m, width), whole),
                pl.BlockSpec((width, LANES), whole),
                pl.BlockSpec((m, 1), whole),
                tile,
            ]
            + weights,
            out_specs=[tile, tile, tile, pl.BlockSpec((m, LANES), whole)],
            scratch_shapes=[
                pltpu.VMEM((m, LANES), F32),
                pltpu.VMEM((m, 1), F32),
                pltpu.VMEM((m, 1), F32),
                pltpu.VMEM((m, LANES), F32),
                pltpu.VMEM((m, LANES), F32),
                pltpu.VMEM((width, tile_size), BF16),
                pltpu.VMEM((width, tile_size), BF16),
            ],
        ),
        compiler_params=params(52),
        cost_estimate=cost(4 * m * width * columns, 40 * MIB),
        name="ffn",
    )(gates.places, ups.places, here, acts, router, kept, gh, *gates.arrays, *ups.arrays)


def spread_kernel(arrays, half, extra, *refs):
    pairs = len(arrays)
    places, refs = refs[0], refs[1:]
    i = pl.program_id(0)
    acts, refs = refs[:pairs], refs[pairs:]
    weights = []
    for found in arrays:
        n = max(array for array, _ in found) + 1
        weights.append(refs[:n])
        refs = refs[n:]
    out, held = refs[-1 - pairs], refs[-pairs:]
    step = min(out.shape[0], 1024)
    for k in range(len(arrays[0])):

        @pl.when(i == k)
        def _(k=k):
            for pair in range(pairs):
                array, row = arrays[pair][k]
                held[pair][...] = weights[pair][array][row : row + half, :]

    @pl.loop(0, out.shape[0] // step)
    def _(c):
        rows = pl.ds(pl.multiple_of(c * step, step), step)
        total = right_dot(acts[0][rows, :], held[0][...])
        for pair in range(1, pairs):
            total += right_dot(acts[pair][rows, :], held[pair][...])
        if extra:
            total += right_dot(refs[0][rows, :], refs[1][...])
        out[rows, :] = total.astype(BF16)


def spread(pairs, extra=None):
    acts = [a for a, _ in pairs]
    first = pairs[0][1]
    half, steps = first.half, sum(first.counts)
    m = acts[0].shape[0]
    width = steps * half
    whole = lambda i, p: (0, 0)
    specs = [pl.BlockSpec(a.shape, whole) for a in acts]
    operands, arrays = list(acts), []
    for _, pieces in pairs:
        specs += [pl.BlockSpec(a.shape, whole) for a in pieces.arrays]
        operands += pieces.arrays
        arrays.append(tuple(pieces.found[k] for k in first.keys))
    if extra is not None:
        specs.append(pl.BlockSpec(extra[0].shape, whole))
        specs.append(pl.BlockSpec((half, LANES), lambda i, p: (p[i], 0)))
        operands += list(extra)
    return pl.pallas_call(
        functools.partial(spread_kernel, tuple(arrays), half, extra is not None),
        out_shape=jax.ShapeDtypeStruct((m, width), BF16),
        grid_spec=pltpu.PrefetchScalarGridSpec(
            num_scalar_prefetch=1,
            grid=(steps,),
            in_specs=specs,
            out_specs=pl.BlockSpec((m, half), lambda i, p: (0, p[i])),
            scratch_shapes=[pltpu.VMEM((half, first.columns), BF16)] * len(pairs),
        ),
        compiler_params=params(60),
        cost_estimate=cost(2 * m * width * first.columns * len(pairs), 20 * MIB),
        name="spread",
    )(first.places, *operands)


def turn(x):
    return pltpu.roll(x, HD // 2, 1)


def qkv_kernel(counts, half, wide, places, tok, gain, bias, cosine, sine, *refs):
    normed, query, key_value, inverse, full = refs[-5:]

    @pl.when(pl.program_id(0) == 0)
    def _():
        assemble(places, full, refs[:-5], counts, half)

    values = tok[...].astype(F32)
    inv = lax.rsqrt(jnp.mean(values * values, -1, keepdims=True) + EPSILON)
    inverse[...] = inv
    normed[...] = (values * inv * gain[...]).astype(BF16)
    out = mat_dot(normed[...], full[...]) + bias[...]
    for h in range(2 * wide // HD):
        head = out[:, h * HD : (h + 1) * HD]
        head = (head * cosine[...] + turn(head) * sine[...]).astype(BF16)
        if h < wide // HD:
            query[:, h * HD : (h + 1) * HD] = head
        else:
            key_value[:, h * HD - wide : (h + 1) * HD - wide] = head
    key_value[:, wide:] = out[:, 2 * wide :].astype(BF16)


def qkv_project(tok, gain, bias, cosine, sine, pieces, wide):
    m, width = tok.shape
    step = 256
    row = lambda i, p: (i, 0)
    whole = lambda i, p: (0, 0)
    return pl.pallas_call(
        functools.partial(qkv_kernel, pieces.counts, pieces.half, wide),
        out_shape=(
            jax.ShapeDtypeStruct((m, width), BF16),
            jax.ShapeDtypeStruct((m, wide), BF16),
            jax.ShapeDtypeStruct((m, 2 * wide), BF16),
            jax.ShapeDtypeStruct((m, 1), F32),
        ),
        grid_spec=pltpu.PrefetchScalarGridSpec(
            num_scalar_prefetch=1,
            grid=(m // step,),
            in_specs=[
                pl.BlockSpec((step, width), row),
                pl.BlockSpec((1, width), whole),
                pl.BlockSpec((1, 3 * wide), whole),
                pl.BlockSpec((step, HD), row),
                pl.BlockSpec((step, HD), row),
            ]
            + [pl.BlockSpec(a.shape, whole) for a in pieces.arrays],
            out_specs=[
                pl.BlockSpec((step, width), row),
                pl.BlockSpec((step, wide), row),
                pl.BlockSpec((step, 2 * wide), row),
                pl.BlockSpec((step, 1), row),
            ],
            scratch_shapes=[pltpu.VMEM((width, 3 * wide), BF16)],
        ),
        compiler_params=params(32),
        cost_estimate=cost(6 * m * width * wide, 12 * MIB),
        name="qkv_project",
    )(pieces.places, tok, gain, bias, cosine, sine, *pieces.arrays)


def head_probs(query, kvs, allowed, h):
    own = slice(h * HD, (h + 1) * HD)
    scores = jnp.concatenate([right_dot(query[:, own], kv[:, own]) for kv in kvs], -1)
    scores = jnp.where(allowed, scores * HD ** (-0.5), NEGATIVE)
    expo = jnp.exp(scores - jnp.max(scores, -1, keepdims=True))
    return expo / jnp.sum(expo, -1, keepdims=True)


def attend_kernel(nc, wide, query, allowed, w_o, *refs):
    kvs, mixed, out = refs[:nc], refs[nc], refs[nc + 1]
    tok = query.shape[0]
    for h in range(wide // HD):
        value = slice(wide + h * HD, wide + (h + 1) * HD)
        prob = head_probs(query, kvs, allowed[0] > 0.0, h).astype(BF16)
        total = mat_dot(prob[:, :tok], kvs[0][:, value])
        for s in range(1, nc):
            total += mat_dot(prob[:, s * tok : (s + 1) * tok], kvs[s][:, value])
        mixed[:, h * HD : (h + 1) * HD] = total.astype(BF16)
    out[...] = mat_dot(mixed[...], w_o[...]).astype(BF16)


def attend(query, kvs, allowed, w_o):
    m, wide = query.shape
    groups, tok, keys = allowed.shape
    width = w_o.shape[1]
    row = lambda g: (g, 0)
    return pl.pallas_call(
        functools.partial(attend_kernel, len(kvs), wide),
        out_shape=(
            jax.ShapeDtypeStruct((m, wide), BF16),
            jax.ShapeDtypeStruct((m, width), BF16),
        ),
        grid=(groups,),
        in_specs=[
            pl.BlockSpec((tok, wide), row),
            pl.BlockSpec((1, tok, keys), lambda g: (g, 0, 0)),
            pl.BlockSpec((wide, width), lambda g: (0, 0)),
        ]
        + [pl.BlockSpec((tok, 2 * wide), row)] * len(kvs),
        out_specs=[pl.BlockSpec((tok, wide), row), pl.BlockSpec((tok, width), row)],
        compiler_params=params(32),
        cost_estimate=cost(2 * m * width * wide + 4 * m * keys * wide, 8 * MIB),
        name="attend",
    )(query, allowed, w_o, *kvs)


def attend_back_kernel(nc, wide, query, allowed, w_o, grads, cosine, sine, *refs):
    kvs, grad_query, grad_own, grad_far = refs[:nc], refs[nc], refs[nc + 1], refs[nc + 2 :]
    tok = query.shape[0]
    grad_mixed = right_dot(grads[...], w_o[...]).astype(BF16)
    scale = HD ** (-0.5)
    for h in range(wide // HD):
        key = slice(h * HD, (h + 1) * HD)
        value = slice(wide + h * HD, wide + (h + 1) * HD)
        prob = head_probs(query, kvs, allowed[0] > 0.0, h)
        low = prob.astype(BF16)
        mixed = grad_mixed[:, key]
        grad = jnp.concatenate([right_dot(mixed, kv[:, value]) for kv in kvs], -1)
        inner = jnp.sum(grad * prob, -1, keepdims=True)
        grad = (prob * (grad - inner)).astype(BF16)
        total = None
        for s in range(nc):
            block = slice(s * tok, (s + 1) * tok)
            term = mat_dot(grad[:, block], kvs[s][:, key])
            total = term if total is None else total + term
            grad_key = left_dot(grad[:, block], query[:, key]) * scale
            grad_value = left_dot(low[:, block], mixed)
            if s == 0:
                grad_own[:, key] = grad_key
                grad_own[:, value] = grad_value
            else:
                grad_far[s - 1][:, key] = grad_key.astype(BF16)
                grad_far[s - 1][:, value] = grad_value.astype(BF16)
        total = total * scale
        total = total * cosine[...] - turn(total) * sine[...]
        grad_query[:, key] = total.astype(BF16)


def attend_back(query, kvs, allowed, w_o, grads, cosine, sine):
    m, wide = query.shape
    groups, tok, keys = allowed.shape
    width = w_o.shape[1]
    nc = len(kvs)
    row = lambda g: (g, 0)
    both = pl.BlockSpec((tok, 2 * wide), row)
    return pl.pallas_call(
        functools.partial(attend_back_kernel, nc, wide),
        out_shape=(
            jax.ShapeDtypeStruct((m, wide), BF16),
            jax.ShapeDtypeStruct((m, 2 * wide), F32),
            *[jax.ShapeDtypeStruct((m, 2 * wide), BF16)] * (nc - 1),
        ),
        grid=(groups,),
        in_specs=[
            pl.BlockSpec((tok, wide), row),
            pl.BlockSpec((1, tok, keys), lambda g: (g, 0, 0)),
            pl.BlockSpec((wide, width), lambda g: (0, 0)),
            pl.BlockSpec((tok, width), row),
            pl.BlockSpec((tok, HD), row),
            pl.BlockSpec((tok, HD), row),
        ]
        + [both] * nc,
        out_specs=[pl.BlockSpec((tok, wide), row)] + [both] * nc,
        compiler_params=params(32),
        cost_estimate=cost(2 * m * width * wide + 12 * m * keys * wide, 8 * MIB),
        name="attend_back",
    )(query, allowed, w_o, grads, cosine, sine, *kvs)


def join_kernel(wide, grad_query, grad_own, cosine, sine, *refs):
    far, out, sums = refs[:-2], refs[-2], refs[-1]
    total = grad_own[...]
    for ref in far:
        total = total + ref[...].astype(F32)
    out[:, :wide] = grad_query[...]
    for h in range(wide // HD):
        head = total[:, h * HD : (h + 1) * HD]
        head = head * cosine[...] - turn(head) * sine[...]
        out[:, wide + h * HD : wide + (h + 1) * HD] = head.astype(BF16)
    out[:, 2 * wide :] = total[:, wide:].astype(BF16)

    @pl.when(pl.program_id(0) == 0)
    def _():
        sums[...] = jnp.zeros_like(sums)

    sums[...] += jnp.sum(out[...].astype(F32), 0, keepdims=True)


def join(grad_query, grad_own, far, cosine, sine):
    m, wide = grad_query.shape
    step = 256
    row = lambda i: (i, 0)
    both = pl.BlockSpec((step, 2 * wide), row)
    return pl.pallas_call(
        functools.partial(join_kernel, wide),
        out_shape=(
            jax.ShapeDtypeStruct((m, 3 * wide), BF16),
            jax.ShapeDtypeStruct((1, 3 * wide), F32),
        ),
        grid=(m // step,),
        in_specs=[
            pl.BlockSpec((step, wide), row),
            both,
            pl.BlockSpec((step, HD), row),
            pl.BlockSpec((step, HD), row),
        ]
        + [both] * len(far),
        out_specs=[
            pl.BlockSpec((step, 3 * wide), row),
            pl.BlockSpec((1, 3 * wide), lambda i: (0, 0)),
        ],
        compiler_params=params(32),
        cost_estimate=cost(20 * m * wide, 6 * MIB),
        name="join",
    )(grad_query, grad_own, cosine, sine, *far)


def rms_unit(values):
    scaling = lax.rsqrt(jnp.mean(values * values, -1, keepdims=True) + EPSILON)
    return values * scaling, scaling


def body(
    tokens,
    cotangent,
    deal_order,
    seq_lengths,
    expert_ids,
    w_query,
    w_key,
    w_value,
    w_out,
    bias_query,
    bias_key,
    bias_value,
    norm_attn,
    norm_ffn,
    w_router,
    shared_gate,
    shared_up,
    shared_down,
    shared_switch,
    expert_gate,
    expert_up,
    expert_down,
):
    ndp, nc, dp, ctx = plane_blocks()
    planes = ndp * nc
    count = lax.axis_size("expert")
    here = lax.axis_index("expert")
    tok_count, width = tokens.shape[1], tokens.shape[2]
    group_tok = deal_order.shape[1]
    seqs = seq_lengths.shape[1]
    top = expert_ids.shape[2]
    rows_flat = w_query.shape[0]
    part = HD // rows_flat
    heads = planes // part
    runs = count // part
    run, member = here // part, lax.rem(here, part)
    fe_width = expert_gate.shape[2]
    fs_width = shared_gate.shape[1]
    pad = -(fe_width + fs_width) % LANES
    capacity = min(tok_count, 5 * tok_count * top // (4 * count))
    wide = heads * HD
    all_rows = count * tok_count
    block = width // planes

    token_rows = tokens[0]

    def by_head(w):
        w = w.reshape(rows_flat, part, heads, runs, HD).transpose(3, 1, 0, 2, 4)
        return w.reshape(count, rows_flat, wide)

    qkv_out = jnp.concatenate([by_head(w) for w in (w_query, w_key, w_value)], -1)
    all_tokens = lax.all_gather(token_rows, "expert", axis=0, tiled=True)
    qkv_rows = lax.all_to_all(qkv_out, "expert", split_axis=0, concat_axis=0, tiled=True)
    small = jnp.concatenate(
        [
            v.astype(F32).reshape(-1)
            for v in (
                bias_query,
                bias_key,
                bias_value,
                norm_attn,
                norm_ffn,
                shared_switch,
                w_router,
                deal_order,
                seq_lengths,
                expert_ids,
            )
        ]
    )
    small_plane = small_gather(small[None], ("context", "dp"))

    def stacked(routed, shared):
        none = jnp.zeros((routed.shape[0], pad), BF16)
        return jnp.concatenate([routed, shared, none], 1)

    def turned(routed, shared, h):
        columns = slice(h * block // 2, (h + 1) * block // 2)
        return stacked(routed[:, columns].T, shared[:, columns].T)

    def rows_half(x, h):
        return x[h * block // 2 : (h + 1) * block // 2]

    gate = Gather(stacked(expert_gate[0], shared_gate))
    up = Gather(
        *[stacked(rows_half(expert_up[0], h), rows_half(shared_up, h)) for h in range(2)]
    )
    down = Gather(*[turned(expert_down[0], shared_down, h) for h in range(2)])
    out_w = Gather(w_out)
    out_w.direct()
    gate.direct()
    qkv_own = qkv_rows.reshape(count * rows_flat, 3 * wide)
    qkv_own, (gate.across, gate.along, up.own, down.own, small_plane) = tie(
        qkv_own, (gate.across, gate.along, up.own, down.own, small_plane)
    )
    all_grads = lax.all_gather(
        tie(cotangent[0], qkv_own)[0], "expert", axis=0, tiled=True
    )
    qkv_w = Gather(qkv_own)
    qkv_w.direct()
    small_all = small_gather(small_plane.reshape(1, -1), ("expert",))
    small_all = small_all.reshape(count, ndp * nc, -1).transpose(1, 0, 2)
    small_all = small_all.reshape(ndp * nc * count, -1)
    qkv_w.far()
    qkv_pieces = Pieces(qkv_w)
    (out_w.across, out_w.along, gate.across, gate.along, down.own), _ = tie(
        (out_w.across, out_w.along, gate.across, gate.along, down.own),
        (qkv_w.far_top, qkv_w.far_bottom),
    )
    out_w.far()
    gate.far()
    down.send_along(0)
    wo_pieces = Pieces(out_w)
    wo_planes = jnp.zeros((2 * planes, rows_flat // 2, width), BF16)
    for key, number in zip(wo_pieces.keys, list(wo_pieces.places)):
        array, row = wo_pieces.found[key]
        array = wo_pieces.arrays[array][row : row + rows_flat // 2]
        wo_planes = lax.dynamic_update_slice_in_dim(wo_planes, array[None], number, 0)
    wo_mine = core_exchange(wo_planes.reshape(part, heads, rows_flat, width), part)
    w_o = wo_mine.transpose(1, 0, 2, 3).reshape(wide, width)

    columns = {}
    place = 0
    for name in ("bq", "bk", "bv", "na", "nf", "sw"):
        columns[name] = small_all[:, place : place + rows_flat].reshape(-1)
        place += rows_flat
    router = small_all[:, place : place + rows_flat * count].reshape(-1, count).astype(BF16)
    place += rows_flat * count
    plane_small = lax.dynamic_index_in_dim(
        small_all.reshape(ndp, nc, count, -1), dp, 0, keepdims=False
    )
    order = plane_small[0, :, place : place + group_tok].astype(jnp.int32)
    place += group_tok
    lengths = plane_small[0, :, place : place + seqs].astype(jnp.int32)
    place += seqs
    ids = plane_small[..., place:].reshape(nc, count, tok_count, top).astype(jnp.int32)
    gain_attn, gain_ffn = columns["na"], columns["nf"]
    router_switch = jnp.concatenate(
        [
            router,
            columns["sw"].astype(BF16)[:, None],
            jnp.zeros((width, LANES - count - 1), BF16),
        ],
        1,
    )

    local_index = ctx * tok_count + jnp.arange(tok_count, dtype=jnp.int32)
    ends = jnp.cumsum(lengths, 1)
    starts = ends - lengths

    def segments(index):
        segment = jnp.sum((index[None, :, None] >= ends[:, None, :]).astype(jnp.int32), -1)
        hot = segment[..., None] == jnp.arange(seqs, dtype=jnp.int32)
        return segment, index[None, :] - jnp.sum(jnp.where(hot, starts[:, None, :], 0), -1)

    query_segment, position = segments(local_index)
    allowed = []
    for s in range(nc):
        key_index = local_index - s * tok_count
        key_segment, _ = segments(key_index)
        allowed.append(
            (query_segment[:, :, None] == key_segment[:, None, :])
            & (key_index[None, None, :] <= local_index[None, :, None])
            & (key_index >= 0)[None, None, :]
        )
    allowed = jnp.concatenate(allowed, -1).astype(F32)
    frequency = ROPE_BASE ** (-2.0 * jnp.arange(HD // 2, dtype=F32) / HD)
    angles = position.reshape(-1).astype(F32)[:, None] * frequency[None, :]
    cosine = jnp.concatenate([jnp.cos(angles)] * 2, -1)
    sine = jnp.sin(angles)
    sine_table = jnp.concatenate([-sine, sine], -1)

    def own_heads(row):
        row = row.reshape(part, heads, runs, HD)
        row = lax.dynamic_index_in_dim(row, member, 0, keepdims=False)
        return lax.dynamic_index_in_dim(row, run, 1, keepdims=False).reshape(-1)

    bias = jnp.concatenate([own_heads(columns[k]) for k in ("bq", "bk", "bv")])
    normed, queries, key_value, inverse = qkv_project(
        all_tokens, gain_attn[None], bias[None], cosine, sine_table, qkv_pieces, wide
    )
    kvs = [key_value] + [
        lax.ppermute(key_value, "context", [(i, i + s) for i in range(nc - s)])
        for s in range(1, nc)
    ]
    kvs, (gate.far_top, gate.far_bottom, down.along, down.own, all_grads) = tie(
        kvs, (gate.far_top, gate.far_bottom, down.along, down.own, all_grads)
    )
    down.send_across(0)
    down.send_along(1)
    down.send_across(1)
    up.send_along(0)
    mixed, attn_part = attend(queries, kvs, allowed, w_o)
    attn_out = lax.psum_scatter(attn_part, "expert", scatter_dimension=0, tiled=True)
    attn_out, (down.across, down.along, up.along, up.own) = tie(
        attn_out, (down.across, down.along, up.along, up.own)
    )
    up.send_across(0)
    up.send_along(1)
    down.send_far_along()
    up.send_across(1)
    residual = token_rows.astype(F32) + attn_out.astype(F32)
    unit_two, scale_two = rms_unit(residual)
    rows = lax.all_gather(
        (unit_two * gain_ffn).astype(BF16), "expert", axis=0, tiled=True
    )
    rows, (up.across, up.along, down.far_top) = tie(
        rows, (up.across, up.along, down.far_top)
    )
    down.send_far_across()
    up.far()

    (ids, order), _ = tie((ids, order), key_value)
    hit = jnp.any(ids == here, -1)
    below = jnp.arange(tok_count)[:, None] < jnp.arange(tok_count)[None, :]
    slot = mat_dot(hit.reshape(nc * count, tok_count).astype(BF16), below.astype(BF16))
    kept = (hit & (slot.reshape(nc, count, tok_count) < capacity)).astype(F32)
    kept = kept.transpose(1, 0, 2).reshape(count, group_tok)
    kept_rows = jnp.sum(
        jnp.where(order[:, None, :] == local_index[None, :, None], kept[:, None, :], 0.0), -1
    ).reshape(all_rows)

    gate_pieces, up_pieces, down_pieces = Pieces(gate), Pieces(up), Pieces(down)
    gh = hidden_grad(all_grads, down_pieces)
    scaled, grad_gate, grad_up, grad_small = ffn(
        rows,
        router_switch,
        kept_rows[:, None],
        gh,
        here.astype(jnp.int32)[None],
        gate_pieces,
        up_pieces,
        fe_width,
        count,
    )
    def halves_of(acts, grads):
        return lambda numbers, dtype: weight_grad(acts, grads, numbers, block // 2, dtype)

    down_sum = Scatter(halves_of(all_grads, scaled))
    gate_sum = Scatter(halves_of(rows, grad_gate))
    up_sum = Scatter(halves_of(rows, grad_up))
    down_far, down_free = down_sum.far(), down_sum.free()
    grad_rows = spread([(grad_gate, gate_pieces), (grad_up, up_pieces)], (grad_small, router_switch))
    grad_rows, down_far = tie(grad_rows, down_far)
    grad_normed_two = lax.psum_scatter(
        grad_rows, "expert", scatter_dimension=0, tiled=True
    ).astype(F32)
    down_last = down_sum.last(down_far)
    grad_normed_two, (down_free, down_last) = tie(
        grad_normed_two, (down_free, down_last)
    )
    gate_free, gate_far = gate_sum.free(), gate_sum.far()
    grad_router_switch = left_dot(rows, grad_small)

    grad_unit = grad_normed_two * gain_ffn
    grad_residual = cotangent[0].astype(F32) + scale_two * (
        grad_unit - unit_two * jnp.mean(grad_unit * unit_two, -1, keepdims=True)
    )
    grad_gain_ffn = jnp.sum(grad_normed_two * unit_two, 0)
    attn_own = grad_residual.astype(BF16)
    grad_attn = lax.all_gather(attn_own, "expert", axis=0, tiled=True)
    output = lax.psum_scatter(
        spread([(tie(scaled, attn_own)[0], down_pieces)]),
        "expert",
        scatter_dimension=0,
        tiled=True,
    )
    grad_attn, (gate_free, gate_far) = tie(grad_attn, (gate_free, gate_far))
    gate_last = gate_sum.last(gate_far)
    up_free = up_sum.free()
    grad_query, grad_own, *grad_far = attend_back(
        queries, kvs, allowed, w_o, grad_attn, cosine, sine_table
    )
    grad_far, (up_free, gate_last, down_last) = tie(
        grad_far, (up_free, gate_last, down_last)
    )
    grad_down_w = down_sum.finish(down_free, down_last)
    grad_far = [
        lax.ppermute(piece, "context", [(i + s, i) for i in range(nc - s)])
        for s, piece in enumerate(grad_far, 1)
    ]
    up_far = up_sum.far()
    grad_qkv, bias_sums = join(grad_query, grad_own, grad_far, cosine, sine_table)
    grad_qkv, (output, gate_last, mixed) = tie(grad_qkv, (output, gate_last, mixed))
    grad_gate_w = gate_sum.finish(gate_free, gate_last)
    out_tokens = (residual + output.astype(F32)).astype(BF16)
    grad_normed = spread([(grad_qkv, qkv_pieces)])
    grad_normed_own = lax.psum_scatter(
        grad_normed, "expert", scatter_dimension=0, tiled=True
    ).astype(F32)

    qkv_sum = Scatter(halves_of(normed, grad_qkv))
    qkv_far, qkv_free = qkv_sum.far(), qkv_sum.free()
    qkv_far, up_far = tie(qkv_far, up_far)
    qkv_last = qkv_sum.last(qkv_far)
    qkv_last, up_far = tie(qkv_last, up_far)
    up_last = up_sum.last(up_far)
    qkv_grad_rows = qkv_sum.finish(qkv_free, qkv_last)
    grad_up_w = up_sum.finish(up_free, up_last)
    qkv_back = lax.all_to_all(
        qkv_grad_rows.astype(BF16).reshape(count, rows_flat, 3 * wide),
        "expert",
        split_axis=0,
        concat_axis=0,
        tiled=True,
    )

    def from_heads(i):
        w = qkv_back[..., i * wide : (i + 1) * wide].astype(F32)
        w = w.reshape(runs, part, rows_flat, heads, HD).transpose(2, 1, 3, 0, 4)
        return w.reshape(rows_flat, width)

    grad_wo = left_dot(mixed, grad_attn).astype(BF16).reshape(heads, part, rows_flat, width)
    wo_back = core_exchange(grad_wo.transpose(1, 0, 2, 3), part)
    wo_back = wo_back.reshape(2 * planes, rows_flat // 2, width)
    wo_sum = Scatter(
        lambda numbers, dtype: [
            lax.dynamic_index_in_dim(wo_back, i, 0, keepdims=False).astype(dtype)
            for i in numbers
        ]
    )
    grad_w_out = wo_sum.finish(wo_sum.free(), wo_sum.last(wo_sum.far()))

    def to_heads(row):
        full = jnp.zeros((part, heads, runs, HD), F32)
        full = lax.dynamic_update_slice(
            full, row.reshape(1, heads, 1, HD), (member, 0, run, 0)
        )
        return full.reshape(planes * count, rows_flat)

    bias_sums = bias_sums[0]
    grad_gain_attn = jnp.sum(
        grad_normed.astype(F32) * (all_tokens.astype(F32) * inverse), 0
    )
    small_grads = jnp.concatenate(
        [to_heads(bias_sums[i * wide : (i + 1) * wide]) for i in range(3)]
        + [
            grad_gain_attn.reshape(-1, rows_flat),
            grad_gain_ffn.reshape(-1, rows_flat),
            grad_router_switch[:, count].reshape(-1, rows_flat),
            grad_router_switch[:, :count].reshape(planes * count, rows_flat * count),
        ],
        1,
    )
    small_sum = small_scatter(small_grads)
    pieces = [small_sum[i * rows_flat : (i + 1) * rows_flat] for i in range(6)]
    grad_router = small_sum[6 * rows_flat :].reshape(rows_flat, count)

    unit_one, scale_one = rms_unit(token_rows.astype(F32))
    grad_unit = grad_normed_own * gain_attn
    grad_tokens = grad_residual + scale_one * (
        grad_unit - unit_one * jnp.mean(grad_unit * unit_one, -1, keepdims=True)
    )
    return (
        out_tokens[None],
        grad_tokens.astype(BF16)[None],
        from_heads(0),
        from_heads(1),
        from_heads(2),
        grad_w_out,
        pieces[0],
        pieces[1],
        pieces[2],
        pieces[3],
        pieces[4],
        grad_router,
        grad_gate_w[:, fe_width : fe_width + fs_width],
        grad_up_w[:, fe_width : fe_width + fs_width],
        grad_down_w[:, fe_width : fe_width + fs_width].T,
        pieces[5],
        grad_gate_w[None, :, :fe_width],
        grad_up_w[None, :, :fe_width],
        grad_down_w[:, :fe_width].T[None],
    )


def solution(mesh):
    every = ("dp", "context", "expert")
    plane = ("dp", "context")
    rows = P(("dp", "expert"), "context", None)
    groups = P(("dp", "expert"), None)
    return jax.shard_map(
        body,
        mesh=mesh,
        in_specs=(
            rows,
            rows,
            groups,
            groups,
            rows,
            *[P(every, None)] * 4,
            *[P(every)] * 5,
            P(every, None),
            P(plane, "expert"),
            P(plane, "expert"),
            P("expert", plane),
            P(every),
            P("expert", plane, None),
            P("expert", plane, None),
            P("expert", None, plane),
        ),
        out_specs=(
            rows,
            rows,
            *[P(every, None)] * 4,
            *[P(every)] * 5,
            P(every, None),
            P(plane, "expert"),
            P(plane, "expert"),
            P("expert", plane),
            P(every),
            P("expert", plane, None),
            P("expert", plane, None),
            P("expert", None, plane),
        ),
        check_vma=False,
    )
```

```python
import functools

import jax
import jax.numpy as jnp
from jax import lax
from jax.experimental import pallas as pl
from jax.experimental.pallas import tpu as pltpu
from jax.sharding import PartitionSpec as P

HD = 128

EPSILON = 1e-06
ROPE_BASE = 1000000.0
NEGATIVE = -1e30
F32 = jnp.float32
BF16 = jnp.bfloat16


def mat_dot(left_mat, right_mat):
    return jnp.dot(left_mat, right_mat, preferred_element_type=F32)


def left_dot(left_mat, right_mat):
    return lax.dot_general(
        left_mat, right_mat, (((0,), (0,)), ((), ())), preferred_element_type=F32
    )


def right_dot(left_mat, right_mat):
    return lax.dot_general(
        left_mat, right_mat, (((1,), (1,)), ((), ())), preferred_element_type=F32
    )


def shift(x, axis, step):
    n = lax.axis_size(axis)
    return lax.ppermute(x, axis, [(i, (i + step) % n) for i in range(n)])


def tie(value, others):
    return lax.optimization_barrier((value, others))


def plane_blocks():
    return (
        lax.axis_size("dp"),
        lax.axis_size("context"),
        lax.axis_index("dp"),
        lax.axis_index("context"),
    )


def by_context(block_of):
    nc = lax.axis_size("context")
    return {s: shift(block_of(s), "context", s) for s in range(1, nc)}


def by_dp(block_of):
    ndp = lax.axis_size("dp")
    return {d: shift(block_of(d), "dp", d) for d in range(1, ndp)}


class Pieces:
    def __init__(self, found, half):
        ndp, nc, dp, ctx = plane_blocks()
        keys = sorted(found)
        self.parts = [found[key] for key in keys]
        self.arrays = [array for array, _ in self.parts]
        self.half, self.columns = half, self.arrays[0].shape[1]
        self.places = jnp.stack(
            [
                2 * (lax.rem(dp - d + ndp, ndp) * nc + lax.rem(ctx - s + nc, nc)) + h
                for d, s, h in keys
            ]
        ).astype(jnp.int32)


def gather_plain(own):
    half = own.shape[0] // 2
    across, along = by_context(lambda s: own), by_dp(lambda d: own)

    def far(after=None):
        tops = [x[:half] for x in across.values()]
        bottoms = [x[half:] for x in along.values()]
        if after is not None:
            (tops, bottoms), _ = tie((tops, bottoms), after)
        far_x = by_context(lambda s: jnp.concatenate(bottoms, 0))
        far_y = by_dp(lambda d: jnp.concatenate(tops, 0))
        found = {(0, 0, h): (own, h) for h in range(2)}
        for s, x in across.items():
            found.update({(0, s, h): (x, h) for h in range(2)})
        for d, x in along.items():
            found.update({(d, 0, h): (x, h) for h in range(2)})
            found.update({(d, s, 0): (far_y[d], s - 1) for s in across})
            found.update({(d, s, 1): (far_x[s], d - 1) for s in across})
        return found, (far_x, far_y)

    return across, along, far


class Scatter:
    def __init__(self, halves_of, half):
        self.halves_of, self.half = halves_of, half

    def make(self, first=True, last=True):
        ndp, nc, dp, ctx = plane_blocks()
        across, along = range(1, nc), range(1, ndp)

        def group(keys, dtype):
            return [
                2 * (lax.rem(dp + d, ndp) * nc + lax.rem(ctx + s, nc)) + h for d, s, h in keys
            ], dtype

        groups = []
        if first:
            groups += [group([*((d, s, 0) for d in along), (0, s, 0)], BF16) for s in across]
            groups += [group([*((d, s, 1) for s in across), (d, 0, 1)], BF16) for d in along]
        if last:
            groups += [group([(0, s, 1)], F32) for s in across]
            groups += [group([(d, 0, 0)], F32) for d in along]
            groups.append(group([(0, 0, 0), (0, 0, 1)], F32))
        made = list(self.halves_of(groups))
        if first:
            self.to_across = dict(zip(across, made))
            self.to_along = dict(zip(along, made[nc - 1 :]))
            made = made[nc - 1 + ndp - 1 :]
        if last:
            self.near_across = dict(zip(across, made))
            self.near_along = dict(zip(along, made[nc - 1 :]))
            self.own = made[-1]
        return made

    def send_first(self, after=()):
        (across, along), _ = tie((self.to_across, self.to_along), after)
        self.across = by_context(lambda s: across[s])
        self.along = by_dp(lambda d: along[d])
        return self.across, self.along

    def row(self, x, i):
        return x[i * self.half : (i + 1) * self.half].astype(F32)

    def sums(self):
        across = {
            s: (x + sum(self.row(y, s - 1) for y in self.along.values())).astype(BF16)
            for s, x in self.near_across.items()
        }
        along = {
            d: (x + sum(self.row(y, d - 1) for y in self.across.values())).astype(BF16)
            for d, x in self.near_along.items()
        }
        return across, along

    def finish(self, last):
        ndp, nc, _, _ = plane_blocks()
        across, along = last
        top, bottom = self.own[: self.half], self.own[self.half :]
        for x in self.across.values():
            top = top + self.row(x, ndp - 1)
        for x in along.values():
            top = top + x.astype(F32)
        for x in self.along.values():
            bottom = bottom + self.row(x, nc - 1)
        for x in across.values():
            bottom = bottom + x.astype(F32)
        return jnp.concatenate([top, bottom], 0)


def join_last(scatters):
    sums = [scatter.sums() for scatter in scatters]
    return (
        {s: jnp.concatenate([x[0][s] for x in sums], 0) for s in sums[0][0]},
        {d: jnp.concatenate([x[1][d] for x in sums], 0) for d in sums[0][1]},
    )


def send_last(scatters, blocks=None):
    to_across, to_along = join_last(scatters) if blocks is None else blocks
    across = by_context(lambda s: to_across[s])
    along = by_dp(lambda d: to_along[d])
    split, start = [], 0
    for scatter in scatters:
        rows = slice(start, start + scatter.half)
        split.append(
            ({s: x[rows] for s, x in across.items()}, {d: x[rows] for d, x in along.items()})
        )
        start += scatter.half
    return split


def doubling_steps(axis):
    n = lax.axis_size(axis)
    step = 1
    while step < n:
        yield step, [(i, i ^ step) for i in range(n)]
        step *= 2


def small_gather(x, axes):
    for axis in axes:
        place = lax.axis_index(axis)
        for step, pairs in doubling_steps(axis):
            other = lax.ppermute(x, axis, pairs)
            high = (place & step) != 0
            x = jnp.concatenate([jnp.where(high, other, x), jnp.where(high, x, other)], 0)
    return x


def small_scatter(x, axes):
    for axis in axes:
        place = lax.axis_index(axis)
        for step, pairs in reversed(list(doubling_steps(axis))):
            half = x.shape[0] // 2
            high = (place & step) != 0
            low_part, high_part = x[:half], x[half:]
            other = lax.ppermute(jnp.where(high, low_part, high_part), axis, pairs)
            x = jnp.where(high, high_part, low_part) + other
    return x


def core_exchange(x, group):
    count = lax.axis_size("expert")
    place = lax.rem(lax.axis_index("expert"), group)
    out = x
    for s in range(1, group):
        piece = lax.dynamic_slice_in_dim(x, lax.rem(place + s, group), 1)
        pairs = [(i, i // group * group + (i % group + s) % group) for i in range(count)]
        got = lax.ppermute(piece, "expert", pairs)
        out = lax.dynamic_update_slice_in_dim(out, got, lax.rem(place - s + group, group), 0)
    return out


LANES = 128
SCALE = 2
MIB = 1 << 20


def params(mib):
    return pltpu.CompilerParams(
        dimension_semantics=("arbitrary",), vmem_limit_bytes=mib * MIB
    )


def cost(flops, nbytes):
    return pl.CostEstimate(
        flops=flops // SCALE, bytes_accessed=nbytes // SCALE, transcendentals=0
    )


def assemble(places, full, refs, half):
    for i, ref in enumerate(refs):
        full[pl.ds(pl.multiple_of(places[i] * half, half), half), :] = ref[...]


def weight_grad_kernel(counts, half, numbers, *refs):
    n = sum(counts)
    acts, grads, outs, turned = refs[:n], refs[n], refs[n + 1 : -1], refs[-1]
    spots = [(out, i) for out, c in zip(outs, counts) for i in range(c)]

    @pl.when(pl.program_id(0) == 0)
    def _():
        for k in range(n):
            turned[k * half : (k + 1) * half, :] = acts[k][...].T

    step = min(n, max(1, 1024 // half))
    for first in range(0, n, step):
        some = spots[first : first + step]
        total = mat_dot(turned[first * half : (first + len(some)) * half, :], grads[...])
        for i, (out, at) in enumerate(some):
            out[at * half : (at + 1) * half, :] = total[i * half : (i + 1) * half].astype(
                out.dtype
            )


def weight_grad(acts, grads, groups, half):
    m, columns = grads.shape
    numbers = [number for some, _ in groups for number in some]
    counts = tuple(len(some) for some, _ in groups)
    tile = tile_of(m)

    def block(k):
        return pl.BlockSpec((m, half), lambda j, p: (0, p[k]))

    return pl.pallas_call(
        functools.partial(weight_grad_kernel, counts, half),
        out_shape=[
            jax.ShapeDtypeStruct((len(some) * half, columns), dtype) for some, dtype in groups
        ],
        grid_spec=pltpu.PrefetchScalarGridSpec(
            num_scalar_prefetch=1,
            grid=(pl.cdiv(columns, tile),),
            in_specs=[block(k) for k in range(len(numbers))]
            + [pl.BlockSpec((m, tile), lambda j, p: (0, j))],
            out_specs=[pl.BlockSpec((c * half, tile), lambda j, p: (0, j)) for c in counts],
            scratch_shapes=[pltpu.VMEM((len(numbers) * half, m), BF16)],
        ),
        compiler_params=params(52),
        cost_estimate=cost(2 * m * len(numbers) * half * columns, 12 * MIB),
        name="weight_grad",
    )(jnp.stack(numbers).astype(jnp.int32), *[acts] * len(numbers), grads)


def chunk(m):
    return min(m, 512)


def tile_of(m):
    return 768 if m <= 1024 else 256


def hidden_grad_kernel(half, places, acts, *refs):
    out, full = refs[-2], refs[-1]
    assemble(places, full, refs[:-2], half)
    step = chunk(acts.shape[0])

    @pl.loop(0, acts.shape[0] // step)
    def _(c):
        rows = pl.ds(pl.multiple_of(c * step, step), step)
        out[rows, :] = mat_dot(acts[rows, :], full[...])


def hidden_grad(acts, pieces):
    m, width = acts.shape
    tile_size = tile_of(m)
    tiles = pl.cdiv(pieces.columns, tile_size)
    return pl.pallas_call(
        functools.partial(hidden_grad_kernel, pieces.half),
        out_shape=jax.ShapeDtypeStruct((m, pieces.columns), F32),
        grid_spec=pltpu.PrefetchScalarGridSpec(
            num_scalar_prefetch=1,
            grid=(tiles,),
            in_specs=[pl.BlockSpec((m, width), lambda j, p: (0, 0))]
            + [
                pl.BlockSpec((pieces.half, tile_size), lambda j, p, r=r: (r, j))
                for _, r in pieces.parts
            ],
            out_specs=pl.BlockSpec((m, tile_size), lambda j, p: (0, j)),
            scratch_shapes=[pltpu.VMEM((width, tile_size), BF16)],
        ),
        compiler_params=params(44),
        cost_estimate=cost(2 * m * width * pieces.columns, 20 * MIB),
        name="hidden_grad",
    )(pieces.places, acts, *pieces.arrays)


def fold(x):
    total = x[:, :LANES]
    for i in range(1, x.shape[1] // LANES):
        total = total + x[:, i * LANES : (i + 1) * LANES]
    return total


def ffn_kernel(n, half, tile, fe, count, columns, *refs):
    places, here, acts, router, kept, gh = refs[:6]
    gates, ups, refs = refs[6 : 6 + n], refs[6 + n : 6 + 2 * n], refs[6 + 2 * n :]
    scaled, gate_out, up_out, small = refs[:4]
    prob, share, switch, sum_e, sum_s, gate_full, up_full = refs[4:]
    step = chunk(acts.shape[0])
    j = pl.program_id(0)
    chunks = acts.shape[0] // step
    lane = lax.broadcasted_iota(jnp.int32, (1, LANES), 1)

    def rows_of(c):
        return pl.ds(pl.multiple_of(c * step, step), step)

    @pl.when(j == 0)
    def _():
        @pl.loop(0, chunks)
        def _(c):
            rows = rows_of(c)
            logits = mat_dot(acts[rows, :], router[...])
            sig = jax.nn.sigmoid(logits)
            masked = jnp.where(lane < count, logits, NEGATIVE)
            expo = jnp.exp(masked - jnp.max(masked, -1, keepdims=True))
            expo = jnp.where(lane < count, expo, 0.0)
            probs = expo / jnp.sum(expo, -1, keepdims=True)
            prob[rows, :] = probs
            own = jnp.sum(jnp.where(lane == here[0], probs, 0.0), -1, keepdims=True)
            share[rows, :] = own * kept[rows, :]
            switch[rows, :] = jnp.sum(jnp.where(lane == count, sig, 0.0), -1, keepdims=True)
            sum_e[rows, :] = jnp.zeros((step, LANES), F32)
            sum_s[rows, :] = jnp.zeros((step, LANES), F32)

    column = j * tile + lax.broadcasted_iota(jnp.int32, (1, tile), 1)
    routed = column < fe
    shared = (column >= fe) & (column < columns)
    assemble(places, gate_full, gates, half)
    assemble(places, up_full, ups, half)

    @pl.loop(0, chunks)
    def _(c):
        rows = rows_of(c)
        gate = mat_dot(acts[rows, :], gate_full[...])
        up = mat_dot(acts[rows, :], up_full[...])
        scale = jnp.where(routed, share[rows, :], switch[rows, :])
        sig = jax.nn.sigmoid(gate)
        silu = gate * sig
        hidden = silu * up
        grad = gh[rows, :]
        product = grad * hidden
        sum_e[rows, :] += fold(jnp.where(routed, product, 0.0))
        sum_s[rows, :] += fold(jnp.where(shared, product, 0.0))
        grad = grad * scale
        scaled[rows, :] = (scale * hidden).astype(BF16)
        gate_out[rows, :] = (grad * up * (sig + silu * (1.0 - sig))).astype(BF16)
        up_out[rows, :] = (grad * silu).astype(BF16)

    @pl.when(j == pl.num_programs(0) - 1)
    def _():
        @pl.loop(0, chunks)
        def _(c):
            rows = rows_of(c)
            grad_share = jnp.sum(sum_e[rows, :], -1, keepdims=True)
            grad_switch = jnp.sum(sum_s[rows, :], -1, keepdims=True)
            hot = (lane == here[0]).astype(F32)
            logit = grad_share * share[rows, :] * (hot - prob[rows, :])
            sw = switch[rows, :]
            pre = grad_switch * sw * (1.0 - sw)
            value = jnp.where(lane < count, logit, jnp.where(lane == count, pre, 0.0))
            small[rows, :] = value.astype(BF16)


def ffn(acts, router, kept, gh, here, gates, ups, fe, count):
    m, width = acts.shape
    columns = gates.columns
    tile_size = tile_of(m)
    tiles = pl.cdiv(columns, tile_size)
    whole = lambda j, p, h: (0, 0)
    tile = pl.BlockSpec((m, tile_size), lambda j, p, h: (0, j))
    weights = [
        pl.BlockSpec((gates.half, tile_size), lambda j, p, h, r=r: (r, j))
        for _, r in gates.parts + ups.parts
    ]
    hid = jax.ShapeDtypeStruct((m, columns), BF16)
    return pl.pallas_call(
        functools.partial(
            ffn_kernel, len(gates.parts), gates.half, tile_size, fe, count, columns
        ),
        out_shape=(hid, hid, hid, jax.ShapeDtypeStruct((m, LANES), BF16)),
        grid_spec=pltpu.PrefetchScalarGridSpec(
            num_scalar_prefetch=2,
            grid=(tiles,),
            in_specs=[
                pl.BlockSpec((m, width), whole),
                pl.BlockSpec((width, LANES), whole),
                pl.BlockSpec((m, 1), whole),
                tile,
            ]
            + weights,
            out_specs=[tile, tile, tile, pl.BlockSpec((m, LANES), whole)],
            scratch_shapes=[
                pltpu.VMEM((m, LANES), F32),
                pltpu.VMEM((m, 1), F32),
                pltpu.VMEM((m, 1), F32),
                pltpu.VMEM((m, LANES), F32),
                pltpu.VMEM((m, LANES), F32),
                pltpu.VMEM((width, tile_size), BF16),
                pltpu.VMEM((width, tile_size), BF16),
            ],
        ),
        compiler_params=params(52),
        cost_estimate=cost(4 * m * width * columns, 40 * MIB),
        name="ffn",
    )(gates.places, here, acts, router, kept, gh, *gates.arrays, *ups.arrays)


def spread_kernel(n, pairs, extra, places, *refs):
    i = pl.program_id(0)
    acts, refs = refs[:pairs], refs[pairs:]
    weights, refs = [refs[k * n : (k + 1) * n] for k in range(pairs)], refs[pairs * n :]
    out, held = refs[-1 - pairs], refs[-pairs:]
    step = min(out.shape[0], 1024)
    for k in range(n):

        @pl.when(i == k)
        def _(k=k):
            for pair in range(pairs):
                held[pair][...] = weights[pair][k][...]

    @pl.loop(0, out.shape[0] // step)
    def _(c):
        rows = pl.ds(pl.multiple_of(c * step, step), step)
        total = right_dot(acts[0][rows, :], held[0][...])
        for pair in range(1, pairs):
            total += right_dot(acts[pair][rows, :], held[pair][...])
        if extra:
            total += right_dot(refs[0][rows, :], refs[1][...])
        out[rows, :] = total.astype(BF16)


def spread(pairs, extra=None, weight=1):
    acts = [a for a, _ in pairs]
    first = pairs[0][1]
    half, steps = first.half, len(first.parts)
    m = acts[0].shape[0]
    width = steps * half
    whole = lambda i, p: (0, 0)
    specs = [pl.BlockSpec(a.shape, whole) for a in acts]
    operands = list(acts)
    for _, pieces in pairs:
        specs += [
            pl.BlockSpec((half, pieces.columns), lambda i, p, r=r: (r, 0))
            for _, r in pieces.parts
        ]
        operands += pieces.arrays
    if extra is not None:
        specs.append(pl.BlockSpec(extra[0].shape, whole))
        specs.append(pl.BlockSpec((half, LANES), lambda i, p: (p[i], 0)))
        operands += list(extra)
    return pl.pallas_call(
        functools.partial(spread_kernel, steps, len(pairs), extra is not None),
        out_shape=jax.ShapeDtypeStruct((m, width), BF16),
        grid_spec=pltpu.PrefetchScalarGridSpec(
            num_scalar_prefetch=1,
            grid=(steps,),
            in_specs=specs,
            out_specs=pl.BlockSpec((m, half), lambda i, p: (0, p[i])),
            scratch_shapes=[pltpu.VMEM((half, first.columns), BF16)] * len(pairs),
        ),
        compiler_params=params(60),
        cost_estimate=cost(2 * weight * m * width * first.columns * len(pairs), 20 * MIB),
        name="spread",
    )(first.places, *operands)


def turn(x):
    return pltpu.roll(x, HD // 2, 1)


def qkv_kernel(half, wide, places, tok, gain, bias, cosine, sine, *refs):
    normed, query, key_value, full = refs[-4:]

    @pl.when(pl.program_id(0) == 0)
    def _():
        assemble(places, full, refs[:-4], half)

    values = tok[...].astype(F32)
    inv = lax.rsqrt(jnp.mean(values * values, -1, keepdims=True) + EPSILON)
    normed[...] = (values * inv * gain[...]).astype(BF16)
    out = mat_dot(normed[...], full[...]) + bias[...]
    for h in range(2 * wide // HD):
        head = out[:, h * HD : (h + 1) * HD]
        head = (head * cosine[...] + turn(head) * sine[...]).astype(BF16)
        if h < wide // HD:
            query[:, h * HD : (h + 1) * HD] = head
        else:
            key_value[:, h * HD - wide : (h + 1) * HD - wide] = head
    key_value[:, wide:] = out[:, 2 * wide :].astype(BF16)


def qkv_project(tok, gain, bias, cosine, sine, pieces, wide):
    m, width = tok.shape
    step = 256
    row = lambda i, p: (i, 0)
    whole = lambda i, p: (0, 0)
    return pl.pallas_call(
        functools.partial(qkv_kernel, pieces.half, wide),
        out_shape=(
            jax.ShapeDtypeStruct((m, width), BF16),
            jax.ShapeDtypeStruct((m, wide), BF16),
            jax.ShapeDtypeStruct((m, 2 * wide), BF16),
        ),
        grid_spec=pltpu.PrefetchScalarGridSpec(
            num_scalar_prefetch=1,
            grid=(m // step,),
            in_specs=[
                pl.BlockSpec((step, width), row),
                pl.BlockSpec((1, width), whole),
                pl.BlockSpec((1, 3 * wide), whole),
                pl.BlockSpec((step, HD), row),
                pl.BlockSpec((step, HD), row),
            ]
            + [
                pl.BlockSpec((pieces.half, 3 * wide), lambda i, p, r=r: (r, 0))
                for _, r in pieces.parts
            ],
            out_specs=[
                pl.BlockSpec((step, width), row),
                pl.BlockSpec((step, wide), row),
                pl.BlockSpec((step, 2 * wide), row),
            ],
            scratch_shapes=[pltpu.VMEM((width, 3 * wide), BF16)],
        ),
        compiler_params=params(32),
        cost_estimate=cost(6 * m * width * wide, 12 * MIB),
        name="qkv_project",
    )(pieces.places, tok, gain, bias, cosine, sine, *pieces.arrays)


def head_probs(query, kvs, allowed, h):
    own = slice(h * HD, (h + 1) * HD)
    scores = jnp.concatenate([right_dot(query[:, own], kv[:, own]) for kv in kvs], -1)
    scores = jnp.where(allowed, scores * HD ** (-0.5), NEGATIVE)
    expo = jnp.exp(scores - jnp.max(scores, -1, keepdims=True))
    return expo / jnp.sum(expo, -1, keepdims=True)


def attend_kernel(nc, wide, query, allowed, w_o, *refs):
    kvs, mixed, out = refs[:nc], refs[nc], refs[nc + 1]
    tok = query.shape[0]
    for h in range(wide // HD):
        value = slice(wide + h * HD, wide + (h + 1) * HD)
        prob = head_probs(query, kvs, allowed[0] > 0.0, h).astype(BF16)
        total = mat_dot(prob[:, :tok], kvs[0][:, value])
        for s in range(1, nc):
            total += mat_dot(prob[:, s * tok : (s + 1) * tok], kvs[s][:, value])
        mixed[:, h * HD : (h + 1) * HD] = total.astype(BF16)
    out[...] = mat_dot(mixed[...], w_o[...]).astype(BF16)


def attend(query, kvs, allowed, w_o):
    m, wide = query.shape
    groups, tok, keys = allowed.shape
    width = w_o.shape[1]
    row = lambda g: (g, 0)
    return pl.pallas_call(
        functools.partial(attend_kernel, len(kvs), wide),
        out_shape=(
            jax.ShapeDtypeStruct((m, wide), BF16),
            jax.ShapeDtypeStruct((m, width), BF16),
        ),
        grid=(groups,),
        in_specs=[
            pl.BlockSpec((tok, wide), row),
            pl.BlockSpec((1, tok, keys), lambda g: (g, 0, 0)),
            pl.BlockSpec((wide, width), lambda g: (0, 0)),
        ]
        + [pl.BlockSpec((tok, 2 * wide), row)] * len(kvs),
        out_specs=[pl.BlockSpec((tok, wide), row), pl.BlockSpec((tok, width), row)],
        compiler_params=params(32),
        cost_estimate=cost(2 * m * width * wide + 4 * m * keys * wide, 8 * MIB),
        name="attend",
    )(query, allowed, w_o, *kvs)


def attend_back_kernel(nc, wide, query, allowed, w_o, grads, cosine, sine, *refs):
    kvs, grad_query, grad_own, grad_far = refs[:nc], refs[nc], refs[nc + 1], refs[nc + 2 :]
    tok = query.shape[0]
    grad_mixed = right_dot(grads[...], w_o[...]).astype(BF16)
    scale = HD ** (-0.5)
    for h in range(wide // HD):
        key = slice(h * HD, (h + 1) * HD)
        value = slice(wide + h * HD, wide + (h + 1) * HD)
        prob = head_probs(query, kvs, allowed[0] > 0.0, h)
        low = prob.astype(BF16)
        mixed = grad_mixed[:, key]
        grad = jnp.concatenate([right_dot(mixed, kv[:, value]) for kv in kvs], -1)
        inner = jnp.sum(grad * prob, -1, keepdims=True)
        grad = (prob * (grad - inner)).astype(BF16)
        total = None
        for s in range(nc):
            block = slice(s * tok, (s + 1) * tok)
            term = mat_dot(grad[:, block], kvs[s][:, key])
            total = term if total is None else total + term
            grad_key = left_dot(grad[:, block], query[:, key]) * scale
            grad_value = left_dot(low[:, block], mixed)
            if s == 0:
                grad_own[:, key] = grad_key
                grad_own[:, value] = grad_value
            else:
                grad_far[s - 1][:, key] = grad_key.astype(BF16)
                grad_far[s - 1][:, value] = grad_value.astype(BF16)
        total = total * scale
        total = total * cosine[...] - turn(total) * sine[...]
        grad_query[:, key] = total.astype(BF16)


def attend_back(query, kvs, allowed, w_o, grads, cosine, sine):
    m, wide = query.shape
    groups, tok, keys = allowed.shape
    width = w_o.shape[1]
    nc = len(kvs)
    row = lambda g: (g, 0)
    both = pl.BlockSpec((tok, 2 * wide), row)
    return pl.pallas_call(
        functools.partial(attend_back_kernel, nc, wide),
        out_shape=(
            jax.ShapeDtypeStruct((m, wide), BF16),
            jax.ShapeDtypeStruct((m, 2 * wide), F32),
            *[jax.ShapeDtypeStruct((m, 2 * wide), BF16)] * (nc - 1),
        ),
        grid=(groups,),
        in_specs=[
            pl.BlockSpec((tok, wide), row),
            pl.BlockSpec((1, tok, keys), lambda g: (g, 0, 0)),
            pl.BlockSpec((wide, width), lambda g: (0, 0)),
            pl.BlockSpec((tok, width), row),
            pl.BlockSpec((tok, HD), row),
            pl.BlockSpec((tok, HD), row),
        ]
        + [both] * nc,
        out_specs=[pl.BlockSpec((tok, wide), row)] + [both] * nc,
        compiler_params=params(32),
        cost_estimate=cost(2 * m * width * wide + 12 * m * keys * wide, 8 * MIB),
        name="attend_back",
    )(query, allowed, w_o, grads, cosine, sine, *kvs)


def join_kernel(wide, grad_query, grad_own, cosine, sine, *refs):
    far, out, sums = refs[:-2], refs[-2], refs[-1]
    total = grad_own[...]
    for ref in far:
        total = total + ref[...].astype(F32)
    out[:, :wide] = grad_query[...]
    for h in range(wide // HD):
        head = total[:, h * HD : (h + 1) * HD]
        head = head * cosine[...] - turn(head) * sine[...]
        out[:, wide + h * HD : wide + (h + 1) * HD] = head.astype(BF16)
    out[:, 2 * wide :] = total[:, wide:].astype(BF16)

    @pl.when(pl.program_id(0) == 0)
    def _():
        sums[...] = jnp.zeros_like(sums)

    sums[...] += jnp.sum(out[...].astype(F32), 0, keepdims=True)


def join(grad_query, grad_own, far, cosine, sine):
    m, wide = grad_query.shape
    step = 256
    row = lambda i: (i, 0)
    both = pl.BlockSpec((step, 2 * wide), row)
    return pl.pallas_call(
        functools.partial(join_kernel, wide),
        out_shape=(
            jax.ShapeDtypeStruct((m, 3 * wide), BF16),
            jax.ShapeDtypeStruct((1, 3 * wide), F32),
        ),
        grid=(m // step,),
        in_specs=[
            pl.BlockSpec((step, wide), row),
            both,
            pl.BlockSpec((step, HD), row),
            pl.BlockSpec((step, HD), row),
        ]
        + [both] * len(far),
        out_specs=[
            pl.BlockSpec((step, 3 * wide), row),
            pl.BlockSpec((1, 3 * wide), lambda i: (0, 0)),
        ],
        compiler_params=params(32),
        cost_estimate=cost(20 * m * wide, 6 * MIB),
        name="join",
    )(grad_query, grad_own, cosine, sine, *far)


def rms_unit(values):
    scaling = lax.rsqrt(jnp.mean(values * values, -1, keepdims=True) + EPSILON)
    return values * scaling, scaling


def body(
    tokens,
    cotangent,
    deal_order,
    seq_lengths,
    expert_ids,
    w_query,
    w_key,
    w_value,
    w_out,
    bias_query,
    bias_key,
    bias_value,
    norm_attn,
    norm_ffn,
    w_router,
    shared_gate,
    shared_up,
    shared_down,
    shared_switch,
    expert_gate,
    expert_up,
    expert_down,
):
    ndp, nc, dp, ctx = plane_blocks()
    planes = ndp * nc
    count = lax.axis_size("expert")
    here = lax.axis_index("expert")
    tok_count, width = tokens.shape[1], tokens.shape[2]
    group_tok = deal_order.shape[1]
    seqs = seq_lengths.shape[1]
    top = expert_ids.shape[2]
    rows_flat = w_query.shape[0]
    part = HD // rows_flat
    heads = planes // part
    runs = count // part
    run, member = here // part, lax.rem(here, part)
    fe_width = expert_gate.shape[2]
    fs_width = shared_gate.shape[1]
    pad = -(fe_width + fs_width) % LANES
    capacity = min(tok_count, 5 * tok_count * top // (4 * count))
    wide = heads * HD
    all_rows = count * tok_count
    block = width // planes

    token_rows = tokens[0]

    def by_head(w):
        w = w.reshape(rows_flat, part, heads, runs, HD).transpose(3, 1, 0, 2, 4)
        return w.reshape(count, rows_flat, wide)

    qkv_out = jnp.concatenate([by_head(w) for w in (w_query, w_key, w_value)], -1)
    all_tokens = lax.all_gather(token_rows, "expert", axis=0, tiled=True)
    qkv_rows = lax.all_to_all(qkv_out, "expert", split_axis=0, concat_axis=0, tiled=True)
    small = jnp.concatenate(
        [
            v.astype(F32).reshape(-1)
            for v in (
                bias_query,
                bias_key,
                bias_value,
                norm_attn,
                norm_ffn,
                shared_switch,
                w_router,
                deal_order,
                seq_lengths,
                expert_ids,
            )
        ]
    )

    weights, _ = tie((expert_up, shared_up, expert_down, shared_down), qkv_out)
    expert_up, shared_up, expert_down, shared_down = weights

    def stacked(routed, shared):
        none = jnp.zeros((routed.shape[0], pad), BF16)
        return jnp.concatenate([routed, shared, none], 1)

    def turned(routed, shared, h):
        columns = slice(h * block // 2, (h + 1) * block // 2)
        return stacked(routed[:, columns].T, shared[:, columns].T)

    def rows_half(x, h):
        return x[h * block // 2 : (h + 1) * block // 2]

    hb = block // 2
    gate_own = stacked(expert_gate[0], shared_gate)
    d_top, d_low = [turned(expert_down[0], shared_down, h) for h in range(2)]
    u_top, u_low = [stacked(rows_half(expert_up[0], h), rows_half(shared_up, h)) for h in range(2)]
    pair_own = jnp.concatenate([d_top, d_low, u_top, u_low], 0)
    wo_across, wo_along, wo_far = gather_plain(w_out)
    gate_across, gate_along, gate_far = gather_plain(gate_own)
    small, pair_own = tie(small, pair_own)
    small_plane = small_gather(small[None], ("context", "dp"))
    qkv_own = qkv_rows.reshape(count * rows_flat, 3 * wide)
    qkv_own, _ = tie(qkv_own, (gate_across, gate_along, pair_own))
    small_plane, _ = tie(small_plane, qkv_own)
    all_grads = lax.all_gather(
        tie(cotangent[0], qkv_own)[0], "expert", axis=0, tiled=True
    )
    _, _, qkv_far = gather_plain(qkv_own)
    small_all = small_gather(small_plane.reshape(1, -1), ("expert",))
    small_all = small_all.reshape(count, ndp * nc, -1).transpose(1, 0, 2)
    small_all = small_all.reshape(ndp * nc * count, -1)
    qkv_found, qkv_sent = qkv_far()
    qkv_pieces = Pieces(qkv_found, qkv_own.shape[0] // 2)
    wo_found, _ = wo_far(qkv_sent)
    gate_found, gate_sent = gate_far(qkv_sent)
    gate_pieces = Pieces(gate_found, hb)
    columns = {}
    place = 0
    for name in ("bq", "bk", "bv", "na", "nf", "sw"):
        columns[name] = small_all[:, place : place + rows_flat].reshape(-1)
        place += rows_flat
    router = small_all[:, place : place + rows_flat * count].reshape(-1, count).astype(BF16)
    place += rows_flat * count
    plane_small = lax.dynamic_index_in_dim(
        small_all.reshape(ndp, nc, count, -1), dp, 0, keepdims=False
    )
    order = plane_small[0, :, place : place + group_tok].astype(jnp.int32)
    place += group_tok
    lengths = plane_small[0, :, place : place + seqs].astype(jnp.int32)
    place += seqs
    ids = plane_small[..., place:].reshape(nc, count, tok_count, top).astype(jnp.int32)
    gain_attn, gain_ffn = columns["na"], columns["nf"]
    router_switch = jnp.concatenate(
        [
            router,
            columns["sw"].astype(BF16)[:, None],
            jnp.zeros((width, LANES - count - 1), BF16),
        ],
        1,
    )

    local_index = ctx * tok_count + jnp.arange(tok_count, dtype=jnp.int32)
    ends = jnp.cumsum(lengths, 1)
    starts = ends - lengths

    def segments(index):
        segment = jnp.sum((index[None, :, None] >= ends[:, None, :]).astype(jnp.int32), -1)
        hot = segment[..., None] == jnp.arange(seqs, dtype=jnp.int32)
        return segment, index[None, :] - jnp.sum(jnp.where(hot, starts[:, None, :], 0), -1)

    query_segment, position = segments(local_index)
    allowed = []
    for s in range(nc):
        key_index = local_index - s * tok_count
        key_segment, _ = segments(key_index)
        allowed.append(
            (query_segment[:, :, None] == key_segment[:, None, :])
            & (key_index[None, None, :] <= local_index[None, :, None])
            & (key_index >= 0)[None, None, :]
        )
    allowed = jnp.concatenate(allowed, -1).astype(F32)
    frequency = ROPE_BASE ** (-2.0 * jnp.arange(HD // 2, dtype=F32) / HD)
    angles = position.reshape(-1).astype(F32)[:, None] * frequency[None, :]
    cosine = jnp.concatenate([jnp.cos(angles)] * 2, -1)
    sine = jnp.sin(angles)
    sine_table = jnp.concatenate([-sine, sine], -1)

    def own_heads(row):
        row = row.reshape(part, heads, runs, HD)
        row = lax.dynamic_index_in_dim(row, member, 0, keepdims=False)
        return lax.dynamic_index_in_dim(row, run, 1, keepdims=False).reshape(-1)

    bias = jnp.concatenate([own_heads(columns[k]) for k in ("bq", "bk", "bv")])
    normed, queries, key_value = qkv_project(
        all_tokens, gain_attn[None], bias[None], cosine, sine_table, qkv_pieces, wide
    )
    kvs = [key_value] + [
        lax.ppermute(key_value, "context", [(i, i + s) for i in range(nc - s)])
        for s in range(1, nc)
    ]
    wo_arrays, _ = tie({k: array for k, (array, _) in wo_found.items()}, key_value)
    wo_found = {k: (wo_arrays[k], row) for k, (_, row) in wo_found.items()}
    wo_pieces = Pieces(wo_found, rows_flat // 2)
    wo_planes = jnp.zeros((2 * planes, rows_flat // 2, width), BF16)
    for (array, row), number in zip(wo_pieces.parts, list(wo_pieces.places)):
        array = array[row * rows_flat // 2 : (row + 1) * rows_flat // 2]
        wo_planes = lax.dynamic_update_slice_in_dim(wo_planes, array[None], number, 0)
    wo_mine = core_exchange(wo_planes.reshape(part, heads, rows_flat, width), part)
    w_o = wo_mine.transpose(1, 0, 2, 3).reshape(wide, width)

    kvs, (pair_own, _) = tie(kvs, (pair_own, (gate_sent, all_grads)))
    x_one, y_one = by_context(lambda s: pair_own), by_dp(lambda d: pair_own)
    mixed, attn_part = attend(queries, kvs, allowed, w_o)
    attn_out = lax.psum_scatter(attn_part, "expert", scatter_dimension=0, tiled=True)
    attn_out, _ = tie(attn_out, (x_one, y_one))
    x_two = by_context(
        lambda s: jnp.concatenate([y[hb : 2 * hb] for y in y_one.values()], 0)
    )
    y_two = by_dp(lambda d: jnp.concatenate([x[:hb] for x in x_one.values()], 0))
    residual = token_rows.astype(F32) + attn_out.astype(F32)
    unit_two, scale_two = rms_unit(residual)
    rows = lax.all_gather(
        (unit_two * gain_ffn).astype(BF16), "expert", axis=0, tiled=True
    )
    rows, _ = tie(rows, (x_two, y_two))
    x_far = [y[3 * hb :] for y in y_one.values()]
    y_far = [x[2 * hb : 3 * hb] for x in x_one.values()]
    x_three = by_context(lambda s: jnp.concatenate(x_far, 0))
    y_three = by_dp(lambda d: jnp.concatenate(y_far, 0))
    down_found = {(0, 0, h): (pair_own, h) for h in range(2)}
    up_found = {(0, 0, h): (pair_own, 2 + h) for h in range(2)}
    for s, x in x_one.items():
        down_found.update({(0, s, h): (x, h) for h in range(2)})
        up_found.update({(0, s, h): (x, 2 + h) for h in range(2)})
    for d, y in y_one.items():
        down_found.update({(d, 0, h): (y, h) for h in range(2)})
        up_found.update({(d, 0, h): (y, 2 + h) for h in range(2)})
        for s in x_one:
            down_found.update({(d, s, 0): (y_two[d], s - 1), (d, s, 1): (x_two[s], d - 1)})
            up_found.update({(d, s, 0): (y_three[d], s - 1), (d, s, 1): (x_three[s], d - 1)})
    down_pieces, up_pieces = Pieces(down_found, hb), Pieces(up_found, hb)

    (ids, order), _ = tie((ids, order), key_value)
    hit = jnp.any(ids == here, -1)
    below = jnp.arange(tok_count)[:, None] < jnp.arange(tok_count)[None, :]
    slot = mat_dot(hit.reshape(nc * count, tok_count).astype(BF16), below.astype(BF16))
    kept = (hit & (slot.reshape(nc, count, tok_count) < capacity)).astype(F32)
    kept = kept.transpose(1, 0, 2).reshape(count, group_tok)
    kept_rows = jnp.sum(
        jnp.where(order[:, None, :] == local_index[None, :, None], kept[:, None, :], 0.0), -1
    ).reshape(all_rows)

    gh = hidden_grad(all_grads, down_pieces)
    scaled, grad_gate, grad_up, grad_small = ffn(
        rows,
        router_switch,
        kept_rows[:, None],
        gh,
        here.astype(jnp.int32)[None],
        gate_pieces,
        up_pieces,
        fe_width,
        count,
    )
    def scatter_of(acts, grads):
        return Scatter(lambda groups: weight_grad(acts, grads, groups, hb), hb)

    down_sum = scatter_of(all_grads, scaled)
    gate_sum = scatter_of(rows, grad_gate)
    down_sum.make(last=False)
    down_sent = down_sum.send_first()
    grad_rows = spread([(grad_gate, gate_pieces), (grad_up, up_pieces)], (grad_small, router_switch))
    grad_rows, _ = tie(grad_rows, down_sent)
    grad_normed_two = lax.psum_scatter(
        grad_rows, "expert", scatter_dimension=0, tiled=True
    ).astype(F32)
    gate_sum.make(last=False)
    gate_sent = gate_sum.send_first()
    terms = [down_sum.make(first=False), gate_sum.make(first=False)]
    up_sum = scatter_of(rows, grad_up)
    terms.append(up_sum.make())
    grad_normed_two, _ = tie(grad_normed_two, (gate_sent, terms))
    up_sent = up_sum.send_first()
    grad_router_switch = left_dot(rows, grad_small)

    grad_unit = grad_normed_two * gain_ffn
    grad_residual = cotangent[0].astype(F32) + scale_two * (
        grad_unit - unit_two * jnp.mean(grad_unit * unit_two, -1, keepdims=True)
    )
    grad_gain_ffn = jnp.sum(grad_normed_two * unit_two, 0)
    attn_own = grad_residual.astype(BF16)
    grad_attn = lax.all_gather(attn_own, "expert", axis=0, tiled=True)
    grad_attn, _ = tie(grad_attn, up_sent)
    grad_query, grad_own, *grad_far = attend_back(
        queries, kvs, allowed, w_o, grad_attn, cosine, sine_table
    )
    (mixed, scaled), _ = tie((mixed, scaled), grad_query)
    out_part = spread([(scaled, down_pieces)], weight=4)
    three = [down_sum, gate_sum, up_sum]
    blocks = join_last(three)
    grad_own, _ = tie(grad_own, (out_part, blocks))
    output = lax.psum_scatter(out_part, "expert", scatter_dimension=0, tiled=True)
    grad_wo = left_dot(mixed, grad_attn).astype(BF16).reshape(heads, part, rows_flat, width)
    wo_back = core_exchange(grad_wo.transpose(1, 0, 2, 3), part)
    wo_back = wo_back.reshape(2 * planes, rows_flat // 2, width)
    grad_far = [
        lax.ppermute(piece, "context", [(i + s, i) for i in range(nc - s)])
        for s, piece in enumerate(grad_far, 1)
    ]
    grad_qkv, bias_sums = join(grad_query, grad_own, grad_far, cosine, sine_table)
    grad_qkv, wo_back = tie(grad_qkv, wo_back)
    out_tokens = (residual + output.astype(F32)).astype(BF16)
    def to_heads(row):
        full = jnp.zeros((part, heads, runs, HD), F32)
        full = lax.dynamic_update_slice(
            full, row.reshape(1, heads, 1, HD), (member, 0, run, 0)
        )
        return full.reshape(planes * count, rows_flat)

    bias_sums = bias_sums[0]
    small_grads = jnp.concatenate(
        [to_heads(bias_sums[i * wide : (i + 1) * wide]) for i in range(3)]
        + [
            grad_gain_ffn.reshape(-1, rows_flat),
            grad_router_switch[:, count].reshape(-1, rows_flat),
            grad_router_switch[:, :count].reshape(planes * count, rows_flat * count),
        ],
        1,
    )

    wo_sum = Scatter(
        lambda groups: [
            jnp.concatenate(
                [lax.dynamic_index_in_dim(wo_back, i, 0, keepdims=False) for i in some], 0
            ).astype(dtype)
            for some, dtype in groups
        ],
        rows_flat // 2,
    )
    wo_sum.make()
    qkv_sum = scatter_of(normed, grad_qkv)
    lasts = send_last(three, tie(blocks, grad_far)[0])
    down_last, gate_last, up_last = lasts
    qkv_sum.make()
    qkv_sent = qkv_sum.send_first(lasts)
    wo_sum.send_first(lasts)
    small_sum = small_scatter(tie(small_grads, lasts)[0], ("dp", "context"))
    (wo_last,) = send_last([wo_sum])
    (qkv_last,) = send_last([qkv_sum])
    grad_normed = spread([(grad_qkv, qkv_pieces)])
    grad_normed_own = lax.psum_scatter(
        grad_normed, "expert", scatter_dimension=0, tiled=True
    ).astype(F32)
    grad_normed_own, _ = tie(grad_normed_own, (qkv_last, up_last))

    qkv_grad_rows = qkv_sum.finish(qkv_last)
    grad_gate_w = gate_sum.finish(gate_last)
    grad_down_w = down_sum.finish(down_last)
    grad_w_out = wo_sum.finish(wo_last)
    grad_up_w = up_sum.finish(up_last)
    qkv_back = lax.all_to_all(
        qkv_grad_rows.astype(BF16).reshape(count, rows_flat, 3 * wide),
        "expert",
        split_axis=0,
        concat_axis=0,
        tiled=True,
    )

    def from_heads(i):
        w = qkv_back[..., i * wide : (i + 1) * wide].astype(F32)
        w = w.reshape(runs, part, rows_flat, heads, HD).transpose(2, 1, 3, 0, 4)
        return w.reshape(rows_flat, width)

    small_sum, _ = tie(small_sum, (qkv_last, up_last))
    small_sum = small_scatter(small_sum, ("expert",))[0]
    pieces = [small_sum[i * rows_flat : (i + 1) * rows_flat] for i in range(5)]
    grad_router = small_sum[5 * rows_flat :].reshape(rows_flat, count)

    w_grads = [from_heads(i) for i in range(3)]
    grad_gain_attn = sum(
        jnp.sum(w.astype(F32) * grad, 1)
        for w, grad in zip((w_query, w_key, w_value), w_grads)
    ) / norm_attn.astype(F32)

    unit_one, scale_one = rms_unit(token_rows.astype(F32))
    grad_unit = grad_normed_own * gain_attn
    grad_tokens = grad_residual + scale_one * (
        grad_unit - unit_one * jnp.mean(grad_unit * unit_one, -1, keepdims=True)
    )
    return (
        out_tokens[None],
        grad_tokens.astype(BF16)[None],
        *w_grads,
        grad_w_out,
        pieces[0],
        pieces[1],
        pieces[2],
        grad_gain_attn,
        pieces[3],
        grad_router,
        grad_gate_w[:, fe_width : fe_width + fs_width],
        grad_up_w[:, fe_width : fe_width + fs_width],
        grad_down_w[:, fe_width : fe_width + fs_width].T,
        pieces[4],
        grad_gate_w[None, :, :fe_width],
        grad_up_w[None, :, :fe_width],
        grad_down_w[:, :fe_width].T[None],
    )


def solution(mesh):
    every = ("dp", "context", "expert")
    plane = ("dp", "context")
    rows = P(("dp", "expert"), "context", None)
    groups = P(("dp", "expert"), None)
    return jax.shard_map(
        body,
        mesh=mesh,
        in_specs=(
            rows,
            rows,
            groups,
            groups,
            rows,
            *[P(every, None)] * 4,
            *[P(every)] * 5,
            P(every, None),
            P(plane, "expert"),
            P(plane, "expert"),
            P("expert", plane),
            P(every),
            P("expert", plane, None),
            P("expert", plane, None),
            P("expert", None, plane),
        ),
        out_specs=(
            rows,
            rows,
            *[P(every, None)] * 4,
            *[P(every)] * 5,
            P(every, None),
            P(plane, "expert"),
            P(plane, "expert"),
            P("expert", plane),
            P(every),
            P("expert", plane, None),
            P("expert", plane, None),
            P("expert", None, plane),
        ),
        check_vma=False,
    )
```

```python
import functools

import jax
import jax.numpy as jnp
from jax import lax
from jax.experimental import pallas as pl
from jax.experimental.pallas import tpu as pltpu
from jax.sharding import PartitionSpec as P

HD = 128

EPSILON = 1e-06
ROPE_BASE = 1000000.0
NEGATIVE = -1e30
F32 = jnp.float32
BF16 = jnp.bfloat16


def mat_dot(left_mat, right_mat):
    return jnp.dot(left_mat, right_mat, preferred_element_type=F32)


def left_dot(left_mat, right_mat):
    return lax.dot_general(
        left_mat, right_mat, (((0,), (0,)), ((), ())), preferred_element_type=F32
    )


def right_dot(left_mat, right_mat):
    return lax.dot_general(
        left_mat, right_mat, (((1,), (1,)), ((), ())), preferred_element_type=F32
    )


def shift(x, axis, step):
    n = lax.axis_size(axis)
    return lax.ppermute(x, axis, [(i, (i + step) % n) for i in range(n)])


def tie(value, others):
    return lax.optimization_barrier((value, others))


def plane_blocks():
    return (
        lax.axis_size("dp"),
        lax.axis_size("context"),
        lax.axis_index("dp"),
        lax.axis_index("context"),
    )


def by_context(block_of):
    nc = lax.axis_size("context")
    return {s: shift(block_of(s), "context", s) for s in range(1, nc)}


def by_dp(block_of):
    ndp = lax.axis_size("dp")
    return {d: shift(block_of(d), "dp", d) for d in range(1, ndp)}


class Pieces:
    def __init__(self, found, half):
        ndp, nc, dp, ctx = plane_blocks()
        keys = sorted(found)
        self.parts = [found[key] for key in keys]
        self.arrays = [array for array, _ in self.parts]
        self.half, self.columns = half, self.arrays[0].shape[1]
        self.places = jnp.stack(
            [
                2 * (lax.rem(dp - d + ndp, ndp) * nc + lax.rem(ctx - s + nc, nc)) + h
                for d, s, h in keys
            ]
        ).astype(jnp.int32)


def gather_plain(own):
    half = own.shape[0] // 2
    across, along = by_context(lambda s: own), by_dp(lambda d: own)

    def far(after=None):
        tops = [x[:half] for x in across.values()]
        bottoms = [x[half:] for x in along.values()]
        if after is not None:
            (tops, bottoms), _ = tie((tops, bottoms), after)
        far_x = by_context(lambda s: jnp.concatenate(bottoms, 0))
        far_y = by_dp(lambda d: jnp.concatenate(tops, 0))
        found = {(0, 0, h): (own, h) for h in range(2)}
        for s, x in across.items():
            found.update({(0, s, h): (x, h) for h in range(2)})
        for d, x in along.items():
            found.update({(d, 0, h): (x, h) for h in range(2)})
            found.update({(d, s, 0): (far_y[d], s - 1) for s in across})
            found.update({(d, s, 1): (far_x[s], d - 1) for s in across})
        return found, (far_x, far_y)

    return across, along, far


class Scatter:
    def __init__(self, halves_of, half):
        self.halves_of, self.half = halves_of, half

    def make(self, first=True, last=True):
        ndp, nc, dp, ctx = plane_blocks()
        across, along = range(1, nc), range(1, ndp)

        def group(keys, dtype):
            return [
                2 * (lax.rem(dp + d, ndp) * nc + lax.rem(ctx + s, nc)) + h for d, s, h in keys
            ], dtype

        groups = []
        if first:
            groups += [group([*((d, s, 0) for d in along), (0, s, 0)], BF16) for s in across]
            groups += [group([*((d, s, 1) for s in across), (d, 0, 1)], BF16) for d in along]
        if last:
            groups += [group([(0, s, 1)], F32) for s in across]
            groups += [group([(d, 0, 0)], F32) for d in along]
            groups.append(group([(0, 0, 0), (0, 0, 1)], F32))
        made = list(self.halves_of(groups))
        if first:
            self.to_across = dict(zip(across, made))
            self.to_along = dict(zip(along, made[nc - 1 :]))
            made = made[nc - 1 + ndp - 1 :]
        if last:
            self.near_across = dict(zip(across, made))
            self.near_along = dict(zip(along, made[nc - 1 :]))
            self.own = made[-1]
        return made

    def send_first(self, after=()):
        (across, along), _ = tie((self.to_across, self.to_along), after)
        self.across = by_context(lambda s: across[s])
        self.along = by_dp(lambda d: along[d])
        return self.across, self.along

    def row(self, x, i):
        return x[i * self.half : (i + 1) * self.half].astype(F32)

    def sums(self):
        across = {
            s: (x + sum(self.row(y, s - 1) for y in self.along.values())).astype(BF16)
            for s, x in self.near_across.items()
        }
        along = {
            d: (x + sum(self.row(y, d - 1) for y in self.across.values())).astype(BF16)
            for d, x in self.near_along.items()
        }
        return across, along

    def finish(self, last):
        ndp, nc, _, _ = plane_blocks()
        across, along = last
        top, bottom = self.own[: self.half], self.own[self.half :]
        for x in self.across.values():
            top = top + self.row(x, ndp - 1)
        for x in along.values():
            top = top + x.astype(F32)
        for x in self.along.values():
            bottom = bottom + self.row(x, nc - 1)
        for x in across.values():
            bottom = bottom + x.astype(F32)
        return jnp.concatenate([top, bottom], 0)


def join_last(scatters):
    sums = [scatter.sums() for scatter in scatters]
    return (
        {s: jnp.concatenate([x[0][s] for x in sums], 0) for s in sums[0][0]},
        {d: jnp.concatenate([x[1][d] for x in sums], 0) for d in sums[0][1]},
    )


def send_last(scatters, blocks=None):
    to_across, to_along = join_last(scatters) if blocks is None else blocks
    across = by_context(lambda s: to_across[s])
    along = by_dp(lambda d: to_along[d])
    split, start = [], 0
    for scatter in scatters:
        rows = slice(start, start + scatter.half)
        split.append(
            ({s: x[rows] for s, x in across.items()}, {d: x[rows] for d, x in along.items()})
        )
        start += scatter.half
    return split


def doubling_steps(axis):
    n = lax.axis_size(axis)
    step = 1
    while step < n:
        yield step, [(i, i ^ step) for i in range(n)]
        step *= 2


def small_gather(x, axes):
    for axis in axes:
        place = lax.axis_index(axis)
        for step, pairs in doubling_steps(axis):
            other = lax.ppermute(x, axis, pairs)
            high = (place & step) != 0
            x = jnp.concatenate([jnp.where(high, other, x), jnp.where(high, x, other)], 0)
    return x


def small_scatter(x, axes):
    for axis in axes:
        place = lax.axis_index(axis)
        for step, pairs in reversed(list(doubling_steps(axis))):
            half = x.shape[0] // 2
            high = (place & step) != 0
            low_part, high_part = x[:half], x[half:]
            other = lax.ppermute(jnp.where(high, low_part, high_part), axis, pairs)
            x = jnp.where(high, high_part, low_part) + other
    return x


def core_exchange(x, group):
    count = lax.axis_size("expert")
    place = lax.rem(lax.axis_index("expert"), group)
    out = x
    for s in range(1, group):
        piece = lax.dynamic_slice_in_dim(x, lax.rem(place + s, group), 1)
        pairs = [(i, i // group * group + (i % group + s) % group) for i in range(count)]
        got = lax.ppermute(piece, "expert", pairs)
        out = lax.dynamic_update_slice_in_dim(out, got, lax.rem(place - s + group, group), 0)
    return out


LANES = 128
SCALE = 2
MIB = 1 << 20


def params(mib):
    return pltpu.CompilerParams(
        dimension_semantics=("arbitrary",), vmem_limit_bytes=mib * MIB
    )


def cost(flops, nbytes):
    return pl.CostEstimate(
        flops=flops // SCALE, bytes_accessed=nbytes // SCALE, transcendentals=0
    )


def assemble(places, full, refs, half):
    for i, ref in enumerate(refs):
        full[pl.ds(pl.multiple_of(places[i] * half, half), half), :] = ref[...]


def weight_grad_kernel(counts, half, numbers, *refs):
    n = sum(counts)
    acts, grads, outs, turned = refs[:n], refs[n], refs[n + 1 : -1], refs[-1]
    spots = [(out, i) for out, c in zip(outs, counts) for i in range(c)]

    @pl.when(pl.program_id(0) == 0)
    def _():
        for k in range(n):
            turned[k * half : (k + 1) * half, :] = acts[k][...].T

    step = min(n, max(1, 1024 // half))
    for first in range(0, n, step):
        some = spots[first : first + step]
        total = mat_dot(turned[first * half : (first + len(some)) * half, :], grads[...])
        for i, (out, at) in enumerate(some):
            out[at * half : (at + 1) * half, :] = total[i * half : (i + 1) * half].astype(
                out.dtype
            )


def weight_grad(acts, grads, groups, half):
    m, columns = grads.shape
    numbers = [number for some, _ in groups for number in some]
    counts = tuple(len(some) for some, _ in groups)
    tile = tile_of(m)

    def block(k):
        return pl.BlockSpec((m, half), lambda j, p: (0, p[k]))

    return pl.pallas_call(
        functools.partial(weight_grad_kernel, counts, half),
        out_shape=[
            jax.ShapeDtypeStruct((len(some) * half, columns), dtype) for some, dtype in groups
        ],
        grid_spec=pltpu.PrefetchScalarGridSpec(
            num_scalar_prefetch=1,
            grid=(pl.cdiv(columns, tile),),
            in_specs=[block(k) for k in range(len(numbers))]
            + [pl.BlockSpec((m, tile), lambda j, p: (0, j))],
            out_specs=[pl.BlockSpec((c * half, tile), lambda j, p: (0, j)) for c in counts],
            scratch_shapes=[pltpu.VMEM((len(numbers) * half, m), BF16)],
        ),
        compiler_params=params(52),
        cost_estimate=cost(2 * m * len(numbers) * half * columns, 12 * MIB),
        name="weight_grad",
    )(jnp.stack(numbers).astype(jnp.int32), *[acts] * len(numbers), grads)


def chunk(m):
    return min(m, 512)


def tile_of(m):
    return 768 if m <= 1024 else 256


def hidden_grad_kernel(half, places, acts, *refs):
    out, full = refs[-2], refs[-1]
    assemble(places, full, refs[:-2], half)
    step = chunk(acts.shape[0])

    @pl.loop(0, acts.shape[0] // step)
    def _(c):
        rows = pl.ds(pl.multiple_of(c * step, step), step)
        out[rows, :] = mat_dot(acts[rows, :], full[...])


def hidden_grad(acts, pieces):
    m, width = acts.shape
    tile_size = tile_of(m)
    tiles = pl.cdiv(pieces.columns, tile_size)
    return pl.pallas_call(
        functools.partial(hidden_grad_kernel, pieces.half),
        out_shape=jax.ShapeDtypeStruct((m, pieces.columns), F32),
        grid_spec=pltpu.PrefetchScalarGridSpec(
            num_scalar_prefetch=1,
            grid=(tiles,),
            in_specs=[pl.BlockSpec((m, width), lambda j, p: (0, 0))]
            + [
                pl.BlockSpec((pieces.half, tile_size), lambda j, p, r=r: (r, j))
                for _, r in pieces.parts
            ],
            out_specs=pl.BlockSpec((m, tile_size), lambda j, p: (0, j)),
            scratch_shapes=[pltpu.VMEM((width, tile_size), BF16)],
        ),
        compiler_params=params(44),
        cost_estimate=cost(2 * m * width * pieces.columns, 20 * MIB),
        name="hidden_grad",
    )(pieces.places, acts, *pieces.arrays)


def fold(x):
    total = x[:, :LANES]
    for i in range(1, x.shape[1] // LANES):
        total = total + x[:, i * LANES : (i + 1) * LANES]
    return total


def ffn_kernel(n, half, tile, fe, count, columns, *refs):
    places, here, acts, router, kept, gh = refs[:6]
    gates, ups, refs = refs[6 : 6 + n], refs[6 + n : 6 + 2 * n], refs[6 + 2 * n :]
    scaled, gate_out, up_out, small = refs[:4]
    prob, share, switch, sum_e, sum_s, gate_full, up_full = refs[4:]
    step = chunk(acts.shape[0])
    j = pl.program_id(0)
    chunks = acts.shape[0] // step
    lane = lax.broadcasted_iota(jnp.int32, (1, LANES), 1)

    def rows_of(c):
        return pl.ds(pl.multiple_of(c * step, step), step)

    @pl.when(j == 0)
    def _():
        @pl.loop(0, chunks)
        def _(c):
            rows = rows_of(c)
            logits = mat_dot(acts[rows, :], router[...])
            sig = jax.nn.sigmoid(logits)
            masked = jnp.where(lane < count, logits, NEGATIVE)
            expo = jnp.exp(masked - jnp.max(masked, -1, keepdims=True))
            expo = jnp.where(lane < count, expo, 0.0)
            probs = expo / jnp.sum(expo, -1, keepdims=True)
            prob[rows, :] = probs
            own = jnp.sum(jnp.where(lane == here[0], probs, 0.0), -1, keepdims=True)
            share[rows, :] = own * kept[rows, :]
            switch[rows, :] = jnp.sum(jnp.where(lane == count, sig, 0.0), -1, keepdims=True)
            sum_e[rows, :] = jnp.zeros((step, LANES), F32)
            sum_s[rows, :] = jnp.zeros((step, LANES), F32)

    column = j * tile + lax.broadcasted_iota(jnp.int32, (1, tile), 1)
    routed = column < fe
    shared = (column >= fe) & (column < columns)
    assemble(places, gate_full, gates, half)
    assemble(places, up_full, ups, half)

    @pl.loop(0, chunks)
    def _(c):
        rows = rows_of(c)
        gate = mat_dot(acts[rows, :], gate_full[...])
        up = mat_dot(acts[rows, :], up_full[...])
        scale = jnp.where(routed, share[rows, :], switch[rows, :])
        sig = jax.nn.sigmoid(gate)
        silu = gate * sig
        hidden = silu * up
        grad = gh[rows, :]
        product = grad * hidden
        sum_e[rows, :] += fold(jnp.where(routed, product, 0.0))
        sum_s[rows, :] += fold(jnp.where(shared, product, 0.0))
        grad = grad * scale
        scaled[rows, :] = (scale * hidden).astype(BF16)
        gate_out[rows, :] = (grad * up * (sig + silu * (1.0 - sig))).astype(BF16)
        up_out[rows, :] = (grad * silu).astype(BF16)

    @pl.when(j == pl.num_programs(0) - 1)
    def _():
        @pl.loop(0, chunks)
        def _(c):
            rows = rows_of(c)
            grad_share = jnp.sum(sum_e[rows, :], -1, keepdims=True)
            grad_switch = jnp.sum(sum_s[rows, :], -1, keepdims=True)
            hot = (lane == here[0]).astype(F32)
            logit = grad_share * share[rows, :] * (hot - prob[rows, :])
            sw = switch[rows, :]
            pre = grad_switch * sw * (1.0 - sw)
            value = jnp.where(lane < count, logit, jnp.where(lane == count, pre, 0.0))
            small[rows, :] = value.astype(BF16)


def ffn(acts, router, kept, gh, here, gates, ups, fe, count):
    m, width = acts.shape
    columns = gates.columns
    tile_size = tile_of(m)
    tiles = pl.cdiv(columns, tile_size)
    whole = lambda j, p, h: (0, 0)
    tile = pl.BlockSpec((m, tile_size), lambda j, p, h: (0, j))
    weights = [
        pl.BlockSpec((gates.half, tile_size), lambda j, p, h, r=r: (r, j))
        for _, r in gates.parts + ups.parts
    ]
    hid = jax.ShapeDtypeStruct((m, columns), BF16)
    return pl.pallas_call(
        functools.partial(
            ffn_kernel, len(gates.parts), gates.half, tile_size, fe, count, columns
        ),
        out_shape=(hid, hid, hid, jax.ShapeDtypeStruct((m, LANES), BF16)),
        grid_spec=pltpu.PrefetchScalarGridSpec(
            num_scalar_prefetch=2,
            grid=(tiles,),
            in_specs=[
                pl.BlockSpec((m, width), whole),
                pl.BlockSpec((width, LANES), whole),
                pl.BlockSpec((m, 1), whole),
                tile,
            ]
            + weights,
            out_specs=[tile, tile, tile, pl.BlockSpec((m, LANES), whole)],
            scratch_shapes=[
                pltpu.VMEM((m, LANES), F32),
                pltpu.VMEM((m, 1), F32),
                pltpu.VMEM((m, 1), F32),
                pltpu.VMEM((m, LANES), F32),
                pltpu.VMEM((m, LANES), F32),
                pltpu.VMEM((width, tile_size), BF16),
                pltpu.VMEM((width, tile_size), BF16),
            ],
        ),
        compiler_params=params(52),
        cost_estimate=cost(4 * m * width * columns, 40 * MIB),
        name="ffn",
    )(gates.places, here, acts, router, kept, gh, *gates.arrays, *ups.arrays)


def spread_kernel(n, pairs, extra, places, *refs):
    i = pl.program_id(0)
    acts, refs = refs[:pairs], refs[pairs:]
    weights, refs = [refs[k * n : (k + 1) * n] for k in range(pairs)], refs[pairs * n :]
    out, held = refs[-1 - pairs], refs[-pairs:]
    step = min(out.shape[0], 1024)
    for k in range(n):

        @pl.when(i == k)
        def _(k=k):
            for pair in range(pairs):
                held[pair][...] = weights[pair][k][...]

    @pl.loop(0, out.shape[0] // step)
    def _(c):
        rows = pl.ds(pl.multiple_of(c * step, step), step)
        total = right_dot(acts[0][rows, :], held[0][...])
        for pair in range(1, pairs):
            total += right_dot(acts[pair][rows, :], held[pair][...])
        if extra:
            total += right_dot(refs[0][rows, :], refs[1][...])
        out[rows, :] = total.astype(BF16)


def spread(pairs, extra=None, weight=1):
    acts = [a for a, _ in pairs]
    first = pairs[0][1]
    half, steps = first.half, len(first.parts)
    m = acts[0].shape[0]
    width = steps * half
    whole = lambda i, p: (0, 0)
    specs = [pl.BlockSpec(a.shape, whole) for a in acts]
    operands = list(acts)
    for _, pieces in pairs:
        specs += [
            pl.BlockSpec((half, pieces.columns), lambda i, p, r=r: (r, 0))
            for _, r in pieces.parts
        ]
        operands += pieces.arrays
    if extra is not None:
        specs.append(pl.BlockSpec(extra[0].shape, whole))
        specs.append(pl.BlockSpec((half, LANES), lambda i, p: (p[i], 0)))
        operands += list(extra)
    return pl.pallas_call(
        functools.partial(spread_kernel, steps, len(pairs), extra is not None),
        out_shape=jax.ShapeDtypeStruct((m, width), BF16),
        grid_spec=pltpu.PrefetchScalarGridSpec(
            num_scalar_prefetch=1,
            grid=(steps,),
            in_specs=specs,
            out_specs=pl.BlockSpec((m, half), lambda i, p: (0, p[i])),
            scratch_shapes=[pltpu.VMEM((half, first.columns), BF16)] * len(pairs),
        ),
        compiler_params=params(60),
        cost_estimate=cost(2 * weight * m * width * first.columns * len(pairs), 20 * MIB),
        name="spread",
    )(first.places, *operands)


def turn(x):
    return pltpu.roll(x, HD // 2, 1)


def qkv_kernel(half, wide, places, tok, gain, bias, cosine, sine, *refs):
    normed, query, key_value, full = refs[-4:]

    @pl.when(pl.program_id(0) == 0)
    def _():
        assemble(places, full, refs[:-4], half)

    values = tok[...].astype(F32)
    inv = lax.rsqrt(jnp.mean(values * values, -1, keepdims=True) + EPSILON)
    normed[...] = (values * inv * gain[...]).astype(BF16)
    out = mat_dot(normed[...], full[...]) + bias[...]
    for h in range(2 * wide // HD):
        head = out[:, h * HD : (h + 1) * HD]
        head = (head * cosine[...] + turn(head) * sine[...]).astype(BF16)
        if h < wide // HD:
            query[:, h * HD : (h + 1) * HD] = head
        else:
            key_value[:, h * HD - wide : (h + 1) * HD - wide] = head
    key_value[:, wide:] = out[:, 2 * wide :].astype(BF16)


def qkv_project(tok, gain, bias, cosine, sine, pieces, wide):
    m, width = tok.shape
    step = 256
    row = lambda i, p: (i, 0)
    whole = lambda i, p: (0, 0)
    return pl.pallas_call(
        functools.partial(qkv_kernel, pieces.half, wide),
        out_shape=(
            jax.ShapeDtypeStruct((m, width), BF16),
            jax.ShapeDtypeStruct((m, wide), BF16),
            jax.ShapeDtypeStruct((m, 2 * wide), BF16),
        ),
        grid_spec=pltpu.PrefetchScalarGridSpec(
            num_scalar_prefetch=1,
            grid=(m // step,),
            in_specs=[
                pl.BlockSpec((step, width), row),
                pl.BlockSpec((1, width), whole),
                pl.BlockSpec((1, 3 * wide), whole),
                pl.BlockSpec((step, HD), row),
                pl.BlockSpec((step, HD), row),
            ]
            + [
                pl.BlockSpec((pieces.half, 3 * wide), lambda i, p, r=r: (r, 0))
                for _, r in pieces.parts
            ],
            out_specs=[
                pl.BlockSpec((step, width), row),
                pl.BlockSpec((step, wide), row),
                pl.BlockSpec((step, 2 * wide), row),
            ],
            scratch_shapes=[pltpu.VMEM((width, 3 * wide), BF16)],
        ),
        compiler_params=params(32),
        cost_estimate=cost(6 * m * width * wide, 12 * MIB),
        name="qkv_project",
    )(pieces.places, tok, gain, bias, cosine, sine, *pieces.arrays)


def head_probs(query, kvs, allowed, h):
    own = slice(h * HD, (h + 1) * HD)
    scores = jnp.concatenate([right_dot(query[:, own], kv[:, own]) for kv in kvs], -1)
    scores = jnp.where(allowed, scores * HD ** (-0.5), NEGATIVE)
    expo = jnp.exp(scores - jnp.max(scores, -1, keepdims=True))
    return expo / jnp.sum(expo, -1, keepdims=True)


def attend_kernel(nc, wide, query, allowed, w_o, *refs):
    kvs, mixed, out = refs[:nc], refs[nc], refs[nc + 1]
    tok = query.shape[0]
    for h in range(wide // HD):
        value = slice(wide + h * HD, wide + (h + 1) * HD)
        prob = head_probs(query, kvs, allowed[0] > 0.0, h).astype(BF16)
        total = mat_dot(prob[:, :tok], kvs[0][:, value])
        for s in range(1, nc):
            total += mat_dot(prob[:, s * tok : (s + 1) * tok], kvs[s][:, value])
        mixed[:, h * HD : (h + 1) * HD] = total.astype(BF16)
    out[...] = mat_dot(mixed[...], w_o[...]).astype(BF16)


def attend(query, kvs, allowed, w_o):
    m, wide = query.shape
    groups, tok, keys = allowed.shape
    width = w_o.shape[1]
    row = lambda g: (g, 0)
    return pl.pallas_call(
        functools.partial(attend_kernel, len(kvs), wide),
        out_shape=(
            jax.ShapeDtypeStruct((m, wide), BF16),
            jax.ShapeDtypeStruct((m, width), BF16),
        ),
        grid=(groups,),
        in_specs=[
            pl.BlockSpec((tok, wide), row),
            pl.BlockSpec((1, tok, keys), lambda g: (g, 0, 0)),
            pl.BlockSpec((wide, width), lambda g: (0, 0)),
        ]
        + [pl.BlockSpec((tok, 2 * wide), row)] * len(kvs),
        out_specs=[pl.BlockSpec((tok, wide), row), pl.BlockSpec((tok, width), row)],
        compiler_params=params(32),
        cost_estimate=cost(2 * m * width * wide + 4 * m * keys * wide, 8 * MIB),
        name="attend",
    )(query, allowed, w_o, *kvs)


def attend_back_kernel(nc, wide, query, allowed, w_o, grads, cosine, sine, *refs):
    kvs, grad_query, grad_own, grad_far = refs[:nc], refs[nc], refs[nc + 1], refs[nc + 2 :]
    tok = query.shape[0]
    grad_mixed = right_dot(grads[...], w_o[...]).astype(BF16)
    scale = HD ** (-0.5)
    for h in range(wide // HD):
        key = slice(h * HD, (h + 1) * HD)
        value = slice(wide + h * HD, wide + (h + 1) * HD)
        prob = head_probs(query, kvs, allowed[0] > 0.0, h)
        low = prob.astype(BF16)
        mixed = grad_mixed[:, key]
        grad = jnp.concatenate([right_dot(mixed, kv[:, value]) for kv in kvs], -1)
        inner = jnp.sum(grad * prob, -1, keepdims=True)
        grad = (prob * (grad - inner)).astype(BF16)
        total = None
        for s in range(nc):
            block = slice(s * tok, (s + 1) * tok)
            term = mat_dot(grad[:, block], kvs[s][:, key])
            total = term if total is None else total + term
            grad_key = left_dot(grad[:, block], query[:, key]) * scale
            grad_value = left_dot(low[:, block], mixed)
            if s == 0:
                grad_own[:, key] = grad_key
                grad_own[:, value] = grad_value
            else:
                grad_far[s - 1][:, key] = grad_key.astype(BF16)
                grad_far[s - 1][:, value] = grad_value.astype(BF16)
        total = total * scale
        total = total * cosine[...] - turn(total) * sine[...]
        grad_query[:, key] = total.astype(BF16)


def attend_back(query, kvs, allowed, w_o, grads, cosine, sine):
    m, wide = query.shape
    groups, tok, keys = allowed.shape
    width = w_o.shape[1]
    nc = len(kvs)
    row = lambda g: (g, 0)
    both = pl.BlockSpec((tok, 2 * wide), row)
    return pl.pallas_call(
        functools.partial(attend_back_kernel, nc, wide),
        out_shape=(
            jax.ShapeDtypeStruct((m, wide), BF16),
            jax.ShapeDtypeStruct((m, 2 * wide), F32),
            *[jax.ShapeDtypeStruct((m, 2 * wide), BF16)] * (nc - 1),
        ),
        grid=(groups,),
        in_specs=[
            pl.BlockSpec((tok, wide), row),
            pl.BlockSpec((1, tok, keys), lambda g: (g, 0, 0)),
            pl.BlockSpec((wide, width), lambda g: (0, 0)),
            pl.BlockSpec((tok, width), row),
            pl.BlockSpec((tok, HD), row),
            pl.BlockSpec((tok, HD), row),
        ]
        + [both] * nc,
        out_specs=[pl.BlockSpec((tok, wide), row)] + [both] * nc,
        compiler_params=params(32),
        cost_estimate=cost(2 * m * width * wide + 12 * m * keys * wide, 8 * MIB),
        name="attend_back",
    )(query, allowed, w_o, grads, cosine, sine, *kvs)


def join_kernel(wide, grad_query, grad_own, cosine, sine, *refs):
    far, out, sums = refs[:-2], refs[-2], refs[-1]
    total = grad_own[...]
    for ref in far:
        total = total + ref[...].astype(F32)
    out[:, :wide] = grad_query[...]
    for h in range(wide // HD):
        head = total[:, h * HD : (h + 1) * HD]
        head = head * cosine[...] - turn(head) * sine[...]
        out[:, wide + h * HD : wide + (h + 1) * HD] = head.astype(BF16)
    out[:, 2 * wide :] = total[:, wide:].astype(BF16)

    @pl.when(pl.program_id(0) == 0)
    def _():
        sums[...] = jnp.zeros_like(sums)

    sums[...] += jnp.sum(out[...].astype(F32), 0, keepdims=True)


def join(grad_query, grad_own, far, cosine, sine):
    m, wide = grad_query.shape
    step = 256
    row = lambda i: (i, 0)
    both = pl.BlockSpec((step, 2 * wide), row)
    return pl.pallas_call(
        functools.partial(join_kernel, wide),
        out_shape=(
            jax.ShapeDtypeStruct((m, 3 * wide), BF16),
            jax.ShapeDtypeStruct((1, 3 * wide), F32),
        ),
        grid=(m // step,),
        in_specs=[
            pl.BlockSpec((step, wide), row),
            both,
            pl.BlockSpec((step, HD), row),
            pl.BlockSpec((step, HD), row),
        ]
        + [both] * len(far),
        out_specs=[
            pl.BlockSpec((step, 3 * wide), row),
            pl.BlockSpec((1, 3 * wide), lambda i: (0, 0)),
        ],
        compiler_params=params(32),
        cost_estimate=cost(20 * m * wide, 6 * MIB),
        name="join",
    )(grad_query, grad_own, cosine, sine, *far)


def rms_unit(values):
    scaling = lax.rsqrt(jnp.mean(values * values, -1, keepdims=True) + EPSILON)
    return values * scaling, scaling


def body(
    tokens,
    cotangent,
    deal_order,
    seq_lengths,
    expert_ids,
    w_query,
    w_key,
    w_value,
    w_out,
    bias_query,
    bias_key,
    bias_value,
    norm_attn,
    norm_ffn,
    w_router,
    shared_gate,
    shared_up,
    shared_down,
    shared_switch,
    expert_gate,
    expert_up,
    expert_down,
):
    ndp, nc, dp, ctx = plane_blocks()
    planes = ndp * nc
    count = lax.axis_size("expert")
    here = lax.axis_index("expert")
    tok_count, width = tokens.shape[1], tokens.shape[2]
    group_tok = deal_order.shape[1]
    seqs = seq_lengths.shape[1]
    top = expert_ids.shape[2]
    rows_flat = w_query.shape[0]
    part = HD // rows_flat
    heads = planes // part
    runs = count // part
    run, member = here // part, lax.rem(here, part)
    fe_width = expert_gate.shape[2]
    fs_width = shared_gate.shape[1]
    pad = -(fe_width + fs_width) % LANES
    capacity = min(tok_count, 5 * tok_count * top // (4 * count))
    wide = heads * HD
    all_rows = count * tok_count
    block = width // planes

    token_rows = tokens[0]

    def by_head(w):
        w = w.reshape(rows_flat, part, heads, runs, HD).transpose(3, 1, 0, 2, 4)
        return w.reshape(count, rows_flat, wide)

    qkv_out = jnp.concatenate([by_head(w) for w in (w_query, w_key, w_value)], -1)
    all_tokens = lax.all_gather(token_rows, "expert", axis=0, tiled=True)
    qkv_rows = lax.all_to_all(qkv_out, "expert", split_axis=0, concat_axis=0, tiled=True)
    small = jnp.concatenate(
        [
            v.astype(F32).reshape(-1)
            for v in (
                bias_query,
                bias_key,
                bias_value,
                norm_attn,
                norm_ffn,
                shared_switch,
                w_router,
                deal_order,
                seq_lengths,
                expert_ids,
            )
        ]
    )

    weights, _ = tie((expert_up, shared_up, expert_down, shared_down), qkv_out)
    expert_up, shared_up, expert_down, shared_down = weights

    def stacked(routed, shared):
        none = jnp.zeros((routed.shape[0], pad), BF16)
        return jnp.concatenate([routed, shared, none], 1)

    def turned(routed, shared, h):
        columns = slice(h * block // 2, (h + 1) * block // 2)
        return stacked(routed[:, columns].T, shared[:, columns].T)

    def rows_half(x, h):
        return x[h * block // 2 : (h + 1) * block // 2]

    hb = block // 2
    gate_own = stacked(expert_gate[0], shared_gate)
    d_top, d_low = [turned(expert_down[0], shared_down, h) for h in range(2)]
    u_top, u_low = [stacked(rows_half(expert_up[0], h), rows_half(shared_up, h)) for h in range(2)]
    pair_own = jnp.concatenate([d_top, d_low, u_top, u_low], 0)
    wo_across, wo_along, wo_far = gather_plain(w_out)
    gate_across, gate_along, gate_far = gather_plain(gate_own)
    small, pair_own = tie(small, pair_own)
    small_plane = small_gather(small[None], ("context", "dp"))
    qkv_own = qkv_rows.reshape(count * rows_flat, 3 * wide)
    qkv_own, _ = tie(qkv_own, (gate_across, gate_along, pair_own))
    small_plane, _ = tie(small_plane, qkv_own)
    all_grads = lax.all_gather(
        tie(cotangent[0], qkv_own)[0], "expert", axis=0, tiled=True
    )
    _, _, qkv_far = gather_plain(qkv_own)
    small_all = small_gather(small_plane.reshape(1, -1), ("expert",))
    small_all = small_all.reshape(count, ndp * nc, -1).transpose(1, 0, 2)
    small_all = small_all.reshape(ndp * nc * count, -1)
    qkv_found, qkv_sent = qkv_far()
    qkv_pieces = Pieces(qkv_found, qkv_own.shape[0] // 2)
    wo_found, _ = wo_far(qkv_sent)
    gate_found, gate_sent = gate_far(qkv_sent)
    gate_pieces = Pieces(gate_found, hb)
    columns = {}
    place = 0
    for name in ("bq", "bk", "bv", "na", "nf", "sw"):
        columns[name] = small_all[:, place : place + rows_flat].reshape(-1)
        place += rows_flat
    router = small_all[:, place : place + rows_flat * count].reshape(-1, count).astype(BF16)
    place += rows_flat * count
    plane_small = lax.dynamic_index_in_dim(
        small_all.reshape(ndp, nc, count, -1), dp, 0, keepdims=False
    )
    order = plane_small[0, :, place : place + group_tok].astype(jnp.int32)
    place += group_tok
    lengths = plane_small[0, :, place : place + seqs].astype(jnp.int32)
    place += seqs
    ids = plane_small[..., place:].reshape(nc, count, tok_count, top).astype(jnp.int32)
    gain_attn, gain_ffn = columns["na"], columns["nf"]
    router_switch = jnp.concatenate(
        [
            router,
            columns["sw"].astype(BF16)[:, None],
            jnp.zeros((width, LANES - count - 1), BF16),
        ],
        1,
    )

    local_index = ctx * tok_count + jnp.arange(tok_count, dtype=jnp.int32)
    ends = jnp.cumsum(lengths, 1)
    starts = ends - lengths

    def segments(index):
        segment = jnp.sum((index[None, :, None] >= ends[:, None, :]).astype(jnp.int32), -1)
        hot = segment[..., None] == jnp.arange(seqs, dtype=jnp.int32)
        return segment, index[None, :] - jnp.sum(jnp.where(hot, starts[:, None, :], 0), -1)

    query_segment, position = segments(local_index)
    allowed = []
    for s in range(nc):
        key_index = local_index - s * tok_count
        key_segment, _ = segments(key_index)
        allowed.append(
            (query_segment[:, :, None] == key_segment[:, None, :])
            & (key_index[None, None, :] <= local_index[None, :, None])
            & (key_index >= 0)[None, None, :]
        )
    allowed = jnp.concatenate(allowed, -1).astype(F32)
    frequency = ROPE_BASE ** (-2.0 * jnp.arange(HD // 2, dtype=F32) / HD)
    angles = position.reshape(-1).astype(F32)[:, None] * frequency[None, :]
    cosine = jnp.concatenate([jnp.cos(angles)] * 2, -1)
    sine = jnp.sin(angles)
    sine_table = jnp.concatenate([-sine, sine], -1)

    def own_heads(row):
        row = row.reshape(part, heads, runs, HD)
        row = lax.dynamic_index_in_dim(row, member, 0, keepdims=False)
        return lax.dynamic_index_in_dim(row, run, 1, keepdims=False).reshape(-1)

    bias = jnp.concatenate([own_heads(columns[k]) for k in ("bq", "bk", "bv")])
    normed, queries, key_value = qkv_project(
        all_tokens, gain_attn[None], bias[None], cosine, sine_table, qkv_pieces, wide
    )
    kvs = [key_value] + [
        lax.ppermute(key_value, "context", [(i, i + s) for i in range(nc - s)])
        for s in range(1, nc)
    ]
    wo_arrays, _ = tie({k: array for k, (array, _) in wo_found.items()}, key_value)
    wo_found = {k: (wo_arrays[k], row) for k, (_, row) in wo_found.items()}
    wo_pieces = Pieces(wo_found, rows_flat // 2)
    wo_planes = jnp.zeros((2 * planes, rows_flat // 2, width), BF16)
    for (array, row), number in zip(wo_pieces.parts, list(wo_pieces.places)):
        array = array[row * rows_flat // 2 : (row + 1) * rows_flat // 2]
        wo_planes = lax.dynamic_update_slice_in_dim(wo_planes, array[None], number, 0)
    wo_mine = core_exchange(wo_planes.reshape(part, heads, rows_flat, width), part)
    w_o = wo_mine.transpose(1, 0, 2, 3).reshape(wide, width)

    kvs, (pair_own, _) = tie(kvs, (pair_own, (gate_sent, all_grads)))
    x_one, y_one = by_context(lambda s: pair_own), by_dp(lambda d: pair_own)
    mixed, attn_part = attend(queries, kvs, allowed, w_o)
    attn_out = lax.psum_scatter(attn_part, "expert", scatter_dimension=0, tiled=True)
    attn_out, _ = tie(attn_out, (x_one, y_one))
    x_two = by_context(
        lambda s: jnp.concatenate([y[hb : 2 * hb] for y in y_one.values()], 0)
    )
    y_two = by_dp(lambda d: jnp.concatenate([x[:hb] for x in x_one.values()], 0))
    residual = token_rows.astype(F32) + attn_out.astype(F32)
    unit_two, scale_two = rms_unit(residual)
    rows = lax.all_gather(
        (unit_two * gain_ffn).astype(BF16), "expert", axis=0, tiled=True
    )
    rows, _ = tie(rows, (x_two, y_two))
    x_far = [y[3 * hb :] for y in y_one.values()]
    y_far = [x[2 * hb : 3 * hb] for x in x_one.values()]
    x_three = by_context(lambda s: jnp.concatenate(x_far, 0))
    y_three = by_dp(lambda d: jnp.concatenate(y_far, 0))
    down_found = {(0, 0, h): (pair_own, h) for h in range(2)}
    up_found = {(0, 0, h): (pair_own, 2 + h) for h in range(2)}
    for s, x in x_one.items():
        down_found.update({(0, s, h): (x, h) for h in range(2)})
        up_found.update({(0, s, h): (x, 2 + h) for h in range(2)})
    for d, y in y_one.items():
        down_found.update({(d, 0, h): (y, h) for h in range(2)})
        up_found.update({(d, 0, h): (y, 2 + h) for h in range(2)})
        for s in x_one:
            down_found.update({(d, s, 0): (y_two[d], s - 1), (d, s, 1): (x_two[s], d - 1)})
            up_found.update({(d, s, 0): (y_three[d], s - 1), (d, s, 1): (x_three[s], d - 1)})
    down_pieces, up_pieces = Pieces(down_found, hb), Pieces(up_found, hb)

    (ids, order), _ = tie((ids, order), key_value)
    hit = jnp.any(ids == here, -1)
    below = jnp.arange(tok_count)[:, None] < jnp.arange(tok_count)[None, :]
    slot = mat_dot(hit.reshape(nc * count, tok_count).astype(BF16), below.astype(BF16))
    kept = (hit & (slot.reshape(nc, count, tok_count) < capacity)).astype(F32)
    kept = kept.transpose(1, 0, 2).reshape(count, group_tok)
    kept_rows = jnp.sum(
        jnp.where(order[:, None, :] == local_index[None, :, None], kept[:, None, :], 0.0), -1
    ).reshape(all_rows)

    gh = hidden_grad(all_grads, down_pieces)
    scaled, grad_gate, grad_up, grad_small = ffn(
        rows,
        router_switch,
        kept_rows[:, None],
        gh,
        here.astype(jnp.int32)[None],
        gate_pieces,
        up_pieces,
        fe_width,
        count,
    )
    def scatter_of(acts, grads):
        return Scatter(lambda groups: weight_grad(acts, grads, groups, hb), hb)

    down_sum = scatter_of(all_grads, scaled)
    gate_sum = scatter_of(rows, grad_gate)
    down_sum.make(last=False)
    down_sent = down_sum.send_first()
    grad_rows = spread([(grad_gate, gate_pieces), (grad_up, up_pieces)], (grad_small, router_switch))
    grad_rows, _ = tie(grad_rows, down_sent)
    grad_normed_two = lax.psum_scatter(
        grad_rows, "expert", scatter_dimension=0, tiled=True
    ).astype(F32)
    gate_sum.make(last=False)
    gate_sent = gate_sum.send_first()
    terms = [down_sum.make(first=False), gate_sum.make(first=False)]
    up_sum = scatter_of(rows, grad_up)
    terms.append(up_sum.make())
    grad_normed_two, _ = tie(grad_normed_two, (gate_sent, terms))
    up_sent = up_sum.send_first()
    grad_router_switch = left_dot(rows, grad_small)

    grad_unit = grad_normed_two * gain_ffn
    grad_residual = cotangent[0].astype(F32) + scale_two * (
        grad_unit - unit_two * jnp.mean(grad_unit * unit_two, -1, keepdims=True)
    )
    grad_gain_ffn = jnp.sum(grad_normed_two * unit_two, 0)
    attn_own = grad_residual.astype(BF16)
    grad_attn = lax.all_gather(attn_own, "expert", axis=0, tiled=True)
    grad_attn, _ = tie(grad_attn, up_sent)
    grad_query, grad_own, *grad_far = attend_back(
        queries, kvs, allowed, w_o, grad_attn, cosine, sine_table
    )
    (mixed, scaled), _ = tie((mixed, scaled), grad_query)
    out_part = spread([(scaled, down_pieces)], weight=4)
    three = [down_sum, gate_sum, up_sum]
    blocks = join_last(three)
    grad_own, _ = tie(grad_own, (out_part, blocks))
    output = lax.psum_scatter(out_part, "expert", scatter_dimension=0, tiled=True)
    grad_wo = left_dot(mixed, grad_attn).astype(BF16).reshape(heads, part, rows_flat, width)
    wo_back = core_exchange(grad_wo.transpose(1, 0, 2, 3), part)
    wo_back = wo_back.reshape(2 * planes, rows_flat // 2, width)
    grad_far = [
        lax.ppermute(piece, "context", [(i + s, i) for i in range(nc - s)])
        for s, piece in enumerate(grad_far, 1)
    ]
    grad_qkv, bias_sums = join(grad_query, grad_own, grad_far, cosine, sine_table)
    grad_qkv, wo_back = tie(grad_qkv, wo_back)
    out_tokens = (residual + output.astype(F32)).astype(BF16)
    def to_heads(row):
        full = jnp.zeros((part, heads, runs, HD), F32)
        full = lax.dynamic_update_slice(
            full, row.reshape(1, heads, 1, HD), (member, 0, run, 0)
        )
        return full.reshape(planes * count, rows_flat)

    bias_sums = bias_sums[0]
    small_grads = jnp.concatenate(
        [to_heads(bias_sums[i * wide : (i + 1) * wide]) for i in range(3)]
        + [
            grad_gain_ffn.reshape(-1, rows_flat),
            grad_router_switch[:, count].reshape(-1, rows_flat),
            grad_router_switch[:, :count].reshape(planes * count, rows_flat * count),
        ],
        1,
    )

    wo_sum = Scatter(
        lambda groups: [
            jnp.concatenate(
                [lax.dynamic_index_in_dim(wo_back, i, 0, keepdims=False) for i in some], 0
            ).astype(dtype)
            for some, dtype in groups
        ],
        rows_flat // 2,
    )
    wo_sum.make()
    qkv_sum = scatter_of(normed, grad_qkv)
    lasts = send_last(three, tie(blocks, grad_far)[0])
    down_last, gate_last, up_last = lasts
    qkv_sum.make()
    qkv_sent = qkv_sum.send_first()
    wo_sum.send_first(qkv_sent)
    small_sum = small_scatter(tie(small_grads, qkv_sent)[0], ("dp", "context"))
    (wo_last,) = send_last([wo_sum])
    (qkv_last,) = send_last([qkv_sum], tie(join_last([qkv_sum]), lasts)[0])
    grad_normed = spread([(grad_qkv, qkv_pieces)])
    grad_normed_own = lax.psum_scatter(
        grad_normed, "expert", scatter_dimension=0, tiled=True
    ).astype(F32)
    grad_normed_own, _ = tie(grad_normed_own, (qkv_last, up_last))

    qkv_grad_rows = qkv_sum.finish(qkv_last)
    grad_gate_w = gate_sum.finish(gate_last)
    grad_down_w = down_sum.finish(down_last)
    grad_w_out = wo_sum.finish(wo_last)
    grad_up_w = up_sum.finish(up_last)
    qkv_back = lax.all_to_all(
        qkv_grad_rows.astype(BF16).reshape(count, rows_flat, 3 * wide),
        "expert",
        split_axis=0,
        concat_axis=0,
        tiled=True,
    )

    def from_heads(i):
        w = qkv_back[..., i * wide : (i + 1) * wide].astype(F32)
        w = w.reshape(runs, part, rows_flat, heads, HD).transpose(2, 1, 3, 0, 4)
        return w.reshape(rows_flat, width)

    small_sum, _ = tie(small_sum, (qkv_last, up_last))
    small_sum = small_scatter(small_sum, ("expert",))[0]
    pieces = [small_sum[i * rows_flat : (i + 1) * rows_flat] for i in range(5)]
    grad_router = small_sum[5 * rows_flat :].reshape(rows_flat, count)

    w_grads = [from_heads(i) for i in range(3)]
    grad_gain_attn = sum(
        jnp.sum(w.astype(F32) * grad, 1)
        for w, grad in zip((w_query, w_key, w_value), w_grads)
    ) / norm_attn.astype(F32)

    unit_one, scale_one = rms_unit(token_rows.astype(F32))
    grad_unit = grad_normed_own * gain_attn
    grad_tokens = grad_residual + scale_one * (
        grad_unit - unit_one * jnp.mean(grad_unit * unit_one, -1, keepdims=True)
    )
    return (
        out_tokens[None],
        grad_tokens.astype(BF16)[None],
        *w_grads,
        grad_w_out,
        pieces[0],
        pieces[1],
        pieces[2],
        grad_gain_attn,
        pieces[3],
        grad_router,
        grad_gate_w[:, fe_width : fe_width + fs_width],
        grad_up_w[:, fe_width : fe_width + fs_width],
        grad_down_w[:, fe_width : fe_width + fs_width].T,
        pieces[4],
        grad_gate_w[None, :, :fe_width],
        grad_up_w[None, :, :fe_width],
        grad_down_w[:, :fe_width].T[None],
    )


def solution(mesh):
    every = ("dp", "context", "expert")
    plane = ("dp", "context")
    rows = P(("dp", "expert"), "context", None)
    groups = P(("dp", "expert"), None)
    return jax.shard_map(
        body,
        mesh=mesh,
        in_specs=(
            rows,
            rows,
            groups,
            groups,
            rows,
            *[P(every, None)] * 4,
            *[P(every)] * 5,
            P(every, None),
            P(plane, "expert"),
            P(plane, "expert"),
            P("expert", plane),
            P(every),
            P("expert", plane, None),
            P("expert", plane, None),
            P("expert", None, plane),
        ),
        out_specs=(
            rows,
            rows,
            *[P(every, None)] * 4,
            *[P(every)] * 5,
            P(every, None),
            P(plane, "expert"),
            P(plane, "expert"),
            P("expert", plane),
            P(every),
            P("expert", plane, None),
            P("expert", plane, None),
            P("expert", None, plane),
        ),
        check_vma=False,
    )
```

```python
import functools

import jax
import jax.numpy as jnp
from jax import lax
from jax.experimental import pallas as pl
from jax.experimental.pallas import tpu as pltpu
from jax.sharding import PartitionSpec as P

HD = 128

EPSILON = 1e-06
ROPE_BASE = 1000000.0
NEGATIVE = -1e30
F32 = jnp.float32
BF16 = jnp.bfloat16


def mat_dot(left_mat, right_mat):
    return jnp.dot(left_mat, right_mat, preferred_element_type=F32)


def left_dot(left_mat, right_mat):
    return lax.dot_general(
        left_mat, right_mat, (((0,), (0,)), ((), ())), preferred_element_type=F32
    )


def right_dot(left_mat, right_mat):
    return lax.dot_general(
        left_mat, right_mat, (((1,), (1,)), ((), ())), preferred_element_type=F32
    )


def shift(x, axis, step):
    n = lax.axis_size(axis)
    return lax.ppermute(x, axis, [(i, (i + step) % n) for i in range(n)])


def tie(value, others):
    return lax.optimization_barrier((value, others))


def plane_blocks():
    return (
        lax.axis_size("dp"),
        lax.axis_size("context"),
        lax.axis_index("dp"),
        lax.axis_index("context"),
    )


def by_context(block_of):
    nc = lax.axis_size("context")
    return {s: shift(block_of(s), "context", s) for s in range(1, nc)}


def by_dp(block_of):
    ndp = lax.axis_size("dp")
    return {d: shift(block_of(d), "dp", d) for d in range(1, ndp)}


class Pieces:
    def __init__(self, found, half):
        ndp, nc, dp, ctx = plane_blocks()
        keys = sorted(found)
        self.parts = [found[key] for key in keys]
        self.arrays = [array for array, _ in self.parts]
        self.half, self.columns = half, self.arrays[0].shape[1]
        self.places = jnp.stack(
            [
                2 * (lax.rem(dp - d + ndp, ndp) * nc + lax.rem(ctx - s + nc, nc)) + h
                for d, s, h in keys
            ]
        ).astype(jnp.int32)


def gather_plain(own):
    half = own.shape[0] // 2
    across, along = by_context(lambda s: own), by_dp(lambda d: own)

    def far(after=None):
        tops = [x[:half] for x in across.values()]
        bottoms = [x[half:] for x in along.values()]
        if after is not None:
            (tops, bottoms), _ = tie((tops, bottoms), after)
        far_x = by_context(lambda s: jnp.concatenate(bottoms, 0))
        far_y = by_dp(lambda d: jnp.concatenate(tops, 0))
        found = {(0, 0, h): (own, h) for h in range(2)}
        for s, x in across.items():
            found.update({(0, s, h): (x, h) for h in range(2)})
        for d, x in along.items():
            found.update({(d, 0, h): (x, h) for h in range(2)})
            found.update({(d, s, 0): (far_y[d], s - 1) for s in across})
            found.update({(d, s, 1): (far_x[s], d - 1) for s in across})
        return found, (far_x, far_y)

    return across, along, far


class Scatter:
    def __init__(self, halves_of, half):
        self.halves_of, self.half = halves_of, half

    def make(self, first=True, last=True):
        ndp, nc, dp, ctx = plane_blocks()
        across, along = range(1, nc), range(1, ndp)

        def group(keys, dtype):
            return [
                2 * (lax.rem(dp + d, ndp) * nc + lax.rem(ctx + s, nc)) + h for d, s, h in keys
            ], dtype

        groups = []
        if first:
            groups += [group([*((d, s, 0) for d in along), (0, s, 0)], BF16) for s in across]
            groups += [group([*((d, s, 1) for s in across), (d, 0, 1)], BF16) for d in along]
        if last:
            groups += [group([(0, s, 1)], F32) for s in across]
            groups += [group([(d, 0, 0)], F32) for d in along]
            groups.append(group([(0, 0, 0), (0, 0, 1)], F32))
        made = list(self.halves_of(groups))
        if first:
            self.to_across = dict(zip(across, made))
            self.to_along = dict(zip(along, made[nc - 1 :]))
            made = made[nc - 1 + ndp - 1 :]
        if last:
            self.near_across = dict(zip(across, made))
            self.near_along = dict(zip(along, made[nc - 1 :]))
            self.own = made[-1]
        return made

    def send_first(self):
        self.across = by_context(lambda s: self.to_across[s])
        self.along = by_dp(lambda d: self.to_along[d])
        return self.across, self.along

    def send_free(self, after):
        (across, along), _ = tie((self.to_across, self.to_along), after)
        self.free = (
            by_context(lambda s: across[s][-self.half :]),
            by_dp(lambda d: along[d][-self.half :]),
        )
        return self.free

    def send_far(self, after):
        across, _ = tie(self.to_across, after)
        far_across = by_context(lambda s: across[s][: -self.half])
        far_along = by_dp(lambda d: self.to_along[d][: -self.half])
        self.across = {
            s: jnp.concatenate([x, self.free[0][s]], 0) for s, x in far_across.items()
        }
        self.along = {
            d: jnp.concatenate([x, self.free[1][d]], 0) for d, x in far_along.items()
        }
        return far_across, far_along

    def row(self, x, i):
        return x[i * self.half : (i + 1) * self.half].astype(F32)

    def sums(self):
        across = {
            s: (x + sum(self.row(y, s - 1) for y in self.along.values())).astype(BF16)
            for s, x in self.near_across.items()
        }
        along = {
            d: (x + sum(self.row(y, d - 1) for y in self.across.values())).astype(BF16)
            for d, x in self.near_along.items()
        }
        return across, along

    def finish(self, last):
        ndp, nc, _, _ = plane_blocks()
        across, along = last
        top, bottom = self.own[: self.half], self.own[self.half :]
        for x in self.across.values():
            top = top + self.row(x, ndp - 1)
        for x in along.values():
            top = top + x.astype(F32)
        for x in self.along.values():
            bottom = bottom + self.row(x, nc - 1)
        for x in across.values():
            bottom = bottom + x.astype(F32)
        return jnp.concatenate([top, bottom], 0)


def send_last(scatters, after=None):
    sums = [scatter.sums() for scatter in scatters]
    if after is not None:
        sums, _ = tie(sums, after)
    across = by_context(lambda s: jnp.concatenate([x[0][s] for x in sums], 0))
    along = by_dp(lambda d: jnp.concatenate([x[1][d] for x in sums], 0))
    split, start = [], 0
    for scatter in scatters:
        rows = slice(start, start + scatter.half)
        split.append(
            ({s: x[rows] for s, x in across.items()}, {d: x[rows] for d, x in along.items()})
        )
        start += scatter.half
    return split


def doubling_steps(axis):
    n = lax.axis_size(axis)
    step = 1
    while step < n:
        yield step, [(i, i ^ step) for i in range(n)]
        step *= 2


def small_gather(x, axes):
    for axis in axes:
        place = lax.axis_index(axis)
        for step, pairs in doubling_steps(axis):
            other = lax.ppermute(x, axis, pairs)
            high = (place & step) != 0
            x = jnp.concatenate([jnp.where(high, other, x), jnp.where(high, x, other)], 0)
    return x


def small_scatter(x, axes):
    for axis in axes:
        place = lax.axis_index(axis)
        for step, pairs in reversed(list(doubling_steps(axis))):
            half = x.shape[0] // 2
            high = (place & step) != 0
            low_part, high_part = x[:half], x[half:]
            other = lax.ppermute(jnp.where(high, low_part, high_part), axis, pairs)
            x = jnp.where(high, high_part, low_part) + other
    return x


def core_exchange(x, group):
    count = lax.axis_size("expert")
    place = lax.rem(lax.axis_index("expert"), group)
    out = x
    for s in range(1, group):
        piece = lax.dynamic_slice_in_dim(x, lax.rem(place + s, group), 1)
        pairs = [(i, i // group * group + (i % group + s) % group) for i in range(count)]
        got = lax.ppermute(piece, "expert", pairs)
        out = lax.dynamic_update_slice_in_dim(out, got, lax.rem(place - s + group, group), 0)
    return out


LANES = 128
SCALE = 2
MIB = 1 << 20


def params(mib):
    return pltpu.CompilerParams(
        dimension_semantics=("arbitrary",), vmem_limit_bytes=mib * MIB
    )


def cost(flops, nbytes):
    return pl.CostEstimate(
        flops=flops // SCALE, bytes_accessed=nbytes // SCALE, transcendentals=0
    )


def assemble(places, full, refs, half):
    for i, ref in enumerate(refs):
        full[pl.ds(pl.multiple_of(places[i] * half, half), half), :] = ref[...]


def weight_grad_kernel(counts, half, numbers, *refs):
    n = sum(counts)
    acts, grads, outs, turned = refs[:n], refs[n], refs[n + 1 : -1], refs[-1]
    spots = [(out, i) for out, c in zip(outs, counts) for i in range(c)]

    @pl.when(pl.program_id(0) == 0)
    def _():
        for k in range(n):
            turned[k * half : (k + 1) * half, :] = acts[k][...].T

    step = min(n, max(1, 1024 // half))
    for first in range(0, n, step):
        some = spots[first : first + step]
        total = mat_dot(turned[first * half : (first + len(some)) * half, :], grads[...])
        for i, (out, at) in enumerate(some):
            out[at * half : (at + 1) * half, :] = total[i * half : (i + 1) * half].astype(
                out.dtype
            )


def weight_grad(acts, grads, groups, half):
    m, columns = grads.shape
    numbers = [number for some, _ in groups for number in some]
    counts = tuple(len(some) for some, _ in groups)
    tile = tile_of(m)

    def block(k):
        return pl.BlockSpec((m, half), lambda j, p: (0, p[k]))

    return pl.pallas_call(
        functools.partial(weight_grad_kernel, counts, half),
        out_shape=[
            jax.ShapeDtypeStruct((len(some) * half, columns), dtype) for some, dtype in groups
        ],
        grid_spec=pltpu.PrefetchScalarGridSpec(
            num_scalar_prefetch=1,
            grid=(pl.cdiv(columns, tile),),
            in_specs=[block(k) for k in range(len(numbers))]
            + [pl.BlockSpec((m, tile), lambda j, p: (0, j))],
            out_specs=[pl.BlockSpec((c * half, tile), lambda j, p: (0, j)) for c in counts],
            scratch_shapes=[pltpu.VMEM((len(numbers) * half, m), BF16)],
        ),
        compiler_params=params(52),
        cost_estimate=cost(2 * m * len(numbers) * half * columns, 12 * MIB),
        name="weight_grad",
    )(jnp.stack(numbers).astype(jnp.int32), *[acts] * len(numbers), grads)


def chunk(m):
    return min(m, 512)


def tile_of(m):
    return 768 if m <= 1024 else 256


def hidden_grad_kernel(half, places, acts, *refs):
    out, full = refs[-2], refs[-1]
    assemble(places, full, refs[:-2], half)
    step = chunk(acts.shape[0])

    @pl.loop(0, acts.shape[0] // step)
    def _(c):
        rows = pl.ds(pl.multiple_of(c * step, step), step)
        out[rows, :] = mat_dot(acts[rows, :], full[...])


def hidden_grad(acts, pieces):
    m, width = acts.shape
    tile_size = tile_of(m)
    tiles = pl.cdiv(pieces.columns, tile_size)
    return pl.pallas_call(
        functools.partial(hidden_grad_kernel, pieces.half),
        out_shape=jax.ShapeDtypeStruct((m, pieces.columns), F32),
        grid_spec=pltpu.PrefetchScalarGridSpec(
            num_scalar_prefetch=1,
            grid=(tiles,),
            in_specs=[pl.BlockSpec((m, width), lambda j, p: (0, 0))]
            + [
                pl.BlockSpec((pieces.half, tile_size), lambda j, p, r=r: (r, j))
                for _, r in pieces.parts
            ],
            out_specs=pl.BlockSpec((m, tile_size), lambda j, p: (0, j)),
            scratch_shapes=[pltpu.VMEM((width, tile_size), BF16)],
        ),
        compiler_params=params(44),
        cost_estimate=cost(2 * m * width * pieces.columns, 20 * MIB),
        name="hidden_grad",
    )(pieces.places, acts, *pieces.arrays)


def fold(x):
    total = x[:, :LANES]
    for i in range(1, x.shape[1] // LANES):
        total = total + x[:, i * LANES : (i + 1) * LANES]
    return total


def ffn_kernel(n, half, tile, fe, count, columns, *refs):
    places, here, acts, router, kept, gh = refs[:6]
    gates, ups, refs = refs[6 : 6 + n], refs[6 + n : 6 + 2 * n], refs[6 + 2 * n :]
    scaled, gate_out, up_out, small = refs[:4]
    prob, share, switch, sum_e, sum_s, gate_full, up_full = refs[4:]
    step = chunk(acts.shape[0])
    j = pl.program_id(0)
    chunks = acts.shape[0] // step
    lane = lax.broadcasted_iota(jnp.int32, (1, LANES), 1)

    def rows_of(c):
        return pl.ds(pl.multiple_of(c * step, step), step)

    @pl.when(j == 0)
    def _():
        @pl.loop(0, chunks)
        def _(c):
            rows = rows_of(c)
            logits = mat_dot(acts[rows, :], router[...])
            sig = jax.nn.sigmoid(logits)
            masked = jnp.where(lane < count, logits, NEGATIVE)
            expo = jnp.exp(masked - jnp.max(masked, -1, keepdims=True))
            expo = jnp.where(lane < count, expo, 0.0)
            probs = expo / jnp.sum(expo, -1, keepdims=True)
            prob[rows, :] = probs
            own = jnp.sum(jnp.where(lane == here[0], probs, 0.0), -1, keepdims=True)
            share[rows, :] = own * kept[rows, :]
            switch[rows, :] = jnp.sum(jnp.where(lane == count, sig, 0.0), -1, keepdims=True)
            sum_e[rows, :] = jnp.zeros((step, LANES), F32)
            sum_s[rows, :] = jnp.zeros((step, LANES), F32)

    column = j * tile + lax.broadcasted_iota(jnp.int32, (1, tile), 1)
    routed = column < fe
    shared = (column >= fe) & (column < columns)
    assemble(places, gate_full, gates, half)
    assemble(places, up_full, ups, half)

    @pl.loop(0, chunks)
    def _(c):
        rows = rows_of(c)
        gate = mat_dot(acts[rows, :], gate_full[...])
        up = mat_dot(acts[rows, :], up_full[...])
        scale = jnp.where(routed, share[rows, :], switch[rows, :])
        sig = jax.nn.sigmoid(gate)
        silu = gate * sig
        hidden = silu * up
        grad = gh[rows, :]
        product = grad * hidden
        sum_e[rows, :] += fold(jnp.where(routed, product, 0.0))
        sum_s[rows, :] += fold(jnp.where(shared, product, 0.0))
        grad = grad * scale
        scaled[rows, :] = (scale * hidden).astype(BF16)
        gate_out[rows, :] = (grad * up * (sig + silu * (1.0 - sig))).astype(BF16)
        up_out[rows, :] = (grad * silu).astype(BF16)

    @pl.when(j == pl.num_programs(0) - 1)
    def _():
        @pl.loop(0, chunks)
        def _(c):
            rows = rows_of(c)
            grad_share = jnp.sum(sum_e[rows, :], -1, keepdims=True)
            grad_switch = jnp.sum(sum_s[rows, :], -1, keepdims=True)
            hot = (lane == here[0]).astype(F32)
            logit = grad_share * share[rows, :] * (hot - prob[rows, :])
            sw = switch[rows, :]
            pre = grad_switch * sw * (1.0 - sw)
            value = jnp.where(lane < count, logit, jnp.where(lane == count, pre, 0.0))
            small[rows, :] = value.astype(BF16)


def ffn(acts, router, kept, gh, here, gates, ups, fe, count):
    m, width = acts.shape
    columns = gates.columns
    tile_size = tile_of(m)
    tiles = pl.cdiv(columns, tile_size)
    whole = lambda j, p, h: (0, 0)
    tile = pl.BlockSpec((m, tile_size), lambda j, p, h: (0, j))
    weights = [
        pl.BlockSpec((gates.half, tile_size), lambda j, p, h, r=r: (r, j))
        for _, r in gates.parts + ups.parts
    ]
    hid = jax.ShapeDtypeStruct((m, columns), BF16)
    return pl.pallas_call(
        functools.partial(
            ffn_kernel, len(gates.parts), gates.half, tile_size, fe, count, columns
        ),
        out_shape=(hid, hid, hid, jax.ShapeDtypeStruct((m, LANES), BF16)),
        grid_spec=pltpu.PrefetchScalarGridSpec(
            num_scalar_prefetch=2,
            grid=(tiles,),
            in_specs=[
                pl.BlockSpec((m, width), whole),
                pl.BlockSpec((width, LANES), whole),
                pl.BlockSpec((m, 1), whole),
                tile,
            ]
            + weights,
            out_specs=[tile, tile, tile, pl.BlockSpec((m, LANES), whole)],
            scratch_shapes=[
                pltpu.VMEM((m, LANES), F32),
                pltpu.VMEM((m, 1), F32),
                pltpu.VMEM((m, 1), F32),
                pltpu.VMEM((m, LANES), F32),
                pltpu.VMEM((m, LANES), F32),
                pltpu.VMEM((width, tile_size), BF16),
                pltpu.VMEM((width, tile_size), BF16),
            ],
        ),
        compiler_params=params(52),
        cost_estimate=cost(4 * m * width * columns, 40 * MIB),
        name="ffn",
    )(gates.places, here, acts, router, kept, gh, *gates.arrays, *ups.arrays)


def spread_kernel(n, pairs, extra, places, *refs):
    i = pl.program_id(0)
    acts, refs = refs[:pairs], refs[pairs:]
    weights, refs = [refs[k * n : (k + 1) * n] for k in range(pairs)], refs[pairs * n :]
    out, held = refs[-1 - pairs], refs[-pairs:]
    step = min(out.shape[0], 1024)
    for k in range(n):

        @pl.when(i == k)
        def _(k=k):
            for pair in range(pairs):
                held[pair][...] = weights[pair][k][...]

    @pl.loop(0, out.shape[0] // step)
    def _(c):
        rows = pl.ds(pl.multiple_of(c * step, step), step)
        total = right_dot(acts[0][rows, :], held[0][...])
        for pair in range(1, pairs):
            total += right_dot(acts[pair][rows, :], held[pair][...])
        if extra:
            total += right_dot(refs[0][rows, :], refs[1][...])
        out[rows, :] = total.astype(BF16)


def spread(pairs, extra=None):
    acts = [a for a, _ in pairs]
    first = pairs[0][1]
    half, steps = first.half, len(first.parts)
    m = acts[0].shape[0]
    width = steps * half
    whole = lambda i, p: (0, 0)
    specs = [pl.BlockSpec(a.shape, whole) for a in acts]
    operands = list(acts)
    for _, pieces in pairs:
        specs += [
            pl.BlockSpec((half, pieces.columns), lambda i, p, r=r: (r, 0))
            for _, r in pieces.parts
        ]
        operands += pieces.arrays
    if extra is not None:
        specs.append(pl.BlockSpec(extra[0].shape, whole))
        specs.append(pl.BlockSpec((half, LANES), lambda i, p: (p[i], 0)))
        operands += list(extra)
    return pl.pallas_call(
        functools.partial(spread_kernel, steps, len(pairs), extra is not None),
        out_shape=jax.ShapeDtypeStruct((m, width), BF16),
        grid_spec=pltpu.PrefetchScalarGridSpec(
            num_scalar_prefetch=1,
            grid=(steps,),
            in_specs=specs,
            out_specs=pl.BlockSpec((m, half), lambda i, p: (0, p[i])),
            scratch_shapes=[pltpu.VMEM((half, first.columns), BF16)] * len(pairs),
        ),
        compiler_params=params(60),
        cost_estimate=cost(2 * m * width * first.columns * len(pairs), 20 * MIB),
        name="spread",
    )(first.places, *operands)


def turn(x):
    return pltpu.roll(x, HD // 2, 1)


def qkv_kernel(half, wide, places, tok, gain, bias, cosine, sine, *refs):
    normed, query, key_value, inverse, full = refs[-5:]

    @pl.when(pl.program_id(0) == 0)
    def _():
        assemble(places, full, refs[:-5], half)

    values = tok[...].astype(F32)
    inv = lax.rsqrt(jnp.mean(values * values, -1, keepdims=True) + EPSILON)
    inverse[...] = inv
    normed[...] = (values * inv * gain[...]).astype(BF16)
    out = mat_dot(normed[...], full[...]) + bias[...]
    for h in range(2 * wide // HD):
        head = out[:, h * HD : (h + 1) * HD]
        head = (head * cosine[...] + turn(head) * sine[...]).astype(BF16)
        if h < wide // HD:
            query[:, h * HD : (h + 1) * HD] = head
        else:
            key_value[:, h * HD - wide : (h + 1) * HD - wide] = head
    key_value[:, wide:] = out[:, 2 * wide :].astype(BF16)


def qkv_project(tok, gain, bias, cosine, sine, pieces, wide):
    m, width = tok.shape
    step = 256
    row = lambda i, p: (i, 0)
    whole = lambda i, p: (0, 0)
    return pl.pallas_call(
        functools.partial(qkv_kernel, pieces.half, wide),
        out_shape=(
            jax.ShapeDtypeStruct((m, width), BF16),
            jax.ShapeDtypeStruct((m, wide), BF16),
            jax.ShapeDtypeStruct((m, 2 * wide), BF16),
            jax.ShapeDtypeStruct((m, 1), F32),
        ),
        grid_spec=pltpu.PrefetchScalarGridSpec(
            num_scalar_prefetch=1,
            grid=(m // step,),
            in_specs=[
                pl.BlockSpec((step, width), row),
                pl.BlockSpec((1, width), whole),
                pl.BlockSpec((1, 3 * wide), whole),
                pl.BlockSpec((step, HD), row),
                pl.BlockSpec((step, HD), row),
            ]
            + [
                pl.BlockSpec((pieces.half, 3 * wide), lambda i, p, r=r: (r, 0))
                for _, r in pieces.parts
            ],
            out_specs=[
                pl.BlockSpec((step, width), row),
                pl.BlockSpec((step, wide), row),
                pl.BlockSpec((step, 2 * wide), row),
                pl.BlockSpec((step, 1), row),
            ],
            scratch_shapes=[pltpu.VMEM((width, 3 * wide), BF16)],
        ),
        compiler_params=params(32),
        cost_estimate=cost(6 * m * width * wide, 12 * MIB),
        name="qkv_project",
    )(pieces.places, tok, gain, bias, cosine, sine, *pieces.arrays)


def head_probs(query, kvs, allowed, h):
    own = slice(h * HD, (h + 1) * HD)
    scores = jnp.concatenate([right_dot(query[:, own], kv[:, own]) for kv in kvs], -1)
    scores = jnp.where(allowed, scores * HD ** (-0.5), NEGATIVE)
    expo = jnp.exp(scores - jnp.max(scores, -1, keepdims=True))
    return expo / jnp.sum(expo, -1, keepdims=True)


def attend_kernel(nc, wide, query, allowed, w_o, *refs):
    kvs, mixed, out = refs[:nc], refs[nc], refs[nc + 1]
    tok = query.shape[0]
    for h in range(wide // HD):
        value = slice(wide + h * HD, wide + (h + 1) * HD)
        prob = head_probs(query, kvs, allowed[0] > 0.0, h).astype(BF16)
        total = mat_dot(prob[:, :tok], kvs[0][:, value])
        for s in range(1, nc):
            total += mat_dot(prob[:, s * tok : (s + 1) * tok], kvs[s][:, value])
        mixed[:, h * HD : (h + 1) * HD] = total.astype(BF16)
    out[...] = mat_dot(mixed[...], w_o[...]).astype(BF16)


def attend(query, kvs, allowed, w_o):
    m, wide = query.shape
    groups, tok, keys = allowed.shape
    width = w_o.shape[1]
    row = lambda g: (g, 0)
    return pl.pallas_call(
        functools.partial(attend_kernel, len(kvs), wide),
        out_shape=(
            jax.ShapeDtypeStruct((m, wide), BF16),
            jax.ShapeDtypeStruct((m, width), BF16),
        ),
        grid=(groups,),
        in_specs=[
            pl.BlockSpec((tok, wide), row),
            pl.BlockSpec((1, tok, keys), lambda g: (g, 0, 0)),
            pl.BlockSpec((wide, width), lambda g: (0, 0)),
        ]
        + [pl.BlockSpec((tok, 2 * wide), row)] * len(kvs),
        out_specs=[pl.BlockSpec((tok, wide), row), pl.BlockSpec((tok, width), row)],
        compiler_params=params(32),
        cost_estimate=cost(2 * m * width * wide + 4 * m * keys * wide, 8 * MIB),
        name="attend",
    )(query, allowed, w_o, *kvs)


def attend_back_kernel(nc, wide, query, allowed, w_o, grads, cosine, sine, *refs):
    kvs, grad_query, grad_own, grad_far = refs[:nc], refs[nc], refs[nc + 1], refs[nc + 2 :]
    tok = query.shape[0]
    grad_mixed = right_dot(grads[...], w_o[...]).astype(BF16)
    scale = HD ** (-0.5)
    for h in range(wide // HD):
        key = slice(h * HD, (h + 1) * HD)
        value = slice(wide + h * HD, wide + (h + 1) * HD)
        prob = head_probs(query, kvs, allowed[0] > 0.0, h)
        low = prob.astype(BF16)
        mixed = grad_mixed[:, key]
        grad = jnp.concatenate([right_dot(mixed, kv[:, value]) for kv in kvs], -1)
        inner = jnp.sum(grad * prob, -1, keepdims=True)
        grad = (prob * (grad - inner)).astype(BF16)
        total = None
        for s in range(nc):
            block = slice(s * tok, (s + 1) * tok)
            term = mat_dot(grad[:, block], kvs[s][:, key])
            total = term if total is None else total + term
            grad_key = left_dot(grad[:, block], query[:, key]) * scale
            grad_value = left_dot(low[:, block], mixed)
            if s == 0:
                grad_own[:, key] = grad_key
                grad_own[:, value] = grad_value
            else:
                grad_far[s - 1][:, key] = grad_key.astype(BF16)
                grad_far[s - 1][:, value] = grad_value.astype(BF16)
        total = total * scale
        total = total * cosine[...] - turn(total) * sine[...]
        grad_query[:, key] = total.astype(BF16)


def attend_back(query, kvs, allowed, w_o, grads, cosine, sine):
    m, wide = query.shape
    groups, tok, keys = allowed.shape
    width = w_o.shape[1]
    nc = len(kvs)
    row = lambda g: (g, 0)
    both = pl.BlockSpec((tok, 2 * wide), row)
    return pl.pallas_call(
        functools.partial(attend_back_kernel, nc, wide),
        out_shape=(
            jax.ShapeDtypeStruct((m, wide), BF16),
            jax.ShapeDtypeStruct((m, 2 * wide), F32),
            *[jax.ShapeDtypeStruct((m, 2 * wide), BF16)] * (nc - 1),
        ),
        grid=(groups,),
        in_specs=[
            pl.BlockSpec((tok, wide), row),
            pl.BlockSpec((1, tok, keys), lambda g: (g, 0, 0)),
            pl.BlockSpec((wide, width), lambda g: (0, 0)),
            pl.BlockSpec((tok, width), row),
            pl.BlockSpec((tok, HD), row),
            pl.BlockSpec((tok, HD), row),
        ]
        + [both] * nc,
        out_specs=[pl.BlockSpec((tok, wide), row)] + [both] * nc,
        compiler_params=params(32),
        cost_estimate=cost(2 * m * width * wide + 12 * m * keys * wide, 8 * MIB),
        name="attend_back",
    )(query, allowed, w_o, grads, cosine, sine, *kvs)


def join_kernel(wide, grad_query, grad_own, cosine, sine, *refs):
    far, out, sums = refs[:-2], refs[-2], refs[-1]
    total = grad_own[...]
    for ref in far:
        total = total + ref[...].astype(F32)
    out[:, :wide] = grad_query[...]
    for h in range(wide // HD):
        head = total[:, h * HD : (h + 1) * HD]
        head = head * cosine[...] - turn(head) * sine[...]
        out[:, wide + h * HD : wide + (h + 1) * HD] = head.astype(BF16)
    out[:, 2 * wide :] = total[:, wide:].astype(BF16)

    @pl.when(pl.program_id(0) == 0)
    def _():
        sums[...] = jnp.zeros_like(sums)

    sums[...] += jnp.sum(out[...].astype(F32), 0, keepdims=True)


def join(grad_query, grad_own, far, cosine, sine):
    m, wide = grad_query.shape
    step = 256
    row = lambda i: (i, 0)
    both = pl.BlockSpec((step, 2 * wide), row)
    return pl.pallas_call(
        functools.partial(join_kernel, wide),
        out_shape=(
            jax.ShapeDtypeStruct((m, 3 * wide), BF16),
            jax.ShapeDtypeStruct((1, 3 * wide), F32),
        ),
        grid=(m // step,),
        in_specs=[
            pl.BlockSpec((step, wide), row),
            both,
            pl.BlockSpec((step, HD), row),
            pl.BlockSpec((step, HD), row),
        ]
        + [both] * len(far),
        out_specs=[
            pl.BlockSpec((step, 3 * wide), row),
            pl.BlockSpec((1, 3 * wide), lambda i: (0, 0)),
        ],
        compiler_params=params(32),
        cost_estimate=cost(20 * m * wide, 6 * MIB),
        name="join",
    )(grad_query, grad_own, cosine, sine, *far)


def rms_unit(values):
    scaling = lax.rsqrt(jnp.mean(values * values, -1, keepdims=True) + EPSILON)
    return values * scaling, scaling


def body(
    tokens,
    cotangent,
    deal_order,
    seq_lengths,
    expert_ids,
    w_query,
    w_key,
    w_value,
    w_out,
    bias_query,
    bias_key,
    bias_value,
    norm_attn,
    norm_ffn,
    w_router,
    shared_gate,
    shared_up,
    shared_down,
    shared_switch,
    expert_gate,
    expert_up,
    expert_down,
):
    ndp, nc, dp, ctx = plane_blocks()
    planes = ndp * nc
    count = lax.axis_size("expert")
    here = lax.axis_index("expert")
    tok_count, width = tokens.shape[1], tokens.shape[2]
    group_tok = deal_order.shape[1]
    seqs = seq_lengths.shape[1]
    top = expert_ids.shape[2]
    rows_flat = w_query.shape[0]
    part = HD // rows_flat
    heads = planes // part
    runs = count // part
    run, member = here // part, lax.rem(here, part)
    fe_width = expert_gate.shape[2]
    fs_width = shared_gate.shape[1]
    pad = -(fe_width + fs_width) % LANES
    capacity = min(tok_count, 5 * tok_count * top // (4 * count))
    wide = heads * HD
    all_rows = count * tok_count
    block = width // planes

    token_rows = tokens[0]

    def by_head(w):
        w = w.reshape(rows_flat, part, heads, runs, HD).transpose(3, 1, 0, 2, 4)
        return w.reshape(count, rows_flat, wide)

    qkv_out = jnp.concatenate([by_head(w) for w in (w_query, w_key, w_value)], -1)
    all_tokens = lax.all_gather(token_rows, "expert", axis=0, tiled=True)
    qkv_rows = lax.all_to_all(qkv_out, "expert", split_axis=0, concat_axis=0, tiled=True)
    small = jnp.concatenate(
        [
            v.astype(F32).reshape(-1)
            for v in (
                bias_query,
                bias_key,
                bias_value,
                norm_attn,
                norm_ffn,
                shared_switch,
                w_router,
                deal_order,
                seq_lengths,
                expert_ids,
            )
        ]
    )

    weights, _ = tie((expert_up, shared_up, expert_down, shared_down), qkv_out)
    expert_up, shared_up, expert_down, shared_down = weights

    def stacked(routed, shared):
        none = jnp.zeros((routed.shape[0], pad), BF16)
        return jnp.concatenate([routed, shared, none], 1)

    def turned(routed, shared, h):
        columns = slice(h * block // 2, (h + 1) * block // 2)
        return stacked(routed[:, columns].T, shared[:, columns].T)

    def rows_half(x, h):
        return x[h * block // 2 : (h + 1) * block // 2]

    hb = block // 2
    gate_own = stacked(expert_gate[0], shared_gate)
    d_top, d_low = [turned(expert_down[0], shared_down, h) for h in range(2)]
    u_top, u_low = [stacked(rows_half(expert_up[0], h), rows_half(shared_up, h)) for h in range(2)]
    pair_own = jnp.concatenate([d_top, d_low, u_top, u_low], 0)
    wo_across, wo_along, wo_far = gather_plain(w_out)
    gate_across, gate_along, gate_far = gather_plain(gate_own)
    small, pair_own = tie(small, pair_own)
    small_plane = small_gather(small[None], ("context", "dp"))
    qkv_own = qkv_rows.reshape(count * rows_flat, 3 * wide)
    qkv_own, _ = tie(qkv_own, (gate_across, gate_along, pair_own))
    small_plane, _ = tie(small_plane, qkv_own)
    all_grads = lax.all_gather(
        tie(cotangent[0], qkv_own)[0], "expert", axis=0, tiled=True
    )
    _, _, qkv_far = gather_plain(qkv_own)
    small_all = small_gather(small_plane.reshape(1, -1), ("expert",))
    small_all = small_all.reshape(count, ndp * nc, -1).transpose(1, 0, 2)
    small_all = small_all.reshape(ndp * nc * count, -1)
    qkv_found, qkv_sent = qkv_far()
    qkv_pieces = Pieces(qkv_found, qkv_own.shape[0] // 2)
    wo_found, _ = wo_far(qkv_sent)
    gate_found, gate_sent = gate_far(qkv_sent)
    gate_pieces = Pieces(gate_found, hb)
    columns = {}
    place = 0
    for name in ("bq", "bk", "bv", "na", "nf", "sw"):
        columns[name] = small_all[:, place : place + rows_flat].reshape(-1)
        place += rows_flat
    router = small_all[:, place : place + rows_flat * count].reshape(-1, count).astype(BF16)
    place += rows_flat * count
    plane_small = lax.dynamic_index_in_dim(
        small_all.reshape(ndp, nc, count, -1), dp, 0, keepdims=False
    )
    order = plane_small[0, :, place : place + group_tok].astype(jnp.int32)
    place += group_tok
    lengths = plane_small[0, :, place : place + seqs].astype(jnp.int32)
    place += seqs
    ids = plane_small[..., place:].reshape(nc, count, tok_count, top).astype(jnp.int32)
    gain_attn, gain_ffn = columns["na"], columns["nf"]
    router_switch = jnp.concatenate(
        [
            router,
            columns["sw"].astype(BF16)[:, None],
            jnp.zeros((width, LANES - count - 1), BF16),
        ],
        1,
    )

    local_index = ctx * tok_count + jnp.arange(tok_count, dtype=jnp.int32)
    ends = jnp.cumsum(lengths, 1)
    starts = ends - lengths

    def segments(index):
        segment = jnp.sum((index[None, :, None] >= ends[:, None, :]).astype(jnp.int32), -1)
        hot = segment[..., None] == jnp.arange(seqs, dtype=jnp.int32)
        return segment, index[None, :] - jnp.sum(jnp.where(hot, starts[:, None, :], 0), -1)

    query_segment, position = segments(local_index)
    allowed = []
    for s in range(nc):
        key_index = local_index - s * tok_count
        key_segment, _ = segments(key_index)
        allowed.append(
            (query_segment[:, :, None] == key_segment[:, None, :])
            & (key_index[None, None, :] <= local_index[None, :, None])
            & (key_index >= 0)[None, None, :]
        )
    allowed = jnp.concatenate(allowed, -1).astype(F32)
    frequency = ROPE_BASE ** (-2.0 * jnp.arange(HD // 2, dtype=F32) / HD)
    angles = position.reshape(-1).astype(F32)[:, None] * frequency[None, :]
    cosine = jnp.concatenate([jnp.cos(angles)] * 2, -1)
    sine = jnp.sin(angles)
    sine_table = jnp.concatenate([-sine, sine], -1)

    def own_heads(row):
        row = row.reshape(part, heads, runs, HD)
        row = lax.dynamic_index_in_dim(row, member, 0, keepdims=False)
        return lax.dynamic_index_in_dim(row, run, 1, keepdims=False).reshape(-1)

    bias = jnp.concatenate([own_heads(columns[k]) for k in ("bq", "bk", "bv")])
    normed, queries, key_value, inverse = qkv_project(
        all_tokens, gain_attn[None], bias[None], cosine, sine_table, qkv_pieces, wide
    )
    kvs = [key_value] + [
        lax.ppermute(key_value, "context", [(i, i + s) for i in range(nc - s)])
        for s in range(1, nc)
    ]
    wo_arrays, _ = tie({k: array for k, (array, _) in wo_found.items()}, key_value)
    wo_found = {k: (wo_arrays[k], row) for k, (_, row) in wo_found.items()}
    wo_pieces = Pieces(wo_found, rows_flat // 2)
    wo_planes = jnp.zeros((2 * planes, rows_flat // 2, width), BF16)
    for (array, row), number in zip(wo_pieces.parts, list(wo_pieces.places)):
        array = array[row * rows_flat // 2 : (row + 1) * rows_flat // 2]
        wo_planes = lax.dynamic_update_slice_in_dim(wo_planes, array[None], number, 0)
    wo_mine = core_exchange(wo_planes.reshape(part, heads, rows_flat, width), part)
    w_o = wo_mine.transpose(1, 0, 2, 3).reshape(wide, width)

    kvs, (pair_own, _) = tie(kvs, (pair_own, (gate_sent, all_grads)))
    x_one, y_one = by_context(lambda s: pair_own), by_dp(lambda d: pair_own)
    mixed, attn_part = attend(queries, kvs, allowed, w_o)
    attn_out = lax.psum_scatter(attn_part, "expert", scatter_dimension=0, tiled=True)
    attn_out, _ = tie(attn_out, (x_one, y_one))
    x_two = by_context(
        lambda s: jnp.concatenate([y[hb : 2 * hb] for y in y_one.values()], 0)
    )
    y_two = by_dp(lambda d: jnp.concatenate([x[:hb] for x in x_one.values()], 0))
    residual = token_rows.astype(F32) + attn_out.astype(F32)
    unit_two, scale_two = rms_unit(residual)
    rows = lax.all_gather(
        (unit_two * gain_ffn).astype(BF16), "expert", axis=0, tiled=True
    )
    rows, _ = tie(rows, (x_two, y_two))
    x_far = [y[3 * hb :] for y in y_one.values()]
    y_far = [x[2 * hb : 3 * hb] for x in x_one.values()]
    x_three = by_context(lambda s: jnp.concatenate(x_far, 0))
    y_three = by_dp(lambda d: jnp.concatenate(y_far, 0))
    down_found = {(0, 0, h): (pair_own, h) for h in range(2)}
    up_found = {(0, 0, h): (pair_own, 2 + h) for h in range(2)}
    for s, x in x_one.items():
        down_found.update({(0, s, h): (x, h) for h in range(2)})
        up_found.update({(0, s, h): (x, 2 + h) for h in range(2)})
    for d, y in y_one.items():
        down_found.update({(d, 0, h): (y, h) for h in range(2)})
        up_found.update({(d, 0, h): (y, 2 + h) for h in range(2)})
        for s in x_one:
            down_found.update({(d, s, 0): (y_two[d], s - 1), (d, s, 1): (x_two[s], d - 1)})
            up_found.update({(d, s, 0): (y_three[d], s - 1), (d, s, 1): (x_three[s], d - 1)})
    down_pieces, up_pieces = Pieces(down_found, hb), Pieces(up_found, hb)

    (ids, order), _ = tie((ids, order), key_value)
    hit = jnp.any(ids == here, -1)
    below = jnp.arange(tok_count)[:, None] < jnp.arange(tok_count)[None, :]
    slot = mat_dot(hit.reshape(nc * count, tok_count).astype(BF16), below.astype(BF16))
    kept = (hit & (slot.reshape(nc, count, tok_count) < capacity)).astype(F32)
    kept = kept.transpose(1, 0, 2).reshape(count, group_tok)
    kept_rows = jnp.sum(
        jnp.where(order[:, None, :] == local_index[None, :, None], kept[:, None, :], 0.0), -1
    ).reshape(all_rows)

    gh = hidden_grad(all_grads, down_pieces)
    scaled, grad_gate, grad_up, grad_small = ffn(
        rows,
        router_switch,
        kept_rows[:, None],
        gh,
        here.astype(jnp.int32)[None],
        gate_pieces,
        up_pieces,
        fe_width,
        count,
    )
    def scatter_of(acts, grads):
        return Scatter(lambda groups: weight_grad(acts, grads, groups, hb), hb)

    down_sum = scatter_of(all_grads, scaled)
    gate_sum = scatter_of(rows, grad_gate)
    down_sum.make(last=False)
    down_sent = down_sum.send_first()
    grad_rows = spread([(grad_gate, gate_pieces), (grad_up, up_pieces)], (grad_small, router_switch))
    grad_rows, _ = tie(grad_rows, down_sent)
    grad_normed_two = lax.psum_scatter(
        grad_rows, "expert", scatter_dimension=0, tiled=True
    ).astype(F32)
    gate_sum.make(last=False)
    gate_sent = gate_sum.send_first()
    terms = [down_sum.make(first=False), gate_sum.make(first=False)]
    out_part = spread([(scaled, down_pieces)])
    grad_normed_two, _ = tie(grad_normed_two, (gate_sent, terms, out_part))
    both = send_last([down_sum, gate_sum])
    down_last, gate_last = both
    grad_up, _ = tie(grad_up, grad_normed_two)
    up_sum = scatter_of(rows, grad_up)
    up_sum.make()
    grad_router_switch = left_dot(rows, grad_small)

    grad_unit = grad_normed_two * gain_ffn
    grad_residual = cotangent[0].astype(F32) + scale_two * (
        grad_unit - unit_two * jnp.mean(grad_unit * unit_two, -1, keepdims=True)
    )
    grad_gain_ffn = jnp.sum(grad_normed_two * unit_two, 0)
    attn_own = grad_residual.astype(BF16)
    grad_attn = lax.all_gather(attn_own, "expert", axis=0, tiled=True)
    output = lax.psum_scatter(
        tie(out_part, attn_own)[0], "expert", scatter_dimension=0, tiled=True
    )
    grad_attn, _ = tie(grad_attn, both)
    up_sent = up_sum.send_free(both)
    grad_query, grad_own, *grad_far = attend_back(
        queries, kvs, allowed, w_o, grad_attn, cosine, sine_table
    )
    grad_far, (down_last, _) = tie(grad_far, (down_last, up_sent))
    grad_down_w = down_sum.finish(down_last)
    mixed, _ = tie(mixed, grad_query)
    grad_wo = left_dot(mixed, grad_attn).astype(BF16).reshape(heads, part, rows_flat, width)
    wo_back = core_exchange(grad_wo.transpose(1, 0, 2, 3), part)
    wo_back = wo_back.reshape(2 * planes, rows_flat // 2, width)
    grad_far = [
        lax.ppermute(piece, "context", [(i + s, i) for i in range(nc - s)])
        for s, piece in enumerate(grad_far, 1)
    ]
    grad_qkv, bias_sums = join(grad_query, grad_own, grad_far, cosine, sine_table)
    grad_qkv, (output, gate_last, wo_back) = tie(grad_qkv, (output, gate_last, wo_back))
    grad_gate_w = gate_sum.finish(gate_last)
    out_tokens = (residual + output.astype(F32)).astype(BF16)
    up_far_sent = up_sum.send_far(grad_far)
    qkv_sum = scatter_of(normed, grad_qkv)
    grad_qkv, _ = tie(grad_qkv, qkv_sum.make())
    qkv_sent = qkv_sum.send_first()
    grad_normed = spread([(grad_qkv, qkv_pieces)])
    grad_normed, _ = tie(grad_normed, up_far_sent)
    grad_normed_own = lax.psum_scatter(
        grad_normed, "expert", scatter_dimension=0, tiled=True
    ).astype(F32)
    (qkv_last,) = send_last([qkv_sum])
    grad_normed_own, _ = tie(grad_normed_own, qkv_last)

    qkv_grad_rows = qkv_sum.finish(qkv_last)
    (up_last,) = send_last([up_sum], qkv_sent)
    grad_up_w = up_sum.finish(up_last)
    qkv_back = lax.all_to_all(
        qkv_grad_rows.astype(BF16).reshape(count, rows_flat, 3 * wide),
        "expert",
        split_axis=0,
        concat_axis=0,
        tiled=True,
    )

    def from_heads(i):
        w = qkv_back[..., i * wide : (i + 1) * wide].astype(F32)
        w = w.reshape(runs, part, rows_flat, heads, HD).transpose(2, 1, 3, 0, 4)
        return w.reshape(rows_flat, width)

    wo_back, _ = tie(wo_back, qkv_last)
    wo_sum = Scatter(
        lambda groups: [
            jnp.concatenate(
                [lax.dynamic_index_in_dim(wo_back, i, 0, keepdims=False) for i in some], 0
            ).astype(dtype)
            for some, dtype in groups
        ],
        rows_flat // 2,
    )
    wo_sum.make()
    wo_sum.send_first()
    grad_w_out = wo_sum.finish(send_last([wo_sum])[0])

    def to_heads(row):
        full = jnp.zeros((part, heads, runs, HD), F32)
        full = lax.dynamic_update_slice(
            full, row.reshape(1, heads, 1, HD), (member, 0, run, 0)
        )
        return full.reshape(planes * count, rows_flat)

    bias_sums = bias_sums[0]
    grad_gain_attn = jnp.sum(
        grad_normed.astype(F32) * (all_tokens.astype(F32) * inverse), 0
    )
    small_grads = jnp.concatenate(
        [to_heads(bias_sums[i * wide : (i + 1) * wide]) for i in range(3)]
        + [
            grad_gain_attn.reshape(-1, rows_flat),
            grad_gain_ffn.reshape(-1, rows_flat),
            grad_router_switch[:, count].reshape(-1, rows_flat),
            grad_router_switch[:, :count].reshape(planes * count, rows_flat * count),
        ],
        1,
    )
    small_grads, _ = tie(small_grads, qkv_last)
    small_sum = small_scatter(small_grads, ("dp", "context"))
    small_sum = small_scatter(small_sum, ("expert",))[0]
    pieces = [small_sum[i * rows_flat : (i + 1) * rows_flat] for i in range(6)]
    grad_router = small_sum[6 * rows_flat :].reshape(rows_flat, count)

    unit_one, scale_one = rms_unit(token_rows.astype(F32))
    grad_unit = grad_normed_own * gain_attn
    grad_tokens = grad_residual + scale_one * (
        grad_unit - unit_one * jnp.mean(grad_unit * unit_one, -1, keepdims=True)
    )
    return (
        out_tokens[None],
        grad_tokens.astype(BF16)[None],
        from_heads(0),
        from_heads(1),
        from_heads(2),
        grad_w_out,
        pieces[0],
        pieces[1],
        pieces[2],
        pieces[3],
        pieces[4],
        grad_router,
        grad_gate_w[:, fe_width : fe_width + fs_width],
        grad_up_w[:, fe_width : fe_width + fs_width],
        grad_down_w[:, fe_width : fe_width + fs_width].T,
        pieces[5],
        grad_gate_w[None, :, :fe_width],
        grad_up_w[None, :, :fe_width],
        grad_down_w[:, :fe_width].T[None],
    )


def solution(mesh):
    every = ("dp", "context", "expert")
    plane = ("dp", "context")
    rows = P(("dp", "expert"), "context", None)
    groups = P(("dp", "expert"), None)
    return jax.shard_map(
        body,
        mesh=mesh,
        in_specs=(
            rows,
            rows,
            groups,
            groups,
            rows,
            *[P(every, None)] * 4,
            *[P(every)] * 5,
            P(every, None),
            P(plane, "expert"),
            P(plane, "expert"),
            P("expert", plane),
            P(every),
            P("expert", plane, None),
            P("expert", plane, None),
            P("expert", None, plane),
        ),
        out_specs=(
            rows,
            rows,
            *[P(every, None)] * 4,
            *[P(every)] * 5,
            P(every, None),
            P(plane, "expert"),
            P(plane, "expert"),
            P("expert", plane),
            P(every),
            P("expert", plane, None),
            P("expert", plane, None),
            P("expert", None, plane),
        ),
        check_vma=False,
    )
```
